32 devices in a mesh: grp: 8 (over y, x, core), ep: 4 (over z).
Axes of the slice: x: 2, y: 2, z: 4, core: 2. Of those that a mesh axis runs over, the one named last changes fastest.
Arguments:
- layer_input: bfloat16 [8192, 2048], P(('grp', 'ep')), may hold values from -6 to 6
- kv_weight: float32 [4096, 2048], P(None, 'grp'), may hold values from -0.125 to 0.125
- norm_gains: float32 [2, 2048], P(None, 'grp'), may hold values from 0.5 to 1.5
- query_maps: float32 [4, 2048, 2048], P('ep', 'grp'), may hold values from -0.125 to 0.125
- output_maps: float32 [4, 2048, 2048], P('ep', 'grp'), may hold values from -1 to 1
- gate_up_maps: float32 [4, 2048, 11264], P('ep', 'grp'), may hold values from -0.125 to 0.125
- down_maps: float32 [4, 5632, 2048], P('ep', 'grp'), may hold values from -0.15625 to 0.15625
- att_routes: int32 [8, 1024, 2], P('grp'), may hold values from 0 to 3, all different within a row; in each aligned block of 256 rows (0 to 255, 256 to 511, ..., all dimensions but the last counted through in order) at most 192 rows name the same one
- att_gates: float32 [8192, 2], P(('grp', 'ep')), may hold values from 0.25 to 0.75
- mlp_routes: int32 [8, 1024, 2], P('grp'), may hold values from 0 to 3, all different within a row; in each aligned block of 256 rows (0 to 255, 256 to 511, ..., all dimensions but the last counted through in order) at most 192 rows name the same one
- mlp_gates: float32 [8192, 2], P(('grp', 'ep')), may hold values from 0.25 to 0.75
- segments: int32 [8, 1024], P('grp'), may hold values from 0 to 1023, as said below
- cotangent: bfloat16 [8192, 2048], P(('grp', 'ep')), may hold values from -6 to 6
Outputs:
- output: bfloat16 [8192, 2048], P(('grp', 'ep'))
- d_input: float32 [8192, 2048], P(('grp', 'ep'))
- d_kv_weight: float32 [4096, 2048], P(None, 'grp')
- d_norm_gains: float32 [2, 2048], P(None, 'grp')
- d_query_maps: float32 [4, 2048, 2048], P('ep', 'grp')
- d_output_maps: float32 [4, 2048, 2048], P('ep', 'grp')
- d_gate_up_maps: float32 [4, 2048, 11264], P('ep', 'grp')
- d_down_maps: float32 [4, 5632, 2048], P('ep', 'grp')
The draws below stay inside these ranges and needn't reach their ends.
Inputs may be any that keep to these rules, and one draw needn't show every extreme that they name: `att_routes`: each token names 2 different experts; among the tokens of one device no expert is named more than 192 times. `mlp_routes`: each token names 2 different experts; among the tokens of one device no expert is named more than 192 times. `segments`: a token's document number is the position of its document's first token in the sequence, so numbers never fall along a sequence; in every sequence one document runs from the first device's tokens into the last device's tokens.
All inputs are finite; a program needn't handle non-finite values.
Results may differ from the reference program's by a relative error of at most 0.019.
Values may be sent and summed in bfloat16 or wider, within the bound.
A program may use at most 384 MiB of HBM per device.

```python
import math
import jax
import jax.numpy as jnp
import numpy as np
from jax import lax

D = 2048
HEADS = 16
HEAD_DIM = 128
FF = 5632
TOP = 2
SEQ = 1024
EXPERTS = 4
KV = 2048
GROUPS = 8
TOK_DEV = 256
TOKENS = 8192
CAPACITY = 192
N_EP = 4


def draw_segments(key, part):
    key = jax.random.fold_in(key, 7)
    first_key, second_key, third_key = jax.random.split(key, 3)
    places = jnp.arange(SEQ, dtype=jnp.int32)[None, :]
    long_start = jax.random.randint(first_key, (GROUPS, 1), 1, TOK_DEV, dtype=jnp.int32)
    long_finish = SEQ - jax.random.randint(second_key, (GROUPS, 1), 2, TOK_DEV // 2 + 2, dtype=jnp.int32)
    coin_flips = jax.random.randint(third_key, (GROUPS, SEQ), 0, 12, dtype=jnp.int32) == 0
    outside = (places < long_start) | (places > long_finish)
    starts = coin_flips & outside | (places == 0) | (places == long_start) | (places == long_finish) | (places == SEQ - 1)
    return lax.cummax(jnp.where(starts, places, 0), axis=1).astype(jnp.int32)


def block_scale(stream_key, dims, cuts, least, top_value):
    level = 1.0
    for axis_at, parts in cuts:
        heights = jax.random.uniform(jax.random.fold_in(jax.random.fold_in(stream_key, 6), axis_at), (parts,), jnp.float32, least / len(cuts), top_value / len(cuts))
        level = level * jnp.repeat(jnp.exp(heights), dims[axis_at] // parts).reshape((-1,) + (1,) * (len(dims) - 1 - axis_at))
    return level


def assign_block(rng, own, number, rows, number_of, top, reach, skew):
    sequence = jax.random.permutation(rng, number_of)
    heavy_load, ordinary = portions_of(number_of, rows * top, reach, skew, True), portions_of(number_of, rows * top, reach, skew, False)
    places = jnp.arange(number_of)

    def named(tallies, turn):
        used = int((tallies > 0).sum())
        fixed = max(1, used // 4)
        shifted = fixed + (places - fixed + turn * (used - fixed)) % max(1, number_of - fixed)
        return jnp.zeros((number_of,), jnp.int32).at[sequence[jnp.where(places < fixed, places, shifted)]].set(jnp.asarray(tallies, jnp.int32))

    tallies = jnp.where(number % 4 == 0, named(heavy_load, number // 4), named(ordinary, number - number // 4 - 1))
    mixed = jax.random.permutation(jax.random.fold_in(own, 3), number_of)
    giver, taker = mixed[0:number_of // 2 * 2:2], mixed[1:number_of // 2 * 2:2]
    slack = jnp.minimum(tallies[giver] - 1, reach - tallies[taker]) // 2
    slack = jnp.where((giver == sequence[0]) | (taker == sequence[0]) | (tallies[taker] == 0), 0, jnp.maximum(slack, 0))
    shifted = jax.random.randint(jax.random.fold_in(own, 4), (number_of // 2,), 0, 1 << 20) % (slack + 1)
    tallies = tallies.at[giver].add(-shifted).at[taker].add(shifted)
    items = jnp.searchsorted(jnp.cumsum(tallies), jnp.arange(rows * top), side="right").astype(jnp.int32)
    grid = items.reshape(top, rows).T
    grid = grid[jax.random.permutation(jax.random.fold_in(own, 1), rows)]
    turn = jax.random.randint(jax.random.fold_in(own, 2), (rows, 1), 0, top)
    return jnp.take_along_axis(grid, (jnp.arange(top)[None, :] + turn) % top, axis=1)


def portions_of(count, total, bound, slope, full):
    loads = [(1 << 20) // math.isqrt(grade ** slope) + 1 for grade in range(1, count + 1)]
    largest = bound if full else min(bound, max(-(-total // count), total * loads[0] // sum(loads)))
    least = 1 if total - largest >= count - 1 else 0
    holding, surplus = [largest] + [least] * (count - 1), total - largest - least * (count - 1)
    while surplus > 0:
        movable = [i for i in range(1, count) if holding[i] < largest] or [i for i in range(1, count) if holding[i] < bound]
        mass, left = sum([loads[i] for i in movable]), surplus
        for i in movable:
            more = min(bound - holding[i], max(1, left * loads[i] // mass), surplus)
            holding[i] = holding[i] + more
            surplus = surplus - more
    return np.array(holding)


def centred(stream_key, shape, width, limit, shards=(), held_as=jnp.bfloat16):
    level = block_scale(stream_key, shape, shards, -0.22, 0.18) if shards else 1.0
    values = jax.random.normal(stream_key, shape, jnp.float32) * width * level
    return jnp.minimum(jnp.maximum(values, -limit), limit).astype(held_as)


def setup_inputs(seed: int = 0) -> dict:
    arg_keys = jax.random.split(jax.random.key(seed), 14)
    layer_input = centred(arg_keys[0], (TOKENS, D), 1.0, 6.0, ((0, 32),))
    kv_weight = centred(arg_keys[1], (2 * KV, D), D ** -0.5, 0.125, ((1, 8),), jnp.float32)
    norm_gains = jnp.clip(1.0 + 0.1 * jax.random.normal(arg_keys[2], (2, D), jnp.float32), 0.5, 1.5)
    query_maps = centred(arg_keys[3], (EXPERTS, D, KV), D ** -0.5, 0.125, ((0, 4), (1, 8)), jnp.float32)
    output_maps = centred(arg_keys[4], (EXPERTS, KV, D), (max(KV // 64, 1)) ** -0.5, 1.0, ((0, 4), (1, 8)), jnp.float32)
    gate_up_maps = centred(arg_keys[5], (EXPERTS, D, 2 * FF), D ** -0.5, 0.125, ((0, 4), (1, 8)), jnp.float32)
    down_maps = centred(arg_keys[6], (EXPERTS, FF, D), (max(FF // 4, 1)) ** -0.5, 0.15625, ((0, 4), (1, 8)), jnp.float32)
    att_routes_keys = jax.random.split(jax.random.fold_in(arg_keys[7], 1), GROUPS * SEQ // TOK_DEV)
    att_routes_turns = jax.random.permutation(jax.random.fold_in(arg_keys[7], 3), GROUPS * SEQ // TOK_DEV)
    att_routes = jax.vmap(lambda own, number: assign_block(jax.random.fold_in(arg_keys[7], 2), own, number, TOK_DEV, EXPERTS, TOP, CAPACITY, 1))(att_routes_keys, att_routes_turns).reshape((GROUPS, SEQ, TOP))
    att_gates = jnp.clip(0.25 + 0.5 * jax.random.uniform(arg_keys[8], (TOKENS, TOP), jnp.float32) ** block_scale(arg_keys[8], (TOKENS, TOP), ((0, 32),), -0.2, 0.2), 0.25, 0.75)
    mlp_routes_keys = jax.random.split(jax.random.fold_in(arg_keys[9], 1), GROUPS * SEQ // TOK_DEV)
    mlp_routes_turns = jax.random.permutation(jax.random.fold_in(arg_keys[9], 3), GROUPS * SEQ // TOK_DEV)
    mlp_routes = jax.vmap(lambda own, number: assign_block(jax.random.fold_in(arg_keys[9], 2), own, number, TOK_DEV, EXPERTS, TOP, CAPACITY, 1))(mlp_routes_keys, mlp_routes_turns).reshape((GROUPS, SEQ, TOP))
    mlp_gates = jnp.clip(0.25 + 0.5 * jax.random.uniform(arg_keys[10], (TOKENS, TOP), jnp.float32) ** block_scale(arg_keys[10], (TOKENS, TOP), ((0, 32),), -0.2, 0.2), 0.25, 0.75)
    segments = draw_segments(jax.random.fold_in(arg_keys[13], 71), 0)
    cotangent = centred(arg_keys[12], (TOKENS, D), 1.0, 6.0, ((0, 32),))
    return {"layer_input": layer_input, "kv_weight": kv_weight, "norm_gains": norm_gains, "query_maps": query_maps, "output_maps": output_maps, "gate_up_maps": gate_up_maps, "down_maps": down_maps, "att_routes": att_routes, "att_gates": att_gates, "mlp_routes": mlp_routes, "mlp_gates": mlp_gates, "segments": segments, "cotangent": cotangent}


EPSILON = 1e-06
NEGATIVE = -1e+30
HIGHEST = lax.Precision.HIGHEST

@jax.custom_vjp
def low(v):
    return lax.optimization_barrier(v.astype(jnp.bfloat16)).astype(jnp.float32)

@jax.custom_vjp
def low_back(v):
    return v

def low_keep(v):
    return (low(v), None)

def low_pass(kept, grad):
    return (grad,)

def back_keep(v):
    return (v, None)

def back_low(kept, grad):
    return (low(grad),)
low.defvjp(low_keep, low_pass)
low_back.defvjp(back_keep, back_low)

def route_slots(routes, sources, capacity, experts):
    routes_flat = routes.reshape(sources, -1).astype(jnp.int32)
    matches = (routes_flat[:, :, None] == jnp.arange(experts, dtype=jnp.int32)[None, None, :]).astype(jnp.int32)
    running = (jnp.cumsum(matches, axis=1) - 1).astype(jnp.int32)
    placed = lax.optimization_barrier(jnp.sum(matches * running, axis=2)).astype(jnp.int32)
    return (routes_flat * capacity + placed).astype(jnp.int32)

def slot_tokens(slots, sources, capacity, experts, choices_each):
    per_source = slots.shape[1]
    token_ids = (jnp.arange(sources * per_source, dtype=jnp.int32) // choices_each).reshape(sources, per_source)
    source_ids = jnp.arange(sources, dtype=jnp.int32)[:, None]
    table = jnp.zeros((sources, experts * capacity), jnp.int32).at[source_ids, slots].set(token_ids)
    return table.reshape(sources, experts, capacity)

def product(left, right):
    return jnp.dot(left, right, precision=HIGHEST)

def norm_rows(values, gain):
    inverse = lax.rsqrt(lax.optimization_barrier(jnp.mean(values * values, axis=-1, keepdims=True)) + EPSILON)
    return values * inverse * gain

def spread_rows(rows, slots):
    per_block = rows.reshape(N_EP, TOK_DEV, rows.shape[1])
    doubled = jnp.repeat(per_block, TOP, axis=1)
    source_ids = jnp.arange(N_EP, dtype=jnp.int32)[:, None]
    buffer = jnp.zeros((N_EP, EXPERTS * CAPACITY, rows.shape[1]), jnp.float32)
    buffer = buffer.at[source_ids, slots].set(doubled)
    return buffer.reshape(N_EP, EXPERTS, CAPACITY, -1).transpose(1, 0, 2, 3).reshape(EXPERTS, N_EP * CAPACITY, -1)

def gather_rows(results, slots):
    by_block = results.reshape(EXPERTS, N_EP, CAPACITY, -1).transpose(1, 0, 2, 3).reshape(N_EP, EXPERTS * CAPACITY, -1)
    picked = jnp.take_along_axis(by_block, slots[:, :, None], axis=1)
    return picked.reshape(SEQ, TOP, -1)

def attend(queries, keys_values, places, segment_ids):
    rows_count = queries.shape[0]
    query_heads = queries.reshape(rows_count, HEADS, HEAD_DIM)
    key_heads = keys_values[:, :HEADS * HEAD_DIM].reshape(SEQ, HEADS, HEAD_DIM)
    value_heads = keys_values[:, HEADS * HEAD_DIM:].reshape(SEQ, HEADS, HEAD_DIM)
    key_places = jnp.arange(SEQ, dtype=jnp.int32)
    allowed = (segment_ids[None, :] == jnp.take(segment_ids, places)[:, None]) & (key_places[None, :] <= places[:, None])
    scores = low_back(jnp.einsum('rhd,khd->hrk', query_heads, key_heads, precision=HIGHEST) * HEAD_DIM ** (-0.5))
    masked = jnp.where(allowed[None], scores, NEGATIVE)
    row_peak = lax.optimization_barrier(jnp.max(masked, axis=-1, keepdims=True))
    exponent = jnp.exp(masked - row_peak)
    attention_weights = exponent / lax.optimization_barrier(jnp.sum(exponent, axis=-1, keepdims=True))
    mixed = jnp.einsum('hrk,khd->rhd', low(attention_weights), value_heads, precision=HIGHEST)
    return mixed.reshape(rows_count, HEADS * HEAD_DIM)

def group_forward(group_data, weights):
    input_rows, att_routes_g, att_gates_g, mlp_routes_g, mlp_gates_g, segment_ids = group_data
    kv_low, gains_low, query_low, output_low, gate_up_low, down_low = weights
    att_slots = route_slots(att_routes_g, N_EP, CAPACITY, EXPERTS)
    mlp_slots = route_slots(mlp_routes_g, N_EP, CAPACITY, EXPERTS)
    query_places = slot_tokens(att_slots, N_EP, CAPACITY, EXPERTS, TOP).transpose(1, 0, 2).reshape(EXPERTS, N_EP * CAPACITY)
    normed_one = low(norm_rows(input_rows, gains_low[0]))
    keys_values = low_back(low(product(normed_one, kv_low.T)))
    att_in = low_back(spread_rows(normed_one, att_slots))

    def attention_expert(operands):
        rows_in, query_w, output_w, places = operands
        queries = low_back(low(product(rows_in, query_w)))
        heads_out = jax.checkpoint(attend)(queries, keys_values, places, segment_ids)
        heads_out = low_back(low(heads_out))
        return low_back(low(product(heads_out, output_w)))
    att_rows = lax.map(attention_expert, (att_in, query_low, output_low, query_places))
    residual_one = input_rows + lax.optimization_barrier(jnp.sum(att_gates_g[:, :, None] * gather_rows(att_rows, att_slots), axis=1))
    normed_two = low(norm_rows(residual_one, gains_low[1]))
    mlp_in = low_back(spread_rows(normed_two, mlp_slots))

    def mlp_expert(operands):
        rows_in, gate_up_w, down_w = operands
        gate_up = low_back(product(rows_in, gate_up_w))
        activated = low(jax.nn.silu(gate_up[:, :FF]) * gate_up[:, FF:])
        return low_back(low(product(activated, down_w)))
    mlp_rows = lax.map(mlp_expert, (mlp_in, gate_up_low, down_low))
    return residual_one + lax.optimization_barrier(jnp.sum(mlp_gates_g[:, :, None] * gather_rows(mlp_rows, mlp_slots), axis=1))

def reference(layer_input, kv_weight, norm_gains, query_maps, output_maps, gate_up_maps, down_maps, att_routes, att_gates, mlp_routes, mlp_gates, segments, cotangent):

    def forward(input_float, kv_master, gain_master, query_master, output_master, gate_up_master, down_master):
        weights = (low(kv_master), low(gain_master), low(query_master), low(output_master), low(gate_up_master), low(down_master))
        grouped = (input_float.reshape(GROUPS, SEQ, D), att_routes, att_gates.reshape(GROUPS, SEQ, TOP), mlp_routes, mlp_gates.reshape(GROUPS, SEQ, TOP), segments)
        results = lax.map(lambda group_data: group_forward(group_data, weights), grouped)
        return results.reshape(TOKENS, D)
    result, pullback = jax.vjp(forward, layer_input.astype(jnp.float32), kv_weight, norm_gains, query_maps, output_maps, gate_up_maps, down_maps)
    grads = pullback(cotangent.astype(jnp.float32))
    return (result.astype(jnp.bfloat16), grads[0], grads[1], grads[2], grads[3], grads[4], grads[5], grads[6])
```

```python
import functools

import jax
import jax.numpy as jnp
from jax import lax
from jax.experimental import pallas as pl
from jax.experimental.pallas import tpu as pltpu
from jax.sharding import PartitionSpec as P

HEADS = 16
HEAD_DIM = 128
TOP = 2


EPSILON = 1e-06
NEGATIVE = -1e30
CONTRACT_ROWS = (((0,), (0,)), ((), ()))
CONTRACT_COLUMNS = (((1,), (1,)), ((), ()))
BF16 = jnp.bfloat16
F32 = jnp.float32
VMEM_BYTES = 56 * 2**20
TILE = 512


def normalize(values):
    inverse = lax.rsqrt(jnp.mean(values * values, axis=-1, keepdims=True) + EPSILON)
    return (inverse, values * inverse)


def norm_backward(grad_normed, unit, inverse, gain):
    grad_unit = grad_normed * gain
    inner = jnp.mean(grad_unit * unit, axis=-1, keepdims=True)
    return (inverse * (grad_unit - unit * inner), jnp.sum(grad_normed * unit, axis=0))


def dot(left, right, dims=(((1,), (0,)), ((), ()))):
    return lax.dot_general(left, right, dims, preferred_element_type=F32)


def high_low(values):
    high = values.astype(BF16)
    return high, (values - high.astype(F32)).astype(BF16)


def expert_places(routes, experts):
    tokens = routes.shape[1]
    ids = jnp.arange(experts, dtype=jnp.int32)
    named = jnp.any(routes[:, None, :, :] == ids[None, :, None, None], axis=3)
    before = (jnp.arange(tokens)[:, None] < jnp.arange(tokens)[None, :]).astype(BF16)
    place = lax.dot_general(
        named.astype(BF16), before, (((2,), (0,)), ((), ())), preferred_element_type=F32
    )
    return named, place.astype(jnp.int32)


def one_hot(named, place, capacity):
    rows = jnp.arange(capacity, dtype=jnp.int32)[:, None]
    return named[..., None, :] & (place[..., None, :] == rows)


def attend_forward_kernel(sources, query_ref, key_ref, value_ref, bounds_ref, out_ref, logsum_ref):
    head = pl.program_id(0)
    capacity = query_ref.shape[0] // sources
    tokens = key_ref.shape[0] // sources
    scaling = HEAD_DIM ** (-0.5)

    @pl.when(head == 0)
    def _():
        logsum_ref[...] = jnp.zeros_like(logsum_ref)

    for source in range(sources):
        rows = slice(source * capacity, (source + 1) * capacity)
        span = (source + 1) * tokens
        first = bounds_ref[rows, 0:1]
        last = bounds_ref[rows, 1:2]
        scores = dot(query_ref[rows, :], key_ref[:span, :], CONTRACT_COLUMNS) * scaling
        places = lax.broadcasted_iota(jnp.int32, scores.shape, 1)
        scores = jnp.where((places >= first) & (places <= last), scores, NEGATIVE)
        peak = jnp.max(scores, axis=1, keepdims=True)
        exponent = jnp.exp(scores - peak)
        total = jnp.sum(exponent, axis=1, keepdims=True)
        probs = (exponent * (1.0 / total)).astype(BF16)
        out_ref[rows, :] = dot(probs, value_ref[:span, :]).astype(BF16)
        lanes = lax.broadcasted_iota(jnp.int32, (capacity, 128), 1)
        logsum_ref[rows, :] = jnp.where(lanes == head, peak + jnp.log(total), logsum_ref[rows, :])


def attend_forward(queries, keys_values, bounds, sources):
    rows, features = queries.shape
    seq = keys_values.shape[0]
    pairs = (sources + 1) / (2 * sources)
    return pl.pallas_call(
        functools.partial(attend_forward_kernel, sources),
        grid=(HEADS,),
        in_specs=[
            pl.BlockSpec((rows, HEAD_DIM), lambda h: (0, h)),
            pl.BlockSpec((seq, HEAD_DIM), lambda h: (0, h)),
            pl.BlockSpec((seq, HEAD_DIM), lambda h: (0, h + HEADS)),
            pl.BlockSpec((rows, 2), lambda h: (0, 0)),
        ],
        out_specs=[
            pl.BlockSpec((rows, HEAD_DIM), lambda h: (0, h)),
            pl.BlockSpec((rows, 128), lambda h: (0, 0)),
        ],
        out_shape=[
            jax.ShapeDtypeStruct((rows, features), BF16),
            jax.ShapeDtypeStruct((rows, 128), F32),
        ],
        compiler_params=pltpu.CompilerParams(vmem_limit_bytes=VMEM_BYTES),
        cost_estimate=pl.CostEstimate(
            flops=int(4 * rows * seq * features * pairs),
            bytes_accessed=4 * (rows + seq) * features,
            transcendentals=int(HEADS * rows * seq * pairs),
        ),
        name="attend_forward",
    )(queries, keys_values, keys_values, bounds)


def attend_backward_kernel(
    sources,
    start,
    query_ref,
    key_ref,
    value_ref,
    grad_ref,
    bounds_ref,
    logsum_ref,
    grad_query_ref,
    grad_key_ref,
    grad_value_ref,
    key_total,
    value_total,
):
    head = pl.program_id(0) + start
    capacity = query_ref.shape[0] // sources
    tokens = key_ref.shape[0] // sources
    scaling = HEAD_DIM ** (-0.5)
    for source in reversed(range(sources)):
        rows = slice(source * capacity, (source + 1) * capacity)
        span = (source + 1) * tokens
        first = bounds_ref[rows, 0:1]
        last = bounds_ref[rows, 1:2]
        query = query_ref[rows, :]
        grad = grad_ref[rows, :]
        lanes = lax.broadcasted_iota(jnp.int32, (capacity, 128), 1)
        logsum = jnp.sum(
            jnp.where(lanes == head, logsum_ref[rows, :], 0.0), axis=1, keepdims=True
        )
        scores = dot(query, key_ref[:span, :], CONTRACT_COLUMNS) * scaling
        places = lax.broadcasted_iota(jnp.int32, scores.shape, 1)
        scores = jnp.where((places >= first) & (places <= last), scores, NEGATIVE)
        probs = jnp.exp(scores - logsum)
        grad_probs = dot(grad, value_ref[:span, :], CONTRACT_COLUMNS)
        weighted = probs * grad_probs
        correction = jnp.sum(weighted, axis=1, keepdims=True)
        grad_scores = (weighted - probs * correction).astype(BF16)
        grad_query_ref[rows, :] = (dot(grad_scores, key_ref[:span, :]) * scaling).astype(BF16)
        key_part = dot(grad_scores, query, CONTRACT_ROWS)
        value_part = dot(probs.astype(BF16), grad, CONTRACT_ROWS)
        if source == sources - 1:
            key_total[...] = key_part
            value_total[...] = value_part
        else:
            key_total[:span, :] += key_part
            value_total[:span, :] += value_part
    grad_key_ref[...] = (key_total[...] * scaling).astype(BF16)
    grad_value_ref[...] = value_total[...].astype(BF16)


def attend_backward(queries, keys_values, grads, bounds, logsums, sources, start, heads):
    rows = queries.shape[0]
    features = heads * HEAD_DIM
    seq = keys_values.shape[0]
    pairs = (sources + 1) / (2 * sources)
    return pl.pallas_call(
        functools.partial(attend_backward_kernel, sources, start),
        grid=(heads,),
        in_specs=[
            pl.BlockSpec((rows, HEAD_DIM), lambda h: (0, h + start)),
            pl.BlockSpec((seq, HEAD_DIM), lambda h: (0, h + start)),
            pl.BlockSpec((seq, HEAD_DIM), lambda h: (0, h + start + HEADS)),
            pl.BlockSpec((rows, HEAD_DIM), lambda h: (0, h + start)),
            pl.BlockSpec((rows, 2), lambda h: (0, 0)),
            pl.BlockSpec((rows, 128), lambda h: (0, 0)),
        ],
        out_specs=[
            pl.BlockSpec((rows, HEAD_DIM), lambda h: (0, h)),
            pl.BlockSpec((seq, HEAD_DIM), lambda h: (0, h)),
            pl.BlockSpec((seq, HEAD_DIM), lambda h: (0, h)),
        ],
        out_shape=[
            jax.ShapeDtypeStruct((rows, features), BF16),
            jax.ShapeDtypeStruct((seq, features), BF16),
            jax.ShapeDtypeStruct((seq, features), BF16),
        ],
        scratch_shapes=[pltpu.VMEM((seq, HEAD_DIM), F32), pltpu.VMEM((seq, HEAD_DIM), F32)],
        compiler_params=pltpu.CompilerParams(vmem_limit_bytes=VMEM_BYTES),
        cost_estimate=pl.CostEstimate(
            flops=int(10 * rows * seq * features * pairs),
            bytes_accessed=8 * (rows + seq) * features,
            transcendentals=int(heads * rows * seq * pairs),
        ),
        name="attend_backward",
    )(queries, keys_values, keys_values, grads, bounds, logsums)


def feed_kernel(in_ref, grad_ref, gate_up_ref, down_ref, act_ref, grad_gate_up_ref):
    rows = in_ref.shape[0]
    step = rows // 3
    units = down_ref.shape[0]

    @pl.loop(0, 3)
    def _(part):
        here = pl.ds(pl.multiple_of(part * step, step), step)
        inputs = in_ref[here, :]
        gate = dot(inputs, gate_up_ref[:, :units])
        up = dot(inputs, gate_up_ref[:, units:])
        grad_act = dot(grad_ref[here, :], down_ref[...], CONTRACT_COLUMNS)
        sigmoid = jax.nn.sigmoid(gate)
        silu = gate * sigmoid
        act_ref[here, :] = (silu * up).astype(BF16)
        grad_gate_up_ref[here, :units] = (
            grad_act * up * sigmoid * (1.0 + gate * (1.0 - sigmoid))
        ).astype(BF16)
        grad_gate_up_ref[here, units:] = (grad_act * silu).astype(BF16)


def feed(inputs, grads, gate_up, down, offset):
    rows, width = inputs.shape
    units = gate_up.shape[1] // 2
    tiles = units // TILE
    start = offset // TILE
    return pl.pallas_call(
        feed_kernel,
        grid=(tiles,),
        in_specs=[
            pl.BlockSpec((rows, width), lambda j: (0, 0)),
            pl.BlockSpec((rows, width), lambda j: (0, 0)),
            pl.BlockSpec((width, 2 * TILE), lambda j: (0, j)),
            pl.BlockSpec((TILE, width), lambda j: (j + start, 0)),
        ],
        out_specs=[
            pl.BlockSpec((rows, TILE), lambda j: (0, j)),
            pl.BlockSpec((rows, 2 * TILE), lambda j: (0, j)),
        ],
        out_shape=[
            jax.ShapeDtypeStruct((rows, units), BF16),
            jax.ShapeDtypeStruct((rows, 2 * units), BF16),
        ],
        compiler_params=pltpu.CompilerParams(vmem_limit_bytes=VMEM_BYTES),
        cost_estimate=pl.CostEstimate(
            flops=6 * rows * width * units,
            bytes_accessed=6 * width * units + 4 * rows * width,
            transcendentals=rows * units,
        ),
        name="feed",
    )(inputs, grads, gate_up, down)


def assemble_kernel(tiles, per_chunk, *refs):
    out_ref = refs[-1]
    chunk = lax.rem(pl.program_id(0), tiles) // per_chunk
    for index, ref in enumerate(refs[:-1]):

        @pl.when(chunk == index)
        def _():
            out_ref[...] = ref[...].astype(F32)


def assemble(chunks, per_chunk):
    rows = chunks[0].shape[0]
    tiles = sum(chunk.shape[1] for chunk in chunks) // (2 * TILE)

    def place(index):
        count = chunks[index].shape[1] // (2 * TILE)

        def block(j):
            tile = j % tiles - index * per_chunk
            return (0, jnp.clip(tile, 0, count - 1) * 2 + j // tiles)

        return block

    return pl.pallas_call(
        functools.partial(assemble_kernel, tiles, per_chunk),
        grid=(2 * tiles,),
        in_specs=[pl.BlockSpec((rows, TILE), place(index)) for index in range(len(chunks))],
        out_specs=pl.BlockSpec((rows, TILE), lambda j: (0, j)),
        out_shape=jax.ShapeDtypeStruct((rows, 2 * tiles * TILE), F32),
        cost_estimate=pl.CostEstimate(
            flops=0, bytes_accessed=12 * rows * tiles * TILE, transcendentals=0
        ),
        name="assemble",
    )(*chunks)


def transpose_kernel(each, first_ref, second_ref, out_ref):
    second = lax.rem(lax.div(pl.program_id(0), each), 2)

    @pl.when(second == 0)
    def _():
        out_ref[...] = first_ref[...].astype(F32).T

    @pl.when(second == 1)
    def _():
        out_ref[...] = second_ref[...].astype(F32).T


def transpose(first, second):
    rows, columns = first.shape
    each = columns // 2 // TILE
    spec = pl.BlockSpec((rows, TILE), lambda j: (0, j // (2 * each) * each + j % each))
    return pl.pallas_call(
        functools.partial(transpose_kernel, each),
        grid=(4 * each,),
        in_specs=[spec, spec],
        out_specs=pl.BlockSpec((TILE, rows), lambda j: (j, 0)),
        out_shape=jax.ShapeDtypeStruct((2 * columns, rows), F32),
        cost_estimate=pl.CostEstimate(
            flops=0, bytes_accessed=12 * rows * columns, transcendentals=0
        ),
        name="transpose",
    )(first, second)


def rotate_gather(block, axis):
    size = lax.axis_size(axis)
    me = lax.axis_index(axis)
    parts = [block]
    for shift in range(1, size):
        parts.append(lax.ppermute(block, axis, [(i, (i + shift) % size) for i in range(size)]))
    stacked = jnp.stack(parts[::-1])
    doubled = jnp.concatenate([stacked, stacked])
    return lax.dynamic_slice_in_dim(doubled, size - 1 - me, size, 0)


def after(values, *tokens):
    return lax.optimization_barrier((values, *tokens))[0]


def flip(values, bit):
    size = lax.axis_size("grp")
    return lax.ppermute(values, "grp", [(i, i ^ (1 << bit)) for i in range(size)])


class Gather:
    def __init__(self, shards, orders):
        self.pieces = [{0: shard} for shard in shards]
        self.orders = [list(order) for order in orders]

    def step(self, *tokens):
        for pieces, order in zip(self.pieces, self.orders):
            bit = order.pop(0)
            for place, piece in list(pieces.items()):
                if tokens:
                    piece = after(piece, *tokens)
                pieces[place ^ (1 << bit)] = flip(piece, bit)

    def finish(self, *tokens):
        size = lax.axis_size("grp")
        me = lax.axis_index("grp")
        rows = [pieces[0].shape[0] for pieces in self.pieces]
        whole = jnp.zeros((size, sum(rows), self.pieces[0][0].shape[1]), BF16)
        offset = 0
        for pieces, count in zip(self.pieces, rows):
            for place, piece in pieces.items():
                if tokens:
                    piece = after(piece, *tokens)
                whole = lax.dynamic_update_slice(whole, piece[None], (me ^ place, offset, 0))
            offset += count
        return whole.reshape(size * sum(rows), -1)


def gather_gains(gains):
    size = lax.axis_size("grp")
    me = lax.axis_index("grp")
    for bit in range(size.bit_length() - 1):
        other = flip(gains, bit)
        upper = (me >> bit) & 1
        gains = jnp.where(
            upper == 0,
            jnp.concatenate([gains, other], axis=1),
            jnp.concatenate([other, gains], axis=1),
        )
    return gains


class Scatter:
    def __init__(self, terms, order):
        self.terms = terms
        self.order = list(order)

    def step(self, *tokens):
        if not self.order:
            return
        bit = self.order.pop(0)
        axis = sum(other > bit for other in self.order)
        mine = (lax.axis_index("grp") >> bit) & 1
        terms = self.terms
        if tokens:
            terms = [after(term, *tokens) for term in terms]

        def part(term, which):
            return lax.dynamic_index_in_dim(term, which, axis, keepdims=False)

        self.sent = sum(part(term, 1 - mine).astype(F32) for term in terms).astype(BF16)
        self.terms = [part(term, mine) for term in terms] + [flip(self.sent, bit)]

    def finish(self):
        while self.order:
            self.step()
        return sum(term.astype(F32) for term in self.terms)


def core_split(values, groups):
    rows, columns = values.shape
    n = columns // groups
    mine = lax.axis_index("grp") & 1
    even = jnp.concatenate([values[:, i * n : (i + 1) * n] for i in range(0, groups, 2)], axis=1)
    odd = jnp.concatenate([values[:, i * n : (i + 1) * n] for i in range(1, groups, 2)], axis=1)
    return jnp.where(mine == 0, even, odd), jnp.where(mine == 0, odd, even)


def scatter_product(split, rights, groups, first=0):
    bits = groups.bit_length() - 1
    results = []
    for place, right in enumerate(rights):
        order = list(range(1, bits))
        if (place + first) % 2:
            order = order[::-1]
        sent = dot(split[1], right, CONTRACT_ROWS).astype(BF16)
        got = flip(sent, 0)
        kept = dot(split[0], right, CONTRACT_ROWS).astype(BF16)
        shape = (2,) * (bits - 1) + (-1, right.shape[1])
        results.append(Scatter([kept.reshape(shape), got.reshape(shape)], order))
        results[-1].sent = sent
    return results


def steps(scatters, *tokens):
    for scatter in scatters:
        scatter.step(*tokens)


def finish(scatters):
    return jnp.concatenate([scatter.finish() for scatter in scatters], axis=1)


def halves(values):
    middle = values.shape[1] // 2
    return values[:, :middle], values[:, middle:]


def exchange(values, experts):
    rows, width = values.shape
    return lax.all_to_all(
        values.reshape(experts, rows // experts, width),
        "ep",
        split_axis=0,
        concat_axis=0,
        tiled=True,
    ).reshape(rows, width)


def local(
    layer_input,
    kv_weight,
    norm_gains,
    query_maps,
    output_maps,
    gate_up_maps,
    down_maps,
    att_routes,
    att_gates,
    mlp_routes,
    mlp_gates,
    segments,
    cotangent,
):
    experts = lax.axis_size("ep")
    groups = lax.axis_size("grp")
    bits = groups.bit_length() - 1
    me_index = lax.axis_index("ep")
    tok_dev = layer_input.shape[0]
    model_width = layer_input.shape[1]
    capacity = 3 * tok_dev // experts
    rows_total = experts * capacity
    hidden = gate_up_maps.shape[2] // 2

    def gather(shard):
        return lax.all_gather(shard, "grp", axis=0, tiled=True)

    gains_full = gather_gains(norm_gains.astype(BF16))
    gain_one = gains_full[0].astype(F32)
    gain_two = gains_full[1].astype(F32)
    xfloat = layer_input.astype(F32)
    inverse_one, unit_one = normalize(xfloat)
    normed_one = (unit_one * gain_one).astype(BF16)
    normed_all = rotate_gather(normed_one, "ep")

    orders = list(range(1, bits)) + [0], list(range(1, bits))[::-1] + [0]
    kv_shard = kv_weight.T.astype(BF16)
    query_shard = after(query_maps[0], normed_one).astype(BF16)
    output_shard = after(output_maps[0], query_shard).astype(BF16)
    kv_full = gather(kv_shard)
    query_gather = Gather([query_shard], orders[:1])
    output_gather = Gather([output_shard], orders[1:])
    query_gather.step()
    output_gather.step()
    units = TILE * 4
    cuts = [(start, min(units, hidden - start)) for start in range(0, hidden, units)]

    def tiles_of(start, size):
        return [
            slice(at, at + TILE)
            for tile in range(start, start + size, TILE)
            for at in (tile, hidden + tile)
        ]

    gate_up_full = []
    shard = output_shard
    for index, cut in enumerate(cuts):
        maps = after(gate_up_maps, shard)
        shard = jnp.concatenate([maps[0, :, here] for here in tiles_of(*cut)], axis=1).astype(BF16)
        gate_up_full.append(gather(shard))
        if index == 0:
            query_gather.step(shard)
            output_gather.step(shard)
            shard = after(down_maps[0], shard).astype(BF16)
            down_full = gather(shard)
    while query_gather.orders[0]:
        query_gather.step(normed_all)
        output_gather.step(normed_all)

    att_named, att_place = expert_places(att_routes[0].reshape(experts, tok_dev, TOP), experts)
    mlp_named, mlp_place = expert_places(mlp_routes[0].reshape(experts, tok_dev, TOP), experts)

    def mine(values, axis):
        return lax.dynamic_index_in_dim(values, me_index, axis, keepdims=False)

    att_pick = one_hot(mine(att_named, 1), mine(att_place, 1), capacity)
    att_send = one_hot(mine(att_named, 0), mine(att_place, 0), capacity).reshape(
        rows_total, tok_dev
    )
    mlp_send = one_hot(mine(mlp_named, 0), mine(mlp_place, 0), capacity).reshape(
        rows_total, tok_dev
    )

    def gates_at(send, routes, gates):
        ids = jnp.arange(experts, dtype=jnp.int32)
        routes = mine(routes.reshape(experts, tok_dev, TOP), 0)
        per_expert = jnp.sum(jnp.where(routes[None] == ids[:, None, None], gates[None], 0.0), axis=2)
        spread = jnp.where(
            send.reshape(experts, capacity, tok_dev), per_expert[:, None, :], 0.0
        ).reshape(rows_total, tok_dev)
        return high_low(spread)

    att_high, att_low = gates_at(att_send, att_routes, att_gates)
    mlp_high, mlp_low = gates_at(mlp_send, mlp_routes, mlp_gates)
    mlp_send = mlp_send.astype(BF16)
    places = jnp.arange(experts * tok_dev, dtype=jnp.int32).reshape(experts, 1, tok_dev)
    starts = segments[0].reshape(experts, 1, tok_dev)
    bounds = jnp.stack(
        [
            jnp.sum(jnp.where(att_pick, starts, 0), axis=2).reshape(-1),
            jnp.sum(jnp.where(att_pick, places, 0), axis=2).reshape(-1),
        ],
        axis=1,
    )
    att_pick = att_pick.astype(BF16)

    cotangent_send = (dot(mlp_high, cotangent) + dot(mlp_low, cotangent)).astype(BF16)
    cotangent_send = after(cotangent_send, normed_all)
    grad_mlp_rows = exchange(cotangent_send, experts)
    att_in = (
        jnp.einsum(
            "sct,std->scd", att_pick, after(normed_all, cotangent_send), preferred_element_type=F32
        )
        .astype(BF16)
        .reshape(rows_total, model_width)
    )
    normed_all = normed_all.reshape(experts * tok_dev, model_width)
    keys_values = dot(after(normed_all, att_in), kv_full).astype(BF16)
    query_full = query_gather.finish(keys_values)
    queries = dot(after(att_in, keys_values), query_full).astype(BF16)
    output_full = output_gather.finish(queries)
    att_heads, logsums = attend_forward(queries, keys_values, bounds, experts)
    att_rows = dot(after(att_heads, grad_mlp_rows), output_full).astype(BF16)
    att_back = exchange(att_rows, experts)
    residual_one = (
        xfloat + dot(att_high, att_back, CONTRACT_ROWS) + dot(att_low, att_back, CONTRACT_ROWS)
    )

    inverse_two, unit_two = normalize(residual_one)
    normed_two = (unit_two * gain_two).astype(BF16)
    mlp_given = dot(mlp_send, normed_two).astype(BF16)
    mlp_in = exchange(mlp_given, experts)
    grad_mlp_in = 0.0
    acts, weight_grads = [], []
    feed_in = mlp_in
    for (start, size), gate_up in zip(cuts, gate_up_full):
        act, grad_gate_up = feed(feed_in, grad_mlp_rows, gate_up, down_full, start)
        grad_mlp_in = grad_mlp_in + dot(grad_gate_up, gate_up, CONTRACT_COLUMNS)
        acts.append(act)
        if start + size == hidden:
            grad_mlp_in = grad_mlp_in.astype(BF16)
            break
        weight_grad = dot(mlp_in, after(grad_gate_up, grad_mlp_in), CONTRACT_ROWS).astype(BF16)
        weight_grads.append(
            lax.psum_scatter(weight_grad, "grp", scatter_dimension=0, tiled=True)
        )
        feed_in = after(mlp_in, weight_grad)
    activated = after(jnp.concatenate(acts, axis=1), grad_mlp_in)
    down_scatter = scatter_product(core_split(activated, groups), halves(grad_mlp_rows), groups)
    mlp_returned = after(
        exchange(grad_mlp_in, experts),
        *[scatter.terms[0] for scatter in down_scatter],
        *[scatter.sent for scatter in down_scatter],
    )

    grad_final = cotangent.astype(F32)
    grad_normed_two = dot(mlp_send, mlp_returned, CONTRACT_ROWS)
    grad_inner_two, grad_gain_two = norm_backward(grad_normed_two, unit_two, inverse_two, gain_two)
    grad_residual = grad_final + grad_inner_two

    res_high, res_low = high_low(grad_residual)
    sent_four = (
        dot(att_high, res_high) + dot(att_low, res_high) + dot(att_high, res_low)
    ).astype(BF16)
    mlp_rows = dot(after(activated, sent_four), down_full).astype(BF16)
    weight_grad = dot(mlp_in, after(grad_gate_up, mlp_rows), CONTRACT_ROWS).astype(BF16)
    weight_grads.append(lax.psum_scatter(weight_grad, "grp", scatter_dimension=0, tiled=True))
    steps(down_scatter, mlp_rows)
    grad_att_rows = after(
        exchange(sent_four, experts),
        mlp_rows,
        weight_grad,
        *[scatter.sent for scatter in down_scatter],
    )
    mlp_back = exchange(after(mlp_rows, grad_att_rows), experts)
    grad_heads = dot(grad_att_rows, output_full, CONTRACT_COLUMNS).astype(BF16)
    normed_split = core_split(normed_all, groups)
    att_split = core_split(att_in, groups)
    half = HEADS // 2
    grad_one, keys_one, values_one = attend_backward(
        queries, keys_values, grad_heads, bounds, logsums, experts, 0, half
    )
    keys_one = after(keys_one, weight_grads[0], weight_grads[1])
    kv_one = scatter_product(normed_split, [keys_one, values_one], groups)
    grad_two, keys_two, values_two = attend_backward(
        after(queries, *[scatter.terms[0] for scatter in kv_one]),
        keys_values,
        grad_heads,
        bounds,
        logsums,
        experts,
        half,
        HEADS - half,
    )
    keys_two = after(keys_two, mlp_back)
    steps(down_scatter, keys_two)
    steps(kv_one, keys_two)
    ready = [scatter.sent for scatter in kv_one + down_scatter]
    query_one, query_two = halves(query_full)
    grad_att_in = (
        dot(after(grad_one, *ready), query_one, CONTRACT_COLUMNS)
        + dot(grad_two, query_two, CONTRACT_COLUMNS)
    ).astype(BF16)
    features = HEADS * HEAD_DIM
    middle = half * HEAD_DIM
    grad_all = (
        jnp.einsum(
            "sct,scd->std",
            att_pick,
            grad_att_in.reshape(experts, capacity, model_width),
            preferred_element_type=F32,
        ).reshape(experts * tok_dev, model_width)
        + dot(keys_one, kv_full[:, :middle], CONTRACT_COLUMNS)
        + dot(keys_two, kv_full[:, middle:features], CONTRACT_COLUMNS)
        + dot(values_one, kv_full[:, features : features + middle], CONTRACT_COLUMNS)
        + dot(values_two, kv_full[:, features + middle :], CONTRACT_COLUMNS)
    ).astype(BF16)
    grad_back = exchange(grad_all, experts)
    steps(kv_one, grad_all, weight_grads[-1])
    ready = [scatter.sent for scatter in kv_one]
    kv_two = scatter_product(normed_split, [after(keys_two, *ready), values_two], groups)
    ready = [scatter.terms[0] for scatter in kv_two]
    part_one = after(finish(kv_one), *ready).astype(BF16)
    kv_grad_one = lax.psum(part_one, "ep")
    steps(kv_two, part_one)
    ready = [scatter.sent for scatter in kv_two]
    query_scatter = scatter_product(att_split, [after(grad_one, *ready)], groups)
    query_scatter += scatter_product(att_split, [after(grad_two, *ready)], groups, 1)
    ready = [scatter.terms[0] for scatter in query_scatter]
    steps(kv_two, *ready)
    ready = [scatter.sent for scatter in kv_two]
    steps(query_scatter, *ready)
    ready = [scatter.sent for scatter in query_scatter]
    output_scatter = scatter_product(
        core_split(att_heads, groups), halves(after(grad_att_rows, *ready)), groups
    )
    ready = [scatter.terms[0] for scatter in output_scatter]
    part_two = after(finish(kv_two), *ready, grad_back).astype(BF16)
    kv_grad_two = lax.psum(after(part_two, kv_grad_one), "ep")
    steps(output_scatter, part_two)
    ready = [scatter.sent for scatter in output_scatter]
    down_grad = finish(down_scatter)[None]
    mlp_back = after(mlp_back, *ready)
    output = (
        residual_one + dot(mlp_high, mlp_back, CONTRACT_ROWS) + dot(mlp_low, mlp_back, CONTRACT_ROWS)
    ).astype(BF16)
    steps(query_scatter, output)
    weight_grads = [after(part, output) for part in weight_grads]
    ready = [scatter.sent for scatter in query_scatter]
    steps(output_scatter, *ready)
    ready = [scatter.sent for scatter in output_scatter]
    grad_normed_one = jnp.sum(
        after(grad_back, *ready).reshape(experts, tok_dev, model_width).astype(F32), axis=0
    )
    query_grad = finish(query_scatter)[None]
    output_grad = finish(output_scatter)[None]
    kv_grad = transpose(kv_grad_one, kv_grad_two)
    gate_up_grad = assemble(weight_grads, units // TILE)[None]
    grad_inner_one, grad_gain_one = norm_backward(grad_normed_one, unit_one, inverse_one, gain_one)
    grad_input = grad_residual + grad_inner_one

    gains_grad = jnp.stack([grad_gain_one, grad_gain_two])
    gains_grad = gains_grad.reshape((2,) + (2,) * bits + (-1,))
    for bit in reversed(range(bits)):
        mine_bit = (lax.axis_index("grp") >> bit) & 1
        kept = lax.dynamic_index_in_dim(gains_grad, mine_bit, 1, keepdims=False)
        sent = lax.dynamic_index_in_dim(gains_grad, 1 - mine_bit, 1, keepdims=False)
        gains_grad = kept + lax.ppermute(
            sent, "grp", [(i, i ^ (1 << bit)) for i in range(groups)]
        )
    for bit in range(experts.bit_length() - 1):
        gains_grad = gains_grad + lax.ppermute(
            gains_grad, "ep", [(i, i ^ (1 << bit)) for i in range(experts)]
        )
    return (
        output,
        grad_input,
        kv_grad,
        gains_grad,
        query_grad,
        output_grad,
        gate_up_grad,
        down_grad,
    )


def solution(mesh):
    placed = (
        P(("grp", "ep"), None),
        P(None, "grp"),
        P(None, "grp"),
        P("ep", "grp", None),
        P("ep", "grp", None),
        P("ep", "grp", None),
        P("ep", "grp", None),
        P("grp", None, None),
        P(("grp", "ep"), None),
        P("grp", None, None),
        P(("grp", "ep"), None),
        P("grp", None),
        P(("grp", "ep"), None),
    )
    return jax.shard_map(
        local,
        mesh=mesh,
        in_specs=placed,
        out_specs=(
            P(("grp", "ep"), None),
            P(("grp", "ep"), None),
            P(None, "grp"),
            P(None, "grp"),
            P("ep", "grp", None),
            P("ep", "grp", None),
            P("ep", "grp", None),
            P("ep", "grp", None),
        ),
        check_vma=False,
    )
```

```python
import functools

import jax
import jax.numpy as jnp
from jax import lax
from jax.experimental import pallas as pl
from jax.experimental.pallas import tpu as pltpu
from jax.sharding import PartitionSpec as P

HEADS = 16
HEAD_DIM = 128
TOP = 2


EPSILON = 1e-06
NEGATIVE = -1e30
CONTRACT_ROWS = (((0,), (0,)), ((), ()))
CONTRACT_COLUMNS = (((1,), (1,)), ((), ()))
BF16 = jnp.bfloat16
F32 = jnp.float32
VMEM_BYTES = 56 * 2**20
TILE = 512


def normalize(values):
    inverse = lax.rsqrt(jnp.mean(values * values, axis=-1, keepdims=True) + EPSILON)
    return (inverse, values * inverse)


def norm_backward(grad_normed, unit, inverse, gain):
    grad_unit = grad_normed * gain
    inner = jnp.mean(grad_unit * unit, axis=-1, keepdims=True)
    return (inverse * (grad_unit - unit * inner), jnp.sum(grad_normed * unit, axis=0))


def dot(left, right, dims=(((1,), (0,)), ((), ()))):
    return lax.dot_general(left, right, dims, preferred_element_type=F32)


def high_low(values):
    high = values.astype(BF16)
    return high, (values - high.astype(F32)).astype(BF16)


def expert_places(routes, experts):
    tokens = routes.shape[1]
    ids = jnp.arange(experts, dtype=jnp.int32)
    named = jnp.any(routes[:, None, :, :] == ids[None, :, None, None], axis=3)
    before = (jnp.arange(tokens)[:, None] < jnp.arange(tokens)[None, :]).astype(BF16)
    place = lax.dot_general(
        named.astype(BF16), before, (((2,), (0,)), ((), ())), preferred_element_type=F32
    )
    return named, place.astype(jnp.int32)


def one_hot(named, place, capacity):
    rows = jnp.arange(capacity, dtype=jnp.int32)[:, None]
    return named[..., None, :] & (place[..., None, :] == rows)


def attend_forward_kernel(sources, query_ref, key_ref, value_ref, bounds_ref, out_ref, logsum_ref):
    head = pl.program_id(0)
    capacity = query_ref.shape[0] // sources
    tokens = key_ref.shape[0] // sources
    scaling = HEAD_DIM ** (-0.5)

    @pl.when(head == 0)
    def _():
        logsum_ref[...] = jnp.zeros_like(logsum_ref)

    for source in range(sources):
        rows = slice(source * capacity, (source + 1) * capacity)
        span = (source + 1) * tokens
        first = bounds_ref[rows, 0:1]
        last = bounds_ref[rows, 1:2]
        scores = dot(query_ref[rows, :], key_ref[:span, :], CONTRACT_COLUMNS) * scaling
        places = lax.broadcasted_iota(jnp.int32, scores.shape, 1)
        scores = jnp.where((places >= first) & (places <= last), scores, NEGATIVE)
        peak = jnp.max(scores, axis=1, keepdims=True)
        exponent = jnp.exp(scores - peak)
        total = jnp.sum(exponent, axis=1, keepdims=True)
        probs = (exponent * (1.0 / total)).astype(BF16)
        out_ref[rows, :] = dot(probs, value_ref[:span, :]).astype(BF16)
        lanes = lax.broadcasted_iota(jnp.int32, (capacity, 128), 1)
        logsum_ref[rows, :] = jnp.where(lanes == head, peak + jnp.log(total), logsum_ref[rows, :])


def attend_forward(queries, keys_values, bounds, sources):
    rows, features = queries.shape
    seq = keys_values.shape[0]
    pairs = (sources + 1) / (2 * sources)
    return pl.pallas_call(
        functools.partial(attend_forward_kernel, sources),
        grid=(HEADS,),
        in_specs=[
            pl.BlockSpec((rows, HEAD_DIM), lambda h: (0, h)),
            pl.BlockSpec((seq, HEAD_DIM), lambda h: (0, 2 * h)),
            pl.BlockSpec((seq, HEAD_DIM), lambda h: (0, 2 * h + 1)),
            pl.BlockSpec((rows, 2), lambda h: (0, 0)),
        ],
        out_specs=[
            pl.BlockSpec((rows, HEAD_DIM), lambda h: (0, h)),
            pl.BlockSpec((rows, 128), lambda h: (0, 0)),
        ],
        out_shape=[
            jax.ShapeDtypeStruct((rows, features), BF16),
            jax.ShapeDtypeStruct((rows, 128), F32),
        ],
        compiler_params=pltpu.CompilerParams(vmem_limit_bytes=VMEM_BYTES),
        cost_estimate=pl.CostEstimate(
            flops=int(4 * rows * seq * features * pairs),
            bytes_accessed=4 * (rows + seq) * features,
            transcendentals=int(HEADS * rows * seq * pairs),
        ),
        name="attend_forward",
    )(queries, keys_values, keys_values, bounds)


def attend_backward_kernel(
    sources,
    start,
    query_ref,
    key_ref,
    value_ref,
    grad_ref,
    bounds_ref,
    logsum_ref,
    grad_query_ref,
    grad_both_ref,
    key_total,
    value_total,
):
    head = pl.program_id(0) + start
    capacity = query_ref.shape[0] // sources
    tokens = key_ref.shape[0] // sources
    scaling = HEAD_DIM ** (-0.5)
    for source in reversed(range(sources)):
        rows = slice(source * capacity, (source + 1) * capacity)
        span = (source + 1) * tokens
        first = bounds_ref[rows, 0:1]
        last = bounds_ref[rows, 1:2]
        query = query_ref[rows, :]
        grad = grad_ref[rows, :]
        lanes = lax.broadcasted_iota(jnp.int32, (capacity, 128), 1)
        logsum = jnp.sum(
            jnp.where(lanes == head, logsum_ref[rows, :], 0.0), axis=1, keepdims=True
        )
        scores = dot(query, key_ref[:span, :], CONTRACT_COLUMNS) * scaling
        places = lax.broadcasted_iota(jnp.int32, scores.shape, 1)
        scores = jnp.where((places >= first) & (places <= last), scores, NEGATIVE)
        probs = jnp.exp(scores - logsum)
        grad_probs = dot(grad, value_ref[:span, :], CONTRACT_COLUMNS)
        weighted = probs * grad_probs
        correction = jnp.sum(weighted, axis=1, keepdims=True)
        grad_scores = (weighted - probs * correction).astype(BF16)
        grad_query_ref[rows, :] = (dot(grad_scores, key_ref[:span, :]) * scaling).astype(BF16)
        key_part = dot(grad_scores, query, CONTRACT_ROWS)
        value_part = dot(probs.astype(BF16), grad, CONTRACT_ROWS)
        if source == sources - 1:
            key_total[...] = key_part
            value_total[...] = value_part
        else:
            key_total[:span, :] += key_part
            value_total[:span, :] += value_part
    grad_both_ref[:, :HEAD_DIM] = (key_total[...] * scaling).astype(BF16)
    grad_both_ref[:, HEAD_DIM:] = value_total[...].astype(BF16)


def attend_backward(queries, keys_values, grads, bounds, logsums, sources, start, heads):
    rows = queries.shape[0]
    features = heads * HEAD_DIM
    seq = keys_values.shape[0]
    pairs = (sources + 1) / (2 * sources)
    return pl.pallas_call(
        functools.partial(attend_backward_kernel, sources, start),
        grid=(heads,),
        in_specs=[
            pl.BlockSpec((rows, HEAD_DIM), lambda h: (0, h + start)),
            pl.BlockSpec((seq, HEAD_DIM), lambda h: (0, 2 * (h + start))),
            pl.BlockSpec((seq, HEAD_DIM), lambda h: (0, 2 * (h + start) + 1)),
            pl.BlockSpec((rows, HEAD_DIM), lambda h: (0, h + start)),
            pl.BlockSpec((rows, 2), lambda h: (0, 0)),
            pl.BlockSpec((rows, 128), lambda h: (0, 0)),
        ],
        out_specs=[
            pl.BlockSpec((rows, HEAD_DIM), lambda h: (0, h)),
            pl.BlockSpec((seq, 2 * HEAD_DIM), lambda h: (0, h)),
        ],
        out_shape=[
            jax.ShapeDtypeStruct((rows, features), BF16),
            jax.ShapeDtypeStruct((seq, 2 * features), BF16),
        ],
        scratch_shapes=[pltpu.VMEM((seq, HEAD_DIM), F32), pltpu.VMEM((seq, HEAD_DIM), F32)],
        compiler_params=pltpu.CompilerParams(vmem_limit_bytes=VMEM_BYTES),
        cost_estimate=pl.CostEstimate(
            flops=int(10 * rows * seq * features * pairs),
            bytes_accessed=8 * (rows + seq) * features,
            transcendentals=int(heads * rows * seq * pairs),
        ),
        name="attend_backward",
    )(queries, keys_values, keys_values, grads, bounds, logsums)


def feed_kernel(in_ref, grad_ref, gate_up_ref, down_ref, act_ref, grad_gate_up_ref):
    rows = in_ref.shape[0]
    step = rows // 3
    units = down_ref.shape[0]

    @pl.loop(0, 3)
    def _(part):
        here = pl.ds(pl.multiple_of(part * step, step), step)
        inputs = in_ref[here, :]
        gate = dot(inputs, gate_up_ref[:, :units])
        up = dot(inputs, gate_up_ref[:, units:])
        grad_act = dot(grad_ref[here, :], down_ref[...], CONTRACT_COLUMNS)
        sigmoid = jax.nn.sigmoid(gate)
        silu = gate * sigmoid
        act_ref[here, :] = (silu * up).astype(BF16)
        grad_gate_up_ref[here, :units] = (
            grad_act * up * sigmoid * (1.0 + gate * (1.0 - sigmoid))
        ).astype(BF16)
        grad_gate_up_ref[here, units:] = (grad_act * silu).astype(BF16)


def feed(inputs, grads, gate_up, down, offset):
    rows, width = inputs.shape
    units = gate_up.shape[1] // 2
    tiles = units // TILE
    start = offset // TILE
    return pl.pallas_call(
        feed_kernel,
        grid=(tiles,),
        in_specs=[
            pl.BlockSpec((rows, width), lambda j: (0, 0)),
            pl.BlockSpec((rows, width), lambda j: (0, 0)),
            pl.BlockSpec((width, 2 * TILE), lambda j: (0, j)),
            pl.BlockSpec((TILE, width), lambda j: (j + start, 0)),
        ],
        out_specs=[
            pl.BlockSpec((rows, TILE), lambda j: (0, j)),
            pl.BlockSpec((rows, 2 * TILE), lambda j: (0, j)),
        ],
        out_shape=[
            jax.ShapeDtypeStruct((rows, units), BF16),
            jax.ShapeDtypeStruct((rows, 2 * units), BF16),
        ],
        compiler_params=pltpu.CompilerParams(vmem_limit_bytes=VMEM_BYTES),
        cost_estimate=pl.CostEstimate(
            flops=6 * rows * width * units,
            bytes_accessed=6 * width * units + 4 * rows * width,
            transcendentals=rows * units,
        ),
        name="feed",
    )(inputs, grads, gate_up, down)


def assemble_kernel(starts, *refs):
    out_ref = refs[-1]
    tile = lax.rem(pl.program_id(0), starts[-1])
    for index, ref in enumerate(refs[:-1]):

        @pl.when((tile >= starts[index]) & (tile < starts[index + 1]))
        def _():
            out_ref[...] = ref[...].astype(F32)


def assemble(chunks):
    rows = chunks[0].shape[0]
    starts = [0]
    for chunk in chunks:
        starts.append(starts[-1] + chunk.shape[1] // (2 * TILE))
    tiles = starts[-1]

    def place(index):
        last = starts[index + 1] - starts[index] - 1

        def block(j):
            return (0, jnp.clip(j % tiles - starts[index], 0, last) * 2 + j // tiles)

        return block

    return pl.pallas_call(
        functools.partial(assemble_kernel, starts),
        grid=(2 * tiles,),
        in_specs=[pl.BlockSpec((rows, TILE), place(index)) for index in range(len(chunks))],
        out_specs=pl.BlockSpec((rows, TILE), lambda j: (0, j)),
        out_shape=jax.ShapeDtypeStruct((rows, 2 * tiles * TILE), F32),
        cost_estimate=pl.CostEstimate(
            flops=0, bytes_accessed=12 * rows * tiles * TILE, transcendentals=0
        ),
        name="assemble",
    )(*chunks)


def transpose_kernel(each, first_ref, second_ref, out_ref):
    head = lax.rem(pl.program_id(0), 2 * each)

    @pl.when(head < each)
    def _():
        out_ref[...] = first_ref[...].astype(F32).T

    @pl.when(head >= each)
    def _():
        out_ref[...] = second_ref[...].astype(F32).T


def transpose(first, second):
    rows, columns = first.shape
    each = columns // (2 * HEAD_DIM)
    spec = pl.BlockSpec((rows, HEAD_DIM), lambda j: (0, j % each * 2 + j // (2 * each)))
    return pl.pallas_call(
        functools.partial(transpose_kernel, each),
        grid=(4 * each,),
        in_specs=[spec, spec],
        out_specs=pl.BlockSpec((HEAD_DIM, rows), lambda j: (j, 0)),
        out_shape=jax.ShapeDtypeStruct((2 * columns, rows), F32),
        cost_estimate=pl.CostEstimate(
            flops=0, bytes_accessed=12 * rows * columns, transcendentals=0
        ),
        name="transpose",
    )(first, second)


MESH = pl.DeviceIdType.MESH


def greet(devices, extra=0):
    barrier = pltpu.get_barrier_semaphore()
    for device in devices:
        pl.semaphore_signal(barrier, inc=1, device_id=device, device_id_type=MESH)
    return barrier


class WeightGather:
    def __init__(self, bits, shard_ref, full_ref, sent, got):
        self.me, self.place = lax.axis_index("grp"), lax.axis_index("ep")
        self.bits, self.rows = bits, shard_ref.shape[0] // 2
        self.shard_ref, self.full_ref, self.sent, self.got = shard_ref, full_ref, sent, got
        self.orders = list(range(1, bits)) + [0], list(range(1, bits))[::-1] + [0]
        self.moves = []
        for index in range(1, 1 << (bits - 1)):
            for part in range(2):
                order = self.orders[part]
                far = sum(1 << bit for at, bit in enumerate(order[:-1]) if index >> at & 1)
                self.moves.append((part, far, order[index.bit_length() :]))

    def neighbours(self):
        return [(self.me ^ (1 << bit), self.place) for bit in range(self.bits)]

    def piece(self, part, far, bit):
        here = pl.ds(part * self.rows, self.rows)
        block = self.full_ref.at[self.me ^ far, here]
        return pltpu.make_async_remote_copy(
            src_ref=self.shard_ref.at[here] if far == 0 else block,
            dst_ref=block,
            send_sem=self.sent.at[part, far, bit],
            recv_sem=self.got.at[part, far ^ (1 << bit)],
            device_id=(self.me ^ (1 << bit), self.place),
            device_id_type=MESH,
        )

    def wait_piece(self, part, far):
        block = self.full_ref.at[self.me ^ far, pl.ds(part * self.rows, self.rows)]
        pltpu.make_async_remote_copy(
            src_ref=block,
            dst_ref=block,
            send_sem=self.sent.at[part, far, 0],
            recv_sem=self.got.at[part, far],
            device_id=(self.me ^ 1, self.place),
            device_id_type=MESH,
        ).wait_recv()

    def first(self):
        for part in range(2):
            for bit in self.orders[part]:
                self.piece(part, 0, bit).start()

    def forward(self, part, far, later):
        self.wait_piece(part, far)
        for bit in later:
            self.piece(part, far, bit).start()

    def finish(self):
        for part in range(2):
            for far in range(1 << (self.bits - 1)):
                self.wait_piece(part, 2 * far + 1)
        for part in range(2):
            for bit in self.orders[part]:
                self.piece(part, 0, bit).wait_send()
        for part, far, later in self.moves:
            for bit in later:
                self.piece(part, far, bit).wait_send()


def weight_gather_semaphores(groups):
    bits = groups.bit_length() - 1
    return [pltpu.SemaphoreType.DMA((2, groups, bits)), pltpu.SemaphoreType.DMA((2, groups))]


def opening_kernel(bits, count, chunks, *refs):
    (tokens_ref, shard_ref, gate_up_ref, down_ref, all_ref, full_ref), refs = refs[:6], refs[6:]
    low_refs, refs = refs[:chunks], refs[chunks:]
    down_low_ref, local, up_send, up_got, down_send, down_got, sent, got = refs
    me = lax.axis_index("grp")
    place = lax.axis_index("ep")
    weights = WeightGather(bits, shard_ref, full_ref, sent, got)

    barrier = greet(weights.neighbours())

    @pl.when(place > 0)
    def _():
        pl.semaphore_signal(barrier, inc=1, device_id=(me, place - 1), device_id_type=MESH)

    @pl.when(place < count - 1)
    def _():
        pl.semaphore_signal(barrier, inc=1, device_id=(me, place + 1), device_id_type=MESH)

    ends = jnp.where(place > 0, 1, 0) + jnp.where(place < count - 1, 1, 0)
    pl.semaphore_wait(barrier, bits + ends)

    def upward(hop):
        block = all_ref.at[jnp.maximum(place - hop, 0)]
        return pltpu.make_async_remote_copy(
            src_ref=tokens_ref if hop == 0 else block,
            dst_ref=block,
            send_sem=up_send.at[hop],
            recv_sem=up_got.at[hop],
            device_id=(me, jnp.minimum(place + 1, count - 1)),
            device_id_type=MESH,
        )

    def downward(hop):
        block = all_ref.at[jnp.minimum(place + hop, count - 1)]
        return pltpu.make_async_remote_copy(
            src_ref=tokens_ref if hop == 0 else block,
            dst_ref=block,
            send_sem=down_send.at[hop],
            recv_sem=down_got.at[hop],
            device_id=(me, jnp.maximum(place - 1, 0)),
            device_id_type=MESH,
        )

    def lines(hop, act):
        @pl.when((place + 1 < count) & (place - hop >= 0))
        def _():
            act(upward(hop))

        @pl.when((place - 1 >= 0) & (place + hop < count))
        def _():
            act(downward(hop))

    def line_got(hop):
        @pl.when(place - hop - 1 >= 0)
        def _():
            upward(hop).wait_recv()

        @pl.when(place + hop + 1 < count)
        def _():
            downward(hop).wait_recv()

    lines(0, lambda copy: copy.start())
    weights.first()
    own = [
        pltpu.make_async_copy(tokens_ref, all_ref.at[place], local.at[0]),
        pltpu.make_async_copy(shard_ref, full_ref.at[me], local.at[1]),
    ]
    for copy in own:
        copy.start()

    def round_block(in_ref, out_ref):
        out_ref[...] = in_ref[...].astype(BF16)

    shard_rows, columns = gate_up_ref.shape
    tiles = columns // (2 * TILE)
    start = 0
    for low_ref in low_refs:
        blocks = low_ref.shape[1] // TILE
        pltpu.emit_pipeline(
            round_block,
            grid=(blocks,),
            in_specs=[
                pl.BlockSpec(
                    (shard_rows, TILE), lambda j, start=start: (0, start + j // 2 + j % 2 * tiles)
                )
            ],
            out_specs=[pl.BlockSpec((shard_rows, TILE), lambda j: (0, j))],
        )(gate_up_ref, low_ref)
        start += blocks // 2
    down_rows, width = down_ref.shape
    step = 176
    pltpu.emit_pipeline(
        round_block,
        grid=(down_rows // step,),
        in_specs=[pl.BlockSpec((step, width), lambda j: (j, 0))],
        out_specs=[pl.BlockSpec((step, width), lambda j: (j, 0))],
    )(down_ref, down_low_ref)

    coming = list(weights.moves)
    hops = list(range(count - 1))
    while hops or coming:
        if hops:
            hop = hops.pop(0)
            line_got(hop)
            if hop + 1 < count - 1:
                lines(hop + 1, lambda copy: copy.start())
        for move in coming[:4]:
            weights.forward(*move)
        coming = coming[4:]
    weights.finish()
    for hop in range(count - 1):
        lines(hop, lambda copy: copy.wait_send())
    for copy in own:
        copy.wait()


def opening(tokens, shard, gate_up, down, cuts):
    groups, count = lax.axis_size("grp"), lax.axis_size("ep")
    bits = groups.bit_length() - 1
    whole, full, *lows = pl.pallas_call(
        functools.partial(opening_kernel, bits, count, len(cuts)),
        in_specs=[pl.BlockSpec(memory_space=pl.ANY)] * 4,
        out_specs=[pl.BlockSpec(memory_space=pl.ANY)] * (3 + len(cuts)),
        out_shape=[
            jax.ShapeDtypeStruct((count, *tokens.shape), BF16),
            jax.ShapeDtypeStruct((groups, *shard.shape), BF16),
            *[jax.ShapeDtypeStruct((gate_up.shape[0], 2 * size), BF16) for _, size in cuts],
            jax.ShapeDtypeStruct(down.shape, BF16),
        ],
        scratch_shapes=[
            pltpu.SemaphoreType.DMA((2,)),
            *[pltpu.SemaphoreType.DMA((count - 1,))] * 4,
            *weight_gather_semaphores(groups),
        ],
        compiler_params=pltpu.CompilerParams(
            collective_id=0, has_side_effects=True, vmem_limit_bytes=VMEM_BYTES
        ),
        name="opening",
    )(tokens, shard, gate_up, down)
    return whole, full.reshape(-1, full.shape[2]), lows[:-1], lows[-1]


def exchange_kernel(
    bits, count, values_ref, shard_ref, back_ref, full_ref, local, out_sent, out_got, sent, got
):
    me = lax.axis_index("grp")
    place = lax.axis_index("ep")
    weights = WeightGather(bits, shard_ref, full_ref, sent, got)
    others = [lax.rem(place + shift, count) for shift in range(1, count)]
    barrier = greet(weights.neighbours() + [(me, other) for other in others])
    pl.semaphore_wait(barrier, bits + count - 1)
    copies = [
        pltpu.make_async_remote_copy(
            src_ref=values_ref.at[other],
            dst_ref=back_ref.at[place],
            send_sem=out_sent.at[index],
            recv_sem=out_got.at[index],
            device_id=(me, other),
            device_id_type=MESH,
        )
        for index, other in enumerate(others)
    ]
    own = [
        pltpu.make_async_copy(values_ref.at[place], back_ref.at[place], local.at[0]),
        pltpu.make_async_copy(shard_ref, full_ref.at[me], local.at[1]),
    ]
    for copy in copies:
        copy.start()
    weights.first()
    for copy in own:
        copy.start()
    for move in weights.moves:
        weights.forward(*move)
    weights.finish()
    for copy in copies:
        copy.wait()
    for copy in own:
        copy.wait()


def exchange_and_gather(values, shard, collective_id):
    groups, count = lax.axis_size("grp"), lax.axis_size("ep")
    bits = groups.bit_length() - 1
    rows, width = values.shape
    shape = (count, rows // count, width)
    back, full = pl.pallas_call(
        functools.partial(exchange_kernel, bits, count),
        in_specs=[pl.BlockSpec(memory_space=pl.ANY)] * 2,
        out_specs=[pl.BlockSpec(memory_space=pl.ANY)] * 2,
        out_shape=[
            jax.ShapeDtypeStruct(shape, BF16),
            jax.ShapeDtypeStruct((groups, *shard.shape), BF16),
        ],
        scratch_shapes=[
            pltpu.SemaphoreType.DMA((2,)),
            *[pltpu.SemaphoreType.DMA((count - 1,))] * 2,
            *weight_gather_semaphores(groups),
        ],
        compiler_params=pltpu.CompilerParams(collective_id=collective_id, has_side_effects=True),
        name="exchange_and_gather",
    )(values.reshape(shape), shard)
    return back.reshape(rows, width), full.reshape(-1, full.shape[2])


def after(values, *tokens):
    return lax.optimization_barrier((values, *tokens))[0]


def flip(values, bit):
    size = lax.axis_size("grp")
    return lax.ppermute(values, "grp", [(i, i ^ (1 << bit)) for i in range(size)])


def gather_gains(gains):
    size = lax.axis_size("grp")
    me = lax.axis_index("grp")
    for bit in range(size.bit_length() - 1):
        other = flip(gains, bit)
        upper = (me >> bit) & 1
        gains = jnp.where(
            upper == 0,
            jnp.concatenate([gains, other], axis=1),
            jnp.concatenate([other, gains], axis=1),
        )
    return gains


class Scatter:
    def __init__(self, terms, order):
        self.terms = terms
        self.order = list(order)

    def step(self, *tokens):
        if not self.order:
            return
        bit = self.order.pop(0)
        axis = sum(other > bit for other in self.order)
        mine = (lax.axis_index("grp") >> bit) & 1
        terms = self.terms
        if tokens:
            terms = [after(term, *tokens) for term in terms]

        def part(term, which):
            return lax.dynamic_index_in_dim(term, which, axis, keepdims=False)

        self.sent = sum(part(term, 1 - mine).astype(F32) for term in terms).astype(BF16)
        self.terms = [part(term, mine) for term in terms] + [flip(self.sent, bit)]

    def finish(self):
        while self.order:
            self.step()
        return sum(term.astype(F32) for term in self.terms)


def core_split(values, groups):
    rows, columns = values.shape
    n = columns // groups
    mine = lax.axis_index("grp") & 1
    even = jnp.concatenate([values[:, i * n : (i + 1) * n] for i in range(0, groups, 2)], axis=1)
    odd = jnp.concatenate([values[:, i * n : (i + 1) * n] for i in range(1, groups, 2)], axis=1)
    return jnp.where(mine == 0, even, odd), jnp.where(mine == 0, odd, even)


def scatter_product(split, rights, groups, first=0):
    bits = groups.bit_length() - 1
    results = []
    for place, right in enumerate(rights):
        order = list(range(1, bits))
        if (place + first) % 2:
            order = order[::-1]
        sent = dot(split[1], right, CONTRACT_ROWS).astype(BF16)
        got = flip(sent, 0)
        kept = dot(split[0], right, CONTRACT_ROWS).astype(BF16)
        shape = (2,) * (bits - 1) + (-1, right.shape[1])
        results.append(Scatter([kept.reshape(shape), got.reshape(shape)], order))
        results[-1].sent = sent
    return results


def steps(scatters, *tokens):
    for scatter in scatters:
        scatter.step(*tokens)


def finish(scatters):
    return jnp.concatenate([scatter.finish() for scatter in scatters], axis=1)


def halves(values):
    middle = values.shape[1] // 2
    return values[:, :middle], values[:, middle:]


def exchange(values, experts):
    rows, width = values.shape
    return lax.all_to_all(
        values.reshape(experts, rows // experts, width),
        "ep",
        split_axis=0,
        concat_axis=0,
        tiled=True,
    ).reshape(rows, width)


def local(
    layer_input,
    kv_weight,
    norm_gains,
    query_maps,
    output_maps,
    gate_up_maps,
    down_maps,
    att_routes,
    att_gates,
    mlp_routes,
    mlp_gates,
    segments,
    cotangent,
):
    experts = lax.axis_size("ep")
    groups = lax.axis_size("grp")
    bits = groups.bit_length() - 1
    me_index = lax.axis_index("ep")
    tok_dev = layer_input.shape[0]
    model_width = layer_input.shape[1]
    capacity = 3 * tok_dev // experts
    rows_total = experts * capacity
    hidden = gate_up_maps.shape[2] // 2

    def gather(shard):
        return lax.all_gather(shard, "grp", axis=0, tiled=True)

    gains_full = gather_gains(norm_gains.astype(BF16))
    gain_one = gains_full[0].astype(F32)
    gain_two = gains_full[1].astype(F32)
    xfloat = layer_input.astype(F32)
    inverse_one, unit_one = normalize(xfloat)
    normed_one = (unit_one * gain_one).astype(BF16)

    kv_heads = kv_weight.reshape(2, HEADS, HEAD_DIM, -1).transpose(1, 0, 2, 3)
    kv_shard = kv_heads.reshape(kv_weight.shape).T.astype(BF16)
    cuts = []
    for count in (4, 2, 2, hidden // TILE - 8):
        cuts.append((sum(size for _, size in cuts), count * TILE))

    def gather(shard):
        return lax.all_gather(shard, "grp", axis=0, tiled=True)

    output_shard = output_maps[0].astype(BF16)
    kv_full = gather(kv_shard)
    output_full = gather(output_shard)
    normed_all, query_full, gate_up_low, down_low = opening(
        after(normed_one, output_shard),
        query_maps[0].astype(BF16),
        gate_up_maps[0],
        down_maps[0],
        cuts,
    )
    down_full = gather(down_low)
    gate_up_full = [gather(gate_up_low[0]), None, None, gather(gate_up_low[3])]

    att_named, att_place = expert_places(att_routes[0].reshape(experts, tok_dev, TOP), experts)
    mlp_named, mlp_place = expert_places(mlp_routes[0].reshape(experts, tok_dev, TOP), experts)

    def mine(values, axis):
        return lax.dynamic_index_in_dim(values, me_index, axis, keepdims=False)

    att_pick = one_hot(mine(att_named, 1), mine(att_place, 1), capacity)
    att_send = one_hot(mine(att_named, 0), mine(att_place, 0), capacity).reshape(
        rows_total, tok_dev
    )
    mlp_send = one_hot(mine(mlp_named, 0), mine(mlp_place, 0), capacity).reshape(
        rows_total, tok_dev
    )

    def gates_at(send, routes, gates):
        ids = jnp.arange(experts, dtype=jnp.int32)
        routes = mine(routes.reshape(experts, tok_dev, TOP), 0)
        per_expert = jnp.sum(jnp.where(routes[None] == ids[:, None, None], gates[None], 0.0), axis=2)
        spread = jnp.where(
            send.reshape(experts, capacity, tok_dev), per_expert[:, None, :], 0.0
        ).reshape(rows_total, tok_dev)
        return high_low(spread)

    att_high, att_low = gates_at(att_send, att_routes, att_gates)
    mlp_high, mlp_low = gates_at(mlp_send, mlp_routes, mlp_gates)
    mlp_send = mlp_send.astype(BF16)
    places = jnp.arange(experts * tok_dev, dtype=jnp.int32).reshape(experts, 1, tok_dev)
    starts = segments[0].reshape(experts, 1, tok_dev)
    bounds = jnp.stack(
        [
            jnp.sum(jnp.where(att_pick, starts, 0), axis=2).reshape(-1),
            jnp.sum(jnp.where(att_pick, places, 0), axis=2).reshape(-1),
        ],
        axis=1,
    )
    att_pick = att_pick.astype(BF16)

    cotangent_send = (dot(mlp_high, cotangent) + dot(mlp_low, cotangent)).astype(BF16)
    cotangent_send = after(cotangent_send, normed_all)
    grad_mlp_rows = exchange(cotangent_send, experts)
    att_in = (
        jnp.einsum(
            "sct,std->scd", att_pick, after(normed_all, cotangent_send), preferred_element_type=F32
        )
        .astype(BF16)
        .reshape(rows_total, model_width)
    )
    normed_all = normed_all.reshape(experts * tok_dev, model_width)
    queries = dot(att_in, query_full).astype(BF16)
    keys_values = dot(after(normed_all, queries), kv_full).astype(BF16)
    att_heads, logsums = attend_forward(queries, keys_values, bounds, experts)
    att_rows = dot(after(att_heads, grad_mlp_rows), output_full).astype(BF16)
    att_back, gate_up_full[1] = exchange_and_gather(att_rows, gate_up_low[1], 1)
    residual_one = (
        xfloat + dot(att_high, att_back, CONTRACT_ROWS) + dot(att_low, att_back, CONTRACT_ROWS)
    )

    inverse_two, unit_two = normalize(residual_one)
    normed_two = (unit_two * gain_two).astype(BF16)
    mlp_given = dot(mlp_send, normed_two).astype(BF16)
    mlp_in, gate_up_full[2] = exchange_and_gather(mlp_given, gate_up_low[2], 2)
    mlp_split = core_split(mlp_in, groups)
    acts = [None] * len(cuts)
    grads = [None] * len(cuts)

    def feed_chunk(index, feed_in, total):
        gate_up = gate_up_full[index]
        acts[index], grads[index] = feed(
            feed_in, grad_mlp_rows, gate_up, down_full, cuts[index][0]
        )
        return total + dot(grads[index], gate_up, CONTRACT_COLUMNS)

    grad_mlp_in = feed_chunk(1, mlp_in, 0.0)
    grad_mlp_in = feed_chunk(2, after(mlp_in, grad_mlp_in), grad_mlp_in)
    middle_scatter = scatter_product(mlp_split, [after(grads[1], grad_mlp_in), grads[2]], groups)
    ready = [scatter.terms[0] for scatter in middle_scatter]
    grad_mlp_in = feed_chunk(0, after(mlp_in, *ready), grad_mlp_in)
    steps(middle_scatter, grad_mlp_in)
    first_grad = dot(
        mlp_in,
        after(grads[0], grad_mlp_in, *[scatter.sent for scatter in middle_scatter]),
        CONTRACT_ROWS,
    ).astype(BF16)
    first_grad_sum = lax.psum_scatter(first_grad, "grp", scatter_dimension=0, tiled=True)
    grad_mlp_in = feed_chunk(3, after(mlp_in, first_grad), grad_mlp_in).astype(BF16)

    activated = after(jnp.concatenate(acts, axis=1), grad_mlp_in)
    mlp_rows = dot(activated, down_full).astype(BF16)
    last_grad = dot(mlp_in, after(grads[3], mlp_rows), CONTRACT_ROWS).astype(BF16)
    last_grad_sum = lax.psum_scatter(last_grad, "grp", scatter_dimension=0, tiled=True)
    steps(middle_scatter, last_grad)
    mlp_returned = after(
        exchange(grad_mlp_in, experts),
        mlp_rows,
        last_grad,
        *[scatter.sent for scatter in middle_scatter],
    )

    grad_final = cotangent.astype(F32)
    grad_normed_two = dot(mlp_send, mlp_returned, CONTRACT_ROWS)
    grad_inner_two, grad_gain_two = norm_backward(grad_normed_two, unit_two, inverse_two, gain_two)
    grad_residual = grad_final + grad_inner_two

    res_high, res_low = high_low(grad_residual)
    sent_four = (
        dot(att_high, res_high) + dot(att_low, res_high) + dot(att_high, res_low)
    ).astype(BF16)
    down_grad = dot(after(activated, sent_four), grad_mlp_rows, CONTRACT_ROWS).astype(BF16)
    down_grad_sum = lax.psum_scatter(down_grad, "grp", scatter_dimension=0, tiled=True)
    grad_att_rows = after(exchange(sent_four, experts), down_grad)
    mlp_back = exchange(after(mlp_rows, grad_att_rows), experts)
    grad_heads = dot(grad_att_rows, output_full, CONTRACT_COLUMNS).astype(BF16)
    normed_split = core_split(normed_all, groups)
    att_split = core_split(att_in, groups)
    normed_split = core_split(normed_all, groups)
    att_split = core_split(att_in, groups)
    half = HEADS // 2
    grad_one, both_one = attend_backward(
        queries, keys_values, grad_heads, bounds, logsums, experts, 0, half
    )
    both_one = after(both_one, first_grad_sum)
    grad_two, both_two = attend_backward(
        after(queries, both_one),
        keys_values,
        grad_heads,
        bounds,
        logsums,
        experts,
        half,
        HEADS - half,
    )
    both_two = after(both_two, mlp_back, last_grad_sum)
    query_one, query_two = halves(query_full)
    kv_full_one, kv_full_two = halves(kv_full)
    grad_att_in = (
        dot(after(grad_one, both_two), query_one, CONTRACT_COLUMNS)
        + dot(grad_two, query_two, CONTRACT_COLUMNS)
    ).astype(BF16)
    grad_all = (
        jnp.einsum(
            "sct,scd->std",
            att_pick,
            grad_att_in.reshape(experts, capacity, model_width),
            preferred_element_type=F32,
        ).reshape(experts * tok_dev, model_width)
        + dot(both_one, kv_full_one, CONTRACT_COLUMNS)
        + dot(both_two, kv_full_two, CONTRACT_COLUMNS)
    ).astype(BF16)
    grad_back = exchange(grad_all, experts)
    kv_one = scatter_product(normed_split, halves(after(both_one, grad_all)), groups)
    ready = [scatter.terms[0] for scatter in kv_one]
    steps(kv_one, *ready)
    ready = [scatter.sent for scatter in kv_one]
    kv_two = scatter_product(normed_split, halves(after(both_two, *ready)), groups)
    ready = [scatter.terms[0] for scatter in kv_two]
    steps(kv_one, *ready)
    steps(kv_two, *[scatter.sent for scatter in kv_one])
    ready = [scatter.sent for scatter in kv_two]
    query_scatter = scatter_product(att_split, [after(grad_one, *ready)], groups)
    query_scatter += scatter_product(att_split, [after(grad_two, *ready)], groups, 1)
    ready = [scatter.terms[0] for scatter in query_scatter]
    part_one = after(finish(kv_one), *ready, down_grad_sum).astype(BF16)
    kv_grad_one = lax.psum(part_one, "ep")
    steps(kv_two, part_one)
    ready = [scatter.sent for scatter in kv_two]
    steps(query_scatter, *ready)
    ready = [scatter.sent for scatter in query_scatter]
    output_scatter = scatter_product(
        core_split(att_heads, groups), halves(after(grad_att_rows, *ready)), groups
    )
    ready = [scatter.terms[0] for scatter in output_scatter]
    part_two = after(finish(kv_two), *ready, grad_back).astype(BF16)
    kv_grad_two = lax.psum(after(part_two, kv_grad_one), "ep")
    steps(output_scatter, part_two)
    ready = [scatter.sent for scatter in output_scatter]
    mlp_back = after(mlp_back, *ready)
    output = (
        residual_one + dot(mlp_high, mlp_back, CONTRACT_ROWS) + dot(mlp_low, mlp_back, CONTRACT_ROWS)
    ).astype(BF16)
    steps(query_scatter, output)
    weight_grads = [
        after(part, output)
        for part in (first_grad_sum, *[scatter.finish() for scatter in middle_scatter], last_grad_sum)
    ]
    down_grad = after(down_grad_sum, output).astype(F32)[None]
    ready = [scatter.sent for scatter in query_scatter]
    steps(output_scatter, *ready)
    ready = [scatter.sent for scatter in output_scatter]
    grad_normed_one = jnp.sum(
        after(grad_back, *ready).reshape(experts, tok_dev, model_width).astype(F32), axis=0
    )
    query_grad = finish(query_scatter)[None]
    output_grad = finish(output_scatter)[None]
    kv_grad = transpose(kv_grad_one, kv_grad_two)
    gate_up_grad = assemble(weight_grads)[None]
    grad_inner_one, grad_gain_one = norm_backward(grad_normed_one, unit_one, inverse_one, gain_one)
    grad_input = grad_residual + grad_inner_one

    gains_grad = jnp.stack([grad_gain_one, grad_gain_two])
    gains_grad = gains_grad.reshape((2,) + (2,) * bits + (-1,))
    for bit in reversed(range(bits)):
        mine_bit = (lax.axis_index("grp") >> bit) & 1
        kept = lax.dynamic_index_in_dim(gains_grad, mine_bit, 1, keepdims=False)
        sent = lax.dynamic_index_in_dim(gains_grad, 1 - mine_bit, 1, keepdims=False)
        gains_grad = kept + lax.ppermute(
            sent, "grp", [(i, i ^ (1 << bit)) for i in range(groups)]
        )
    for bit in range(experts.bit_length() - 1):
        gains_grad = gains_grad + lax.ppermute(
            gains_grad, "ep", [(i, i ^ (1 << bit)) for i in range(experts)]
        )
    return (
        output,
        grad_input,
        kv_grad,
        gains_grad,
        query_grad,
        output_grad,
        gate_up_grad,
        down_grad,
    )


def solution(mesh):
    placed = (
        P(("grp", "ep"), None),
        P(None, "grp"),
        P(None, "grp"),
        P("ep", "grp", None),
        P("ep", "grp", None),
        P("ep", "grp", None),
        P("ep", "grp", None),
        P("grp", None, None),
        P(("grp", "ep"), None),
        P("grp", None, None),
        P(("grp", "ep"), None),
        P("grp", None),
        P(("grp", "ep"), None),
    )
    return jax.shard_map(
        local,
        mesh=mesh,
        in_specs=placed,
        out_specs=(
            P(("grp", "ep"), None),
            P(("grp", "ep"), None),
            P(None, "grp"),
            P(None, "grp"),
            P("ep", "grp", None),
            P("ep", "grp", None),
            P("ep", "grp", None),
            P("ep", "grp", None),
        ),
        check_vma=False,
    )
```

```python
import functools

import jax
import jax.numpy as jnp
from jax import lax
from jax.experimental import pallas as pl
from jax.experimental.pallas import tpu as pltpu
from jax.sharding import PartitionSpec as P

HEADS = 16
HEAD_DIM = 128
TOP = 2


EPSILON = 1e-06
NEGATIVE = -1e30
LOG2_E = 1.4426950408889634
CONTRACT_ROWS = (((0,), (0,)), ((), ()))
CONTRACT_COLUMNS = (((1,), (1,)), ((), ()))
BF16 = jnp.bfloat16
F32 = jnp.float32
VMEM_BYTES = 56 * 2**20
TILE = 512


def normalize(values):
    inverse = lax.rsqrt(jnp.mean(values * values, axis=-1, keepdims=True) + EPSILON)
    return (inverse, values * inverse)


def norm_backward(grad_normed, unit, inverse, gain):
    grad_unit = grad_normed * gain
    inner = jnp.mean(grad_unit * unit, axis=-1, keepdims=True)
    return (inverse * (grad_unit - unit * inner), jnp.sum(grad_normed * unit, axis=0))


def dot(left, right, dims=(((1,), (0,)), ((), ()))):
    return lax.dot_general(left, right, dims, preferred_element_type=F32)


def high_low(values):
    high = values.astype(BF16)
    return high, (values - high.astype(F32)).astype(BF16)


def expert_places(routes, experts):
    tokens = routes.shape[1]
    ids = jnp.arange(experts, dtype=jnp.int32)
    named = jnp.any(routes[:, None, :, :] == ids[None, :, None, None], axis=3)
    before = (jnp.arange(tokens)[:, None] < jnp.arange(tokens)[None, :]).astype(BF16)
    place = lax.dot_general(
        named.astype(BF16), before, (((2,), (0,)), ((), ())), preferred_element_type=F32
    )
    return named, place.astype(jnp.int32)


def one_hot(named, place, capacity):
    rows = jnp.arange(capacity, dtype=jnp.int32)[:, None]
    return named[..., None, :] & (place[..., None, :] == rows)


def attend_forward_kernel(sources, query_ref, key_ref, value_ref, bounds_ref, out_ref, logsum_ref):
    head = pl.program_id(0)
    capacity = query_ref.shape[0] // sources
    tokens = key_ref.shape[0] // sources
    scaling = HEAD_DIM ** (-0.5) * LOG2_E

    @pl.when(head == 0)
    def _():
        logsum_ref[...] = jnp.zeros_like(logsum_ref)

    for source in range(sources):
        rows = slice(source * capacity, (source + 1) * capacity)
        span = (source + 1) * tokens
        first = bounds_ref[rows, 0:1]
        last = bounds_ref[rows, 1:2]
        scores = dot(query_ref[rows, :], key_ref[:span, :], CONTRACT_COLUMNS) * scaling
        places = lax.broadcasted_iota(jnp.int32, scores.shape, 1)
        scores = jnp.where((places >= first) & (places <= last), scores, NEGATIVE)
        peak = jnp.max(scores, axis=1, keepdims=True)
        exponent = jnp.exp2(scores - peak)
        total = jnp.sum(exponent, axis=1, keepdims=True)
        mixed = dot(exponent.astype(BF16), value_ref[:span, :])
        out_ref[rows, :] = (mixed * (1.0 / total)).astype(BF16)
        lanes = lax.broadcasted_iota(jnp.int32, (capacity, 128), 1)
        logsum_ref[rows, :] = jnp.where(lanes == head, peak + jnp.log2(total), logsum_ref[rows, :])


def attend_forward(queries, keys_values, bounds, sources):
    rows, features = queries.shape
    seq = keys_values.shape[0]
    pairs = (sources + 1) / (2 * sources)
    return pl.pallas_call(
        functools.partial(attend_forward_kernel, sources),
        grid=(HEADS,),
        in_specs=[
            pl.BlockSpec((rows, HEAD_DIM), lambda h: (0, h)),
            pl.BlockSpec((seq, HEAD_DIM), lambda h: (0, 2 * h)),
            pl.BlockSpec((seq, HEAD_DIM), lambda h: (0, 2 * h + 1)),
            pl.BlockSpec((rows, 2), lambda h: (0, 0)),
        ],
        out_specs=[
            pl.BlockSpec((rows, HEAD_DIM), lambda h: (0, h)),
            pl.BlockSpec((rows, 128), lambda h: (0, 0)),
        ],
        out_shape=[
            jax.ShapeDtypeStruct((rows, features), BF16),
            jax.ShapeDtypeStruct((rows, 128), F32),
        ],
        compiler_params=pltpu.CompilerParams(vmem_limit_bytes=VMEM_BYTES),
        cost_estimate=pl.CostEstimate(
            flops=int(4 * rows * seq * features * pairs),
            bytes_accessed=4 * (rows + seq) * features,
            transcendentals=int(HEADS * rows * seq * pairs),
        ),
        name="attend_forward",
    )(queries, keys_values, keys_values, bounds)


def attend_backward_kernel(
    sources,
    query_ref,
    key_ref,
    value_ref,
    grad_ref,
    bounds_ref,
    logsum_ref,
    grad_query_ref,
    grad_both_ref,
    key_total,
    value_total,
):
    head = pl.program_id(0)
    capacity = query_ref.shape[0] // sources
    tokens = key_ref.shape[0] // sources
    scaling = HEAD_DIM ** (-0.5)
    for source in reversed(range(sources)):
        rows = slice(source * capacity, (source + 1) * capacity)
        span = (source + 1) * tokens
        first = bounds_ref[rows, 0:1]
        last = bounds_ref[rows, 1:2]
        query = query_ref[rows, :]
        grad = grad_ref[rows, :]
        lanes = lax.broadcasted_iota(jnp.int32, (capacity, 128), 1)
        logsum = jnp.sum(
            jnp.where(lanes == head, logsum_ref[rows, :], 0.0), axis=1, keepdims=True
        )
        scores = dot(query, key_ref[:span, :], CONTRACT_COLUMNS) * (scaling * LOG2_E)
        places = lax.broadcasted_iota(jnp.int32, scores.shape, 1)
        scores = jnp.where((places >= first) & (places <= last), scores, NEGATIVE)
        probs = jnp.exp2(scores - logsum)
        grad_probs = dot(grad, value_ref[:span, :], CONTRACT_COLUMNS)
        weighted = probs * grad_probs
        correction = jnp.sum(weighted, axis=1, keepdims=True)
        grad_scores = (weighted - probs * correction).astype(BF16)
        grad_query_ref[rows, :] = (dot(grad_scores, key_ref[:span, :]) * scaling).astype(BF16)
        key_part = dot(grad_scores, query, CONTRACT_ROWS)
        value_part = dot(probs.astype(BF16), grad, CONTRACT_ROWS)
        if source == sources - 1:
            key_total[...] = key_part
            value_total[...] = value_part
        else:
            key_total[:span, :] += key_part
            value_total[:span, :] += value_part
    grad_both_ref[:, :HEAD_DIM] = (key_total[...] * scaling).astype(BF16)
    grad_both_ref[:, HEAD_DIM:] = value_total[...].astype(BF16)


def attend_backward(queries, keys_values, grads, bounds, logsums, sources):
    rows = queries.shape[0]
    features = HEADS * HEAD_DIM
    seq = keys_values.shape[0]
    pairs = (sources + 1) / (2 * sources)
    return pl.pallas_call(
        functools.partial(attend_backward_kernel, sources),
        grid=(HEADS,),
        in_specs=[
            pl.BlockSpec((rows, HEAD_DIM), lambda h: (0, h)),
            pl.BlockSpec((seq, HEAD_DIM), lambda h: (0, 2 * h)),
            pl.BlockSpec((seq, HEAD_DIM), lambda h: (0, 2 * h + 1)),
            pl.BlockSpec((rows, HEAD_DIM), lambda h: (0, h)),
            pl.BlockSpec((rows, 2), lambda h: (0, 0)),
            pl.BlockSpec((rows, 128), lambda h: (0, 0)),
        ],
        out_specs=[
            pl.BlockSpec((rows, HEAD_DIM), lambda h: (0, h)),
            pl.BlockSpec((seq, 2 * HEAD_DIM), lambda h: (0, h)),
        ],
        out_shape=[
            jax.ShapeDtypeStruct((rows, features), BF16),
            jax.ShapeDtypeStruct((seq, 2 * features), BF16),
        ],
        scratch_shapes=[pltpu.VMEM((seq, HEAD_DIM), F32), pltpu.VMEM((seq, HEAD_DIM), F32)],
        compiler_params=pltpu.CompilerParams(vmem_limit_bytes=VMEM_BYTES),
        cost_estimate=pl.CostEstimate(
            flops=int(10 * rows * seq * features * pairs),
            bytes_accessed=8 * (rows + seq) * features,
            transcendentals=int(HEADS * rows * seq * pairs),
        ),
        name="attend_backward",
    )(queries, keys_values, keys_values, grads, bounds, logsums)


def feed_kernel(in_ref, grad_ref, gate_up_ref, down_ref, act_ref, grad_gate_up_ref):
    units = down_ref.shape[0]
    step = units // 2
    for start in range(0, units, step):
        here = slice(start, start + step)
        there = slice(units + start, units + start + step)
        gate = dot(in_ref[...], gate_up_ref[:, here])
        up = dot(in_ref[...], gate_up_ref[:, there])
        grad_act = dot(grad_ref[...], down_ref[here, :], CONTRACT_COLUMNS)
        sigmoid = jax.nn.sigmoid(gate)
        silu = gate * sigmoid
        act_ref[:, here] = (silu * up).astype(BF16)
        grad_gate_up_ref[:, here] = (
            grad_act * up * sigmoid * (1.0 + gate * (1.0 - sigmoid))
        ).astype(BF16)
        grad_gate_up_ref[:, there] = (grad_act * silu).astype(BF16)


def feed(inputs, grads, gate_up, down, offset):
    rows, width = inputs.shape
    units = gate_up.shape[1] // 2
    tiles = units // TILE
    start = offset // TILE
    return pl.pallas_call(
        feed_kernel,
        grid=(tiles,),
        in_specs=[
            pl.BlockSpec((rows, width), lambda j: (0, 0)),
            pl.BlockSpec((rows, width), lambda j: (0, 0)),
            pl.BlockSpec((width, 2 * TILE), lambda j: (0, j)),
            pl.BlockSpec((TILE, width), lambda j: (j + start, 0)),
        ],
        out_specs=[
            pl.BlockSpec((rows, TILE), lambda j: (0, j)),
            pl.BlockSpec((rows, 2 * TILE), lambda j: (0, j)),
        ],
        out_shape=[
            jax.ShapeDtypeStruct((rows, units), BF16),
            jax.ShapeDtypeStruct((rows, 2 * units), BF16),
        ],
        compiler_params=pltpu.CompilerParams(vmem_limit_bytes=VMEM_BYTES),
        cost_estimate=pl.CostEstimate(
            flops=6 * rows * width * units,
            bytes_accessed=6 * width * units + 4 * rows * width,
            transcendentals=rows * units,
        ),
        name="feed",
    )(inputs, grads, gate_up, down)


def assemble_kernel(counts, *refs):
    *refs, out_ref = refs
    hidden = out_ref.shape[1] // 2
    start = 0
    for count in counts:
        terms, refs = refs[:count], refs[count:]
        for tile in range(terms[0].shape[1] // (2 * TILE)):
            for half in range(2):
                there = half * hidden + start
                here = (2 * tile + half) * TILE
                out_ref[:, there : there + TILE] = sum(
                    term[:, here : here + TILE].astype(F32) for term in terms
                )
            start += TILE


def assemble(chunks):
    arrays = [term for terms in chunks for term in terms]
    rows = arrays[0].shape[0]
    step = 32
    columns = sum(terms[0].shape[1] for terms in chunks)
    return pl.pallas_call(
        functools.partial(assemble_kernel, [len(terms) for terms in chunks]),
        grid=(rows // step,),
        in_specs=[pl.BlockSpec((step, term.shape[1]), lambda i: (i, 0)) for term in arrays],
        out_specs=pl.BlockSpec((step, columns), lambda i: (i, 0)),
        out_shape=jax.ShapeDtypeStruct((rows, columns), F32),
        compiler_params=pltpu.CompilerParams(vmem_limit_bytes=VMEM_BYTES),
        cost_estimate=pl.CostEstimate(
            flops=0, bytes_accessed=6 * rows * columns, transcendentals=0
        ),
        name="assemble",
    )(*arrays)


def transpose_kernel(steps, in_ref, out_ref):
    for value in range(2):

        @pl.when(pl.program_id(0) // steps == value)
        def _():
            for head in range(TILE // HEAD_DIM):
                columns = slice((2 * head + value) * HEAD_DIM, (2 * head + value + 1) * HEAD_DIM)
                rows = slice(head * HEAD_DIM, (head + 1) * HEAD_DIM)
                out_ref[rows, :] = in_ref[:, columns].astype(F32).T


def transpose(values):
    rows, columns = values.shape
    steps = columns // (2 * TILE)
    return pl.pallas_call(
        functools.partial(transpose_kernel, steps),
        grid=(2 * steps,),
        in_specs=[pl.BlockSpec((rows, 2 * TILE), lambda j: (0, j % steps))],
        out_specs=pl.BlockSpec((TILE, rows), lambda j: (j, 0)),
        out_shape=jax.ShapeDtypeStruct((columns, rows), F32),
        cost_estimate=pl.CostEstimate(
            flops=0, bytes_accessed=6 * rows * columns, transcendentals=0
        ),
        name="transpose",
    )(values)


MESH = pl.DeviceIdType.MESH


def greet(devices, extra=0):
    barrier = pltpu.get_barrier_semaphore()
    for device in devices:
        pl.semaphore_signal(barrier, inc=1, device_id=device, device_id_type=MESH)
    return barrier


class WeightGather:
    def __init__(self, bits, shard_ref, full_ref, sent, got):
        self.me, self.place = lax.axis_index("grp"), lax.axis_index("ep")
        self.bits, self.rows = bits, shard_ref.shape[0] // 2
        self.shard_ref, self.full_ref, self.sent, self.got = shard_ref, full_ref, sent, got
        self.orders = list(range(1, bits)) + [0], list(range(1, bits))[::-1] + [0]
        self.moves = []
        for index in range(1, 1 << (bits - 1)):
            for part in range(2):
                order = self.orders[part]
                far = sum(1 << bit for at, bit in enumerate(order[:-1]) if index >> at & 1)
                self.moves.append((part, far, order[index.bit_length() :]))

    def neighbours(self):
        return [(self.me ^ (1 << bit), self.place) for bit in range(self.bits)]

    def piece(self, part, far, bit):
        here = pl.ds(part * self.rows, self.rows)
        block = self.full_ref.at[self.me ^ far, here]
        return pltpu.make_async_remote_copy(
            src_ref=self.shard_ref.at[here] if far == 0 else block,
            dst_ref=block,
            send_sem=self.sent.at[part, far, bit],
            recv_sem=self.got.at[part, far ^ (1 << bit)],
            device_id=(self.me ^ (1 << bit), self.place),
            device_id_type=MESH,
        )

    def wait_piece(self, part, far):
        block = self.full_ref.at[self.me ^ far, pl.ds(part * self.rows, self.rows)]
        pltpu.make_async_remote_copy(
            src_ref=block,
            dst_ref=block,
            send_sem=self.sent.at[part, far, 0],
            recv_sem=self.got.at[part, far],
            device_id=(self.me ^ 1, self.place),
            device_id_type=MESH,
        ).wait_recv()

    def first(self):
        for part in range(2):
            for bit in self.orders[part]:
                self.piece(part, 0, bit).start()

    def forward(self, part, far, later):
        self.wait_piece(part, far)
        for bit in later:
            self.piece(part, far, bit).start()

    def finish(self):
        for part in range(2):
            for far in range(1 << (self.bits - 1)):
                self.wait_piece(part, 2 * far + 1)
        for part in range(2):
            for bit in self.orders[part]:
                self.piece(part, 0, bit).wait_send()
        for part, far, later in self.moves:
            for bit in later:
                self.piece(part, far, bit).wait_send()


def weight_gather_semaphores(groups):
    bits = groups.bit_length() - 1
    return [pltpu.SemaphoreType.DMA((2, groups, bits)), pltpu.SemaphoreType.DMA((2, groups))]


def opening_kernel(bits, count, chunks, *refs):
    (tokens_ref, shard_ref, gate_up_ref, down_ref, all_ref, full_ref), refs = refs[:6], refs[6:]
    low_refs, refs = refs[:chunks], refs[chunks:]
    down_low_ref, local, up_send, up_got, down_send, down_got, sent, got = refs
    me = lax.axis_index("grp")
    place = lax.axis_index("ep")
    weights = WeightGather(bits, shard_ref, full_ref, sent, got)

    barrier = greet(weights.neighbours())

    @pl.when(place > 0)
    def _():
        pl.semaphore_signal(barrier, inc=1, device_id=(me, place - 1), device_id_type=MESH)

    @pl.when(place < count - 1)
    def _():
        pl.semaphore_signal(barrier, inc=1, device_id=(me, place + 1), device_id_type=MESH)

    ends = jnp.where(place > 0, 1, 0) + jnp.where(place < count - 1, 1, 0)
    pl.semaphore_wait(barrier, bits + ends)

    def upward(hop):
        block = all_ref.at[jnp.maximum(place - hop, 0)]
        return pltpu.make_async_remote_copy(
            src_ref=tokens_ref if hop == 0 else block,
            dst_ref=block,
            send_sem=up_send.at[hop],
            recv_sem=up_got.at[hop],
            device_id=(me, jnp.minimum(place + 1, count - 1)),
            device_id_type=MESH,
        )

    def downward(hop):
        block = all_ref.at[jnp.minimum(place + hop, count - 1)]
        return pltpu.make_async_remote_copy(
            src_ref=tokens_ref if hop == 0 else block,
            dst_ref=block,
            send_sem=down_send.at[hop],
            recv_sem=down_got.at[hop],
            device_id=(me, jnp.maximum(place - 1, 0)),
            device_id_type=MESH,
        )

    def lines(hop, act):
        @pl.when((place + 1 < count) & (place - hop >= 0))
        def _():
            act(upward(hop))

        @pl.when((place - 1 >= 0) & (place + hop < count))
        def _():
            act(downward(hop))

    def line_got(hop):
        @pl.when(place - hop - 1 >= 0)
        def _():
            upward(hop).wait_recv()

        @pl.when(place + hop + 1 < count)
        def _():
            downward(hop).wait_recv()

    lines(0, lambda copy: copy.start())
    weights.first()
    own = [
        pltpu.make_async_copy(tokens_ref, all_ref.at[place], local.at[0]),
        pltpu.make_async_copy(shard_ref, full_ref.at[me], local.at[1]),
    ]
    for copy in own:
        copy.start()

    def round_block(in_ref, out_ref):
        out_ref[...] = in_ref[...].astype(BF16)

    shard_rows, columns = gate_up_ref.shape
    tiles = columns // (2 * TILE)
    start = 0
    for low_ref in low_refs:
        blocks = low_ref.shape[1] // TILE
        pltpu.emit_pipeline(
            round_block,
            grid=(blocks,),
            in_specs=[
                pl.BlockSpec(
                    (shard_rows, TILE), lambda j, start=start: (0, start + j // 2 + j % 2 * tiles)
                )
            ],
            out_specs=[pl.BlockSpec((shard_rows, TILE), lambda j: (0, j))],
        )(gate_up_ref, low_ref)
        start += blocks // 2
    down_rows, width = down_ref.shape
    step = 176
    pltpu.emit_pipeline(
        round_block,
        grid=(down_rows // step,),
        in_specs=[pl.BlockSpec((step, width), lambda j: (j, 0))],
        out_specs=[pl.BlockSpec((step, width), lambda j: (j, 0))],
    )(down_ref, down_low_ref)

    coming = list(weights.moves)
    hops = list(range(count - 1))
    while hops or coming:
        if hops:
            hop = hops.pop(0)
            line_got(hop)
            if hop + 1 < count - 1:
                lines(hop + 1, lambda copy: copy.start())
        for move in coming[:4]:
            weights.forward(*move)
        coming = coming[4:]
    weights.finish()
    for hop in range(count - 1):
        lines(hop, lambda copy: copy.wait_send())
    for copy in own:
        copy.wait()


def opening(tokens, shard, gate_up, down, cuts):
    groups, count = lax.axis_size("grp"), lax.axis_size("ep")
    bits = groups.bit_length() - 1
    whole, full, *lows = pl.pallas_call(
        functools.partial(opening_kernel, bits, count, len(cuts)),
        in_specs=[pl.BlockSpec(memory_space=pl.ANY)] * 4,
        out_specs=[pl.BlockSpec(memory_space=pl.ANY)] * (3 + len(cuts)),
        out_shape=[
            jax.ShapeDtypeStruct((count, *tokens.shape), BF16),
            jax.ShapeDtypeStruct((groups, *shard.shape), BF16),
            *[jax.ShapeDtypeStruct((gate_up.shape[0], 2 * size), BF16) for _, size in cuts],
            jax.ShapeDtypeStruct(down.shape, BF16),
        ],
        scratch_shapes=[
            pltpu.SemaphoreType.DMA((2,)),
            *[pltpu.SemaphoreType.DMA((count - 1,))] * 4,
            *weight_gather_semaphores(groups),
        ],
        compiler_params=pltpu.CompilerParams(
            collective_id=0, has_side_effects=True, vmem_limit_bytes=VMEM_BYTES
        ),
        name="opening",
    )(tokens, shard, gate_up, down)
    return whole, full.reshape(-1, full.shape[2]), lows[:-1], lows[-1]


def exchange_kernel(
    bits, count, values_ref, shard_ref, back_ref, full_ref, local, out_sent, out_got, sent, got
):
    me = lax.axis_index("grp")
    place = lax.axis_index("ep")
    weights = WeightGather(bits, shard_ref, full_ref, sent, got)
    others = [lax.rem(place + shift, count) for shift in range(1, count)]
    barrier = greet(weights.neighbours() + [(me, other) for other in others])
    pl.semaphore_wait(barrier, bits + count - 1)
    copies = [
        pltpu.make_async_remote_copy(
            src_ref=values_ref.at[other],
            dst_ref=back_ref.at[place],
            send_sem=out_sent.at[index],
            recv_sem=out_got.at[index],
            device_id=(me, other),
            device_id_type=MESH,
        )
        for index, other in enumerate(others)
    ]
    own = [
        pltpu.make_async_copy(values_ref.at[place], back_ref.at[place], local.at[0]),
        pltpu.make_async_copy(shard_ref, full_ref.at[me], local.at[1]),
    ]
    for copy in copies:
        copy.start()
    weights.first()
    for copy in own:
        copy.start()
    for move in weights.moves:
        weights.forward(*move)
    weights.finish()
    for copy in copies:
        copy.wait()
    for copy in own:
        copy.wait()


def exchange_and_gather(values, shard, collective_id):
    groups, count = lax.axis_size("grp"), lax.axis_size("ep")
    bits = groups.bit_length() - 1
    rows, width = values.shape
    shape = (count, rows // count, width)
    back, full = pl.pallas_call(
        functools.partial(exchange_kernel, bits, count),
        in_specs=[pl.BlockSpec(memory_space=pl.ANY)] * 2,
        out_specs=[pl.BlockSpec(memory_space=pl.ANY)] * 2,
        out_shape=[
            jax.ShapeDtypeStruct(shape, BF16),
            jax.ShapeDtypeStruct((groups, *shard.shape), BF16),
        ],
        scratch_shapes=[
            pltpu.SemaphoreType.DMA((2,)),
            *[pltpu.SemaphoreType.DMA((count - 1,))] * 2,
            *weight_gather_semaphores(groups),
        ],
        compiler_params=pltpu.CompilerParams(collective_id=collective_id, has_side_effects=True),
        name="exchange_and_gather",
    )(values.reshape(shape), shard)
    return back.reshape(rows, width), full.reshape(-1, full.shape[2])


def product_block(dims, left_ref, right_ref, out_ref):
    out_ref[...] = dot(left_ref[...], right_ref[...], dims).astype(BF16)


def multiply_rows(left_ref, right_ref, out_ref):
    (rows, depth), columns = left_ref.shape, right_ref.shape[1]
    tile = TILE // 2
    pltpu.emit_pipeline(
        functools.partial(product_block, (((1,), (0,)), ((), ()))),
        grid=(columns // tile,),
        in_specs=[
            pl.BlockSpec((rows, depth), lambda j: (0, 0)),
            pl.BlockSpec((depth, tile), lambda j: (0, j)),
        ],
        out_specs=[pl.BlockSpec((rows, tile), lambda j: (0, j))],
    )(left_ref, right_ref, out_ref)


def multiply_columns(left_ref, right_ref, out_ref):
    (rows, columns), width = left_ref.shape, right_ref.shape[1]
    tile = TILE // 2
    pltpu.emit_pipeline(
        functools.partial(product_block, CONTRACT_ROWS),
        grid=(columns // tile,),
        in_specs=[
            pl.BlockSpec((rows, tile), lambda j: (0, j)),
            pl.BlockSpec((rows, width), lambda j: (0, 0)),
        ],
        out_specs=[pl.BlockSpec((tile, width), lambda j: (j, 0))],
    )(left_ref, right_ref, out_ref)


def exchange_multiply_kernel(count, jobs, *refs):
    values_ref, refs = refs[0], refs[1:]
    given, refs = refs[: 2 * len(jobs)], refs[2 * len(jobs) :]
    back_ref, *made, local, sent, got = refs
    me = lax.axis_index("grp")
    place = lax.axis_index("ep")
    others = [lax.rem(place + shift, count) for shift in range(1, count)]
    barrier = greet([(me, other) for other in others])
    pl.semaphore_wait(barrier, count - 1)
    copies = [
        pltpu.make_async_remote_copy(
            src_ref=values_ref.at[other],
            dst_ref=back_ref.at[place],
            send_sem=sent.at[index],
            recv_sem=got.at[index],
            device_id=(me, other),
            device_id_type=MESH,
        )
        for index, other in enumerate(others)
    ]
    own = pltpu.make_async_copy(values_ref.at[place], back_ref.at[place], local)
    for copy in copies:
        copy.start()
    own.start()
    for index, job in enumerate(jobs):
        job(given[2 * index], given[2 * index + 1], made[index])
    for copy in copies:
        copy.wait()
    own.wait()


def exchange_and_multiply(values, jobs, collective_id):
    count = lax.axis_size("ep")
    rows, width = values.shape
    shape = (count, rows // count, width)
    outs, flops = [], 0
    for job, left, right in jobs:
        by_rows = job is multiply_rows
        outs.append(
            jax.ShapeDtypeStruct((left.shape[0 if by_rows else 1], right.shape[1]), BF16)
        )
        flops += 2 * left.shape[0] * left.shape[1] * right.shape[1]
    back, *made = pl.pallas_call(
        functools.partial(exchange_multiply_kernel, count, [job for job, _, _ in jobs]),
        in_specs=[pl.BlockSpec(memory_space=pl.ANY)] * (1 + 2 * len(jobs)),
        out_specs=[pl.BlockSpec(memory_space=pl.ANY)] * (1 + len(jobs)),
        out_shape=[jax.ShapeDtypeStruct(shape, BF16), *outs],
        scratch_shapes=[
            pltpu.SemaphoreType.DMA,
            *[pltpu.SemaphoreType.DMA((count - 1,))] * 2,
        ],
        compiler_params=pltpu.CompilerParams(
            collective_id=collective_id, has_side_effects=True, vmem_limit_bytes=VMEM_BYTES
        ),
        cost_estimate=pl.CostEstimate(
            flops=flops, bytes_accessed=4 * rows * width, transcendentals=0
        ),
        name="exchange_and_multiply",
    )(values.reshape(shape), *[array for _, left, right in jobs for array in (left, right)])
    return back.reshape(rows, width), made


def exchange_scatter_kernel(bits, count, lefts, sources, jobs, exchanged, *refs):
    values_ref, refs = (refs[0], refs[1:]) if exchanged else (None, refs)
    splits, refs = refs[: 2 * lefts], refs[2 * lefts :]
    many = 1 + sources[-1][1]
    rights, refs = refs[:many], refs[many:]
    inputs = sum(job.inputs for job in jobs)
    given, refs = refs[:inputs], refs[inputs:]
    back_ref, refs = (refs[0], refs[1:]) if exchanged else (None, refs)
    total_ref, *refs = refs
    made, refs = refs[: len(jobs)], refs[len(jobs) :]
    core_send, core_got, kept, *refs = refs
    stages = bits - 1
    sends, refs = refs[:stages], refs[stages:]
    gots, refs = refs[:stages], refs[stages:]
    local, out_sent, out_got, core_sent, core_came, stage_sent, stage_came = refs
    me = lax.axis_index("grp")
    place = lax.axis_index("ep")
    others = [lax.rem(place + shift, count) for shift in range(1, count)] if exchanged else []
    near = [(me ^ (1 << bit), place) for bit in range(bits)]
    barrier = greet(near + [(me, other) for other in others])
    pl.semaphore_wait(barrier, len(near) + len(others))
    copies = [
        pltpu.make_async_remote_copy(
            src_ref=values_ref.at[other],
            dst_ref=back_ref.at[place],
            send_sem=out_sent.at[index],
            recv_sem=out_got.at[index],
            device_id=(me, other),
            device_id_type=MESH,
        )
        for index, other in enumerate(others)
    ]
    for copy in copies:
        copy.start()
    if exchanged:
        copies.append(pltpu.make_async_copy(values_ref.at[place], back_ref.at[place], local))
        copies[-1].start()

    chunks, blocks, rows, width = kept.shape
    orders = list(range(1, bits)), list(range(1, bits))[::-1]

    def flip(chunk):
        return pltpu.make_async_remote_copy(
            src_ref=core_send.at[chunk],
            dst_ref=core_got.at[chunk],
            send_sem=core_sent.at[chunk],
            recv_sem=core_came.at[chunk],
            device_id=near[0],
            device_id_type=MESH,
        )

    def products(chunk):
        left, source, at = sources[chunk]
        columns = slice(at * width, (at + 1) * width)

        def fill(left_ref, into):
            @pl.loop(0, blocks)
            def _(block):
                offset = pl.multiple_of(((me ^ (2 * block)) // 2) * rows, rows)
                into[chunk, block] = dot(
                    left_ref[:, pl.ds(offset, rows)], rights[source][:, columns], CONTRACT_ROWS
                ).astype(BF16)

        fill(splits[2 * left + 1], core_send)
        flip(chunk).start()
        fill(splits[2 * left], kept)

    def sent_blocks(chunk, stage):
        order = orders[chunk % 2]
        gone = sum(1 << (bit - 1) for bit in order[:stage])
        return [i for i in range(blocks) if not i & gone and i >> (order[stage] - 1) & 1]

    def total_of(chunk, block, stage):
        value = kept[chunk, block].astype(F32) + core_got[chunk, block].astype(F32)
        for before in range(stage):
            bit = 1 << (orders[chunk % 2][before] - 1)
            at = sent_blocks(chunk, before).index(block ^ bit)
            value = value + gots[before][chunk, at].astype(F32)
        return value

    def transfer(chunk, stage):
        return pltpu.make_async_remote_copy(
            src_ref=sends[stage].at[chunk],
            dst_ref=gots[stage].at[chunk],
            send_sem=stage_sent.at[chunk, stage],
            recv_sem=stage_came.at[chunk, stage],
            device_id=near[orders[chunk % 2][stage]],
            device_id_type=MESH,
        )

    def come(chunk, stage):
        if stage == 0:
            flip(chunk).wait_recv()
        else:
            transfer(chunk, stage - 1).wait_recv()

    def advance(chunk, stage):
        come(chunk, stage)
        for at, block in enumerate(sent_blocks(chunk, stage)):
            sends[stage][chunk, at] = total_of(chunk, block, stage).astype(BF16)
        transfer(chunk, stage).start()

    for chunk in range(chunks):
        products(chunk)
        if chunk:
            advance(chunk - 1, 0)
    advance(chunks - 1, 0)
    for job, out_ref in zip(jobs, made):
        job(*given[: job.inputs], out_ref)
        given = given[job.inputs :]
    for stage in range(1, stages):
        for chunk in range(chunks):
            advance(chunk, stage)
    for chunk in range(chunks):
        come(chunk, stages)
        total_ref[:, chunk * width : (chunk + 1) * width] = total_of(chunk, 0, stages).astype(BF16)
    for chunk in range(chunks):
        flip(chunk).wait_send()
        for stage in range(stages):
            transfer(chunk, stage).wait_send()
    for copy in copies:
        copy.wait()


def exchange_and_scatter(values, products, collective_id, jobs=(), costs=True):
    groups, count = lax.axis_size("grp"), lax.axis_size("ep")
    bits = groups.bit_length() - 1
    exchanged = values is not None
    columns = 1024
    splits, rights, sources = [], [], []
    for split, right in products:
        if not splits or splits[-1] is not split:
            splits.append(split)
        for at in range(right.shape[1] // columns):
            sources.append((len(splits) - 1, len(rights), at))
        rights.append(right)
    chunks, blocks = len(sources), groups // 2
    own_rows = splits[0][0].shape[1] // blocks
    block = (own_rows, columns)
    buffer = pltpu.VMEM((chunks, blocks, *block), BF16)
    stages = [pltpu.VMEM((chunks, blocks >> (at + 1), *block), BF16) for at in range(bits - 1)]
    vmem = pl.BlockSpec(memory_space=pltpu.VMEM)
    anywhere = pl.BlockSpec(memory_space=pl.ANY)
    flops = 8 * splits[0][0].size * chunks * columns if costs else 0
    arrays = [array for _, inputs, _ in jobs for array in inputs]
    back_shape = []
    if exchanged:
        rows, width = values.shape
        values = values.reshape(count, rows // count, width)
        back_shape = [jax.ShapeDtypeStruct(values.shape, BF16)]
    outs = pl.pallas_call(
        functools.partial(
            exchange_scatter_kernel,
            bits,
            count,
            len(splits),
            sources,
            [job for job, _, _ in jobs],
            exchanged,
        ),
        in_specs=[anywhere] * exchanged
        + [vmem] * (2 * len(splits) + len(rights))
        + [anywhere] * len(arrays),
        out_specs=[anywhere] * exchanged + [vmem] + [anywhere] * len(jobs),
        out_shape=[
            *back_shape,
            jax.ShapeDtypeStruct((own_rows, chunks * columns), BF16),
            *[out for _, _, out in jobs],
        ],
        scratch_shapes=[
            buffer,
            buffer,
            buffer,
            *stages,
            *stages,
            pltpu.SemaphoreType.DMA,
            *[pltpu.SemaphoreType.DMA((count - 1,))] * 2,
            *[pltpu.SemaphoreType.DMA((chunks,))] * 2,
            *[pltpu.SemaphoreType.DMA((chunks, bits - 1))] * 2,
        ],
        compiler_params=pltpu.CompilerParams(
            collective_id=collective_id, has_side_effects=True, vmem_limit_bytes=60 * 2**20
        ),
        cost_estimate=pl.CostEstimate(flops=flops, bytes_accessed=0, transcendentals=0),
        name="exchange_and_scatter" if exchanged else "scatter",
    )(
        *([values] if exchanged else []),
        *[half for split in splits for half in split],
        *rights,
        *arrays,
    )
    if exchanged:
        return outs[0].reshape(rows, width), outs[1], outs[2:]
    return None, outs[0], outs[1:]


def after(values, *tokens):
    return lax.optimization_barrier((values, *tokens))[0]


def flip(values, bit):
    size = lax.axis_size("grp")
    return lax.ppermute(values, "grp", [(i, i ^ (1 << bit)) for i in range(size)])


def gather_gains(gains):
    size = lax.axis_size("grp")
    me = lax.axis_index("grp")
    for bit in range(size.bit_length() - 1):
        other = flip(gains, bit)
        upper = (me >> bit) & 1
        gains = jnp.where(
            upper == 0,
            jnp.concatenate([gains, other], axis=1),
            jnp.concatenate([other, gains], axis=1),
        )
    return gains


class Scatter:
    def __init__(self, terms, order):
        self.terms = terms
        self.order = list(order)

    def step(self, *tokens):
        if not self.order:
            return
        bit = self.order.pop(0)
        axis = sum(other > bit for other in self.order)
        mine = (lax.axis_index("grp") >> bit) & 1
        terms = self.terms
        if tokens:
            terms = [after(term, *tokens) for term in terms]

        def part(term, which):
            return lax.dynamic_index_in_dim(term, which, axis, keepdims=False)

        self.sent = sum(part(term, 1 - mine).astype(F32) for term in terms).astype(BF16)
        kept = sum(part(term, mine).astype(F32) for term in terms).astype(BF16)
        self.terms = [kept, flip(self.sent, bit)]

    def finish(self):
        while self.order:
            self.step()
        return sum(term.astype(F32) for term in self.terms)


def core_split(values, groups):
    rows, columns = values.shape
    n = columns // groups
    mine = lax.axis_index("grp") & 1
    even = jnp.concatenate([values[:, i * n : (i + 1) * n] for i in range(0, groups, 2)], axis=1)
    odd = jnp.concatenate([values[:, i * n : (i + 1) * n] for i in range(1, groups, 2)], axis=1)
    return jnp.where(mine == 0, even, odd), jnp.where(mine == 0, odd, even)


def scatter_product(split, rights, groups, first=0):
    bits = groups.bit_length() - 1
    results = []
    for place, right in enumerate(rights):
        order = list(range(1, bits))
        if (place + first) % 2:
            order = order[::-1]
        sent = dot(split[1], right, CONTRACT_ROWS).astype(BF16)
        got = flip(sent, 0)
        kept = dot(split[0], right, CONTRACT_ROWS).astype(BF16)
        shape = (2,) * (bits - 1) + (-1, right.shape[1])
        results.append(Scatter([kept.reshape(shape), got.reshape(shape)], order))
        results[-1].sent = sent
    return results


def steps(scatters, *tokens):
    for scatter in scatters:
        scatter.step(*tokens)


def finish(scatters):
    return jnp.concatenate([scatter.finish() for scatter in scatters], axis=1)


def halves(values):
    middle = values.shape[1] // 2
    return values[:, :middle], values[:, middle:]


def exchange(values, experts):
    rows, width = values.shape
    return lax.all_to_all(
        values.reshape(experts, rows // experts, width),
        "ep",
        split_axis=0,
        concat_axis=0,
        tiled=True,
    ).reshape(rows, width)


def local(
    layer_input,
    kv_weight,
    norm_gains,
    query_maps,
    output_maps,
    gate_up_maps,
    down_maps,
    att_routes,
    att_gates,
    mlp_routes,
    mlp_gates,
    segments,
    cotangent,
):
    experts = lax.axis_size("ep")
    groups = lax.axis_size("grp")
    bits = groups.bit_length() - 1
    me_index = lax.axis_index("ep")
    tok_dev = layer_input.shape[0]
    model_width = layer_input.shape[1]
    capacity = 3 * tok_dev // experts
    rows_total = experts * capacity
    hidden = gate_up_maps.shape[2] // 2

    def gather(shard):
        return lax.all_gather(shard, "grp", axis=0, tiled=True)

    gains_full = gather_gains(norm_gains.astype(BF16))
    gain_one = gains_full[0].astype(F32)
    gain_two = gains_full[1].astype(F32)
    xfloat = layer_input.astype(F32)
    inverse_one, unit_one = normalize(xfloat)
    normed_one = (unit_one * gain_one).astype(BF16)

    kv_heads = kv_weight.reshape(2, HEADS, HEAD_DIM, -1).transpose(1, 0, 2, 3)
    kv_shard = kv_heads.reshape(kv_weight.shape).T.astype(BF16)
    cuts = []
    for count in (4, 2, 2, hidden // TILE - 8):
        cuts.append((sum(size for _, size in cuts), count * TILE))

    def gather(shard):
        return lax.all_gather(shard, "grp", axis=0, tiled=True)

    output_shard = output_maps[0].astype(BF16)
    kv_full = gather(kv_shard)
    output_full = gather(output_shard)
    normed_all, query_full, gate_up_low, down_low = opening(
        after(normed_one, output_shard),
        query_maps[0].astype(BF16),
        gate_up_maps[0],
        down_maps[0],
        cuts,
    )
    down_full = gather(down_low)
    gate_up_full = [gather(gate_up_low[0]), None, None, gather(gate_up_low[3])]

    att_named, att_place = expert_places(att_routes[0].reshape(experts, tok_dev, TOP), experts)
    mlp_named, mlp_place = expert_places(mlp_routes[0].reshape(experts, tok_dev, TOP), experts)

    def mine(values, axis):
        return lax.dynamic_index_in_dim(values, me_index, axis, keepdims=False)

    att_pick = one_hot(mine(att_named, 1), mine(att_place, 1), capacity)
    att_send = one_hot(mine(att_named, 0), mine(att_place, 0), capacity).reshape(
        rows_total, tok_dev
    )
    mlp_send = one_hot(mine(mlp_named, 0), mine(mlp_place, 0), capacity).reshape(
        rows_total, tok_dev
    )

    def gates_at(send, routes, gates):
        ids = jnp.arange(experts, dtype=jnp.int32)
        routes = mine(routes.reshape(experts, tok_dev, TOP), 0)
        per_expert = jnp.sum(jnp.where(routes[None] == ids[:, None, None], gates[None], 0.0), axis=2)
        spread = jnp.where(
            send.reshape(experts, capacity, tok_dev), per_expert[:, None, :], 0.0
        ).reshape(rows_total, tok_dev)
        return high_low(spread)

    att_high, att_low = gates_at(att_send, att_routes, att_gates)
    mlp_high, mlp_low = gates_at(mlp_send, mlp_routes, mlp_gates)
    mlp_send = mlp_send.astype(BF16)
    places = jnp.arange(experts * tok_dev, dtype=jnp.int32).reshape(experts, 1, tok_dev)
    starts = segments[0].reshape(experts, 1, tok_dev)
    bounds = jnp.stack(
        [
            jnp.sum(jnp.where(att_pick, starts, 0), axis=2).reshape(-1),
            jnp.sum(jnp.where(att_pick, places, 0), axis=2).reshape(-1),
        ],
        axis=1,
    )
    att_pick = att_pick.astype(BF16)

    cotangent_send = (dot(mlp_high, cotangent) + dot(mlp_low, cotangent)).astype(BF16)
    cotangent_send = after(cotangent_send, normed_all)
    grad_mlp_rows = exchange(cotangent_send, experts)
    att_in = (
        jnp.einsum(
            "sct,std->scd", att_pick, after(normed_all, cotangent_send), preferred_element_type=F32
        )
        .astype(BF16)
        .reshape(rows_total, model_width)
    )
    normed_all = normed_all.reshape(experts * tok_dev, model_width)
    queries = dot(att_in, query_full).astype(BF16)
    keys_values = dot(after(normed_all, queries), kv_full).astype(BF16)
    att_heads, logsums = attend_forward(queries, keys_values, bounds, experts)
    att_rows = dot(after(att_heads, grad_mlp_rows), output_full).astype(BF16)
    att_back, gate_up_full[1] = exchange_and_gather(att_rows, gate_up_low[1], 1)
    residual_one = (
        xfloat + dot(att_high, att_back, CONTRACT_ROWS) + dot(att_low, att_back, CONTRACT_ROWS)
    )

    inverse_two, unit_two = normalize(residual_one)
    normed_two = (unit_two * gain_two).astype(BF16)
    mlp_given = dot(mlp_send, normed_two).astype(BF16)
    mlp_in, gate_up_full[2] = exchange_and_gather(mlp_given, gate_up_low[2], 2)
    mlp_split = core_split(mlp_in, groups)
    acts = [None] * len(cuts)
    grads = [None] * len(cuts)

    def feed_chunk(index, feed_in, total):
        gate_up = gate_up_full[index]
        acts[index], grads[index] = feed(
            feed_in, grad_mlp_rows, gate_up, down_full, cuts[index][0]
        )
        if index == 0:
            steps(middle_scatter, acts[0])
            grads[0] = after(grads[0], *[scatter.sent for scatter in middle_scatter])
        return total + dot(grads[index], gate_up, CONTRACT_COLUMNS)

    normed_split = core_split(normed_all, groups)
    att_split = core_split(att_in, groups)
    heads_split = core_split(att_heads, groups)
    grad_mlp_in = feed_chunk(
        1, after(mlp_in, *mlp_split, *normed_split, *att_split, *heads_split), 0.0
    )
    grad_mlp_in = feed_chunk(2, after(mlp_in, grad_mlp_in), grad_mlp_in)
    middle_scatter = scatter_product(mlp_split, [after(grads[1], grad_mlp_in), grads[2]], groups)
    ready = [array for scatter in middle_scatter for array in (scatter.terms[0], scatter.sent)]
    grad_mlp_in = feed_chunk(0, after(mlp_in, *ready), grad_mlp_in)
    first_grad = dot(
        mlp_in,
        after(grads[0], grad_mlp_in),
        CONTRACT_ROWS,
    ).astype(BF16)
    first_grad_sum = lax.psum_scatter(first_grad, "grp", scatter_dimension=0, tiled=True)
    grad_mlp_in = feed_chunk(3, after(mlp_in, first_grad), grad_mlp_in).astype(BF16)
    activated = jnp.concatenate(acts, axis=1)
    mlp_returned, (down_grad, last_grad) = exchange_and_multiply(
        grad_mlp_in,
        [(multiply_columns, activated, grad_mlp_rows), (multiply_columns, mlp_in, grads[3])],
        3,
    )
    down_grad_sum = lax.psum_scatter(down_grad, "grp", scatter_dimension=0, tiled=True)
    last_grad_sum = lax.psum_scatter(
        after(last_grad, down_grad), "grp", scatter_dimension=0, tiled=True
    )

    grad_final = cotangent.astype(F32)
    grad_normed_two = dot(mlp_send, mlp_returned, CONTRACT_ROWS)
    grad_inner_two, grad_gain_two = norm_backward(grad_normed_two, unit_two, inverse_two, gain_two)
    grad_residual = grad_final + grad_inner_two

    res_high, res_low = high_low(grad_residual)
    sent_four = (
        dot(att_high, res_high) + dot(att_low, res_high) + dot(att_high, res_low)
    ).astype(BF16)
    grad_att_rows, (mlp_rows,) = exchange_and_multiply(
        sent_four, [(multiply_rows, activated, down_full)], 4
    )
    steps(middle_scatter, grad_att_rows)
    ready = [array for scatter in middle_scatter for array in (scatter.terms[0], scatter.sent)]
    grad_heads = dot(
        after(grad_att_rows, *ready), output_full, CONTRACT_COLUMNS
    ).astype(BF16)
    mlp_back = exchange(after(mlp_rows, grad_heads), experts)
    grad_queries, grad_kv = attend_backward(
        queries, keys_values, grad_heads, bounds, logsums, experts
    )
    grad_att_in = dot(grad_queries, query_full, CONTRACT_COLUMNS).astype(BF16)
    grad_all = (
        jnp.einsum(
            "sct,scd->std",
            att_pick,
            grad_att_in.reshape(experts, capacity, model_width),
            preferred_element_type=F32,
        ).reshape(experts * tok_dev, model_width)
        + dot(grad_kv, kv_full, CONTRACT_COLUMNS)
    ).astype(BF16)
    grad_back, kv_part, _ = exchange_and_scatter(
        after(grad_all, mlp_back, first_grad_sum, down_grad_sum), [(normed_split, grad_kv)], 5
    )
    kv_grad = lax.psum(kv_part, "ep")
    while middle_scatter[0].order:
        steps(middle_scatter)
    middle_terms = [[after(term, kv_part) for term in scatter.terms] for scatter in middle_scatter]
    _, both_maps, _ = exchange_and_scatter(
        None,
        [
            (att_split, after(grad_queries, kv_part, last_grad_sum)),
            (heads_split, grad_att_rows),
        ],
        6,
        costs=False,
    )
    kv_grad = after(kv_grad, both_maps)
    chunks = [[first_grad_sum], *middle_terms, [last_grad_sum]]
    gate_up_grad = assemble([[after(term, kv_grad) for term in terms] for terms in chunks])[None]
    down_grad = after(down_grad_sum, kv_grad).astype(F32)[None]
    query_grad, output_grad = [part.astype(F32)[None] for part in halves(both_maps)]
    mlp_back = after(mlp_back, kv_grad)
    output = (
        residual_one + dot(mlp_high, mlp_back, CONTRACT_ROWS) + dot(mlp_low, mlp_back, CONTRACT_ROWS)
    ).astype(BF16)
    grad_normed_one = jnp.sum(
        grad_back.reshape(experts, tok_dev, model_width).astype(F32), axis=0
    )
    kv_grad = transpose(kv_grad)
    grad_inner_one, grad_gain_one = norm_backward(grad_normed_one, unit_one, inverse_one, gain_one)
    grad_input = grad_residual + grad_inner_one

    gains_grad = jnp.stack([grad_gain_one, grad_gain_two])
    gains_grad = gains_grad.reshape((2,) + (2,) * bits + (-1,))
    for bit in reversed(range(bits)):
        mine_bit = (lax.axis_index("grp") >> bit) & 1
        kept = lax.dynamic_index_in_dim(gains_grad, mine_bit, 1, keepdims=False)
        sent = lax.dynamic_index_in_dim(gains_grad, 1 - mine_bit, 1, keepdims=False)
        gains_grad = kept + lax.ppermute(
            sent, "grp", [(i, i ^ (1 << bit)) for i in range(groups)]
        )
    for bit in range(experts.bit_length() - 1):
        gains_grad = gains_grad + lax.ppermute(
            gains_grad, "ep", [(i, i ^ (1 << bit)) for i in range(experts)]
        )
    return (
        output,
        grad_input,
        kv_grad,
        gains_grad,
        query_grad,
        output_grad,
        gate_up_grad,
        down_grad,
    )


def solution(mesh):
    placed = (
        P(("grp", "ep"), None),
        P(None, "grp"),
        P(None, "grp"),
        P("ep", "grp", None),
        P("ep", "grp", None),
        P("ep", "grp", None),
        P("ep", "grp", None),
        P("grp", None, None),
        P(("grp", "ep"), None),
        P("grp", None, None),
        P(("grp", "ep"), None),
        P("grp", None),
        P(("grp", "ep"), None),
    )
    return jax.shard_map(
        local,
        mesh=mesh,
        in_specs=placed,
        out_specs=(
            P(("grp", "ep"), None),
            P(("grp", "ep"), None),
            P(None, "grp"),
            P(None, "grp"),
            P("ep", "grp", None),
            P("ep", "grp", None),
            P("ep", "grp", None),
            P("ep", "grp", None),
        ),
        check_vma=False,
    )
```

```python
import functools

import jax
import jax.numpy as jnp
from jax import lax
from jax.experimental import pallas as pl
from jax.experimental.pallas import tpu as pltpu
from jax.sharding import PartitionSpec as P

HEADS = 16
HEAD_DIM = 128
TOP = 2


EPSILON = 1e-06
NEGATIVE = -1e30
LOG2_E = 1.4426950408889634
CONTRACT_ROWS = (((0,), (0,)), ((), ()))
CONTRACT_COLUMNS = (((1,), (1,)), ((), ()))
BF16 = jnp.bfloat16
F32 = jnp.float32
VMEM_BYTES = 56 * 2**20
TILE = 512
NO_COST = pl.CostEstimate(flops=0, bytes_accessed=0, transcendentals=0)


def normalize(values):
    inverse = lax.rsqrt(jnp.mean(values * values, axis=-1, keepdims=True) + EPSILON)
    return (inverse, values * inverse)


def norm_backward(grad_normed, unit, inverse, gain):
    grad_unit = grad_normed * gain
    inner = jnp.mean(grad_unit * unit, axis=-1, keepdims=True)
    return (inverse * (grad_unit - unit * inner), jnp.sum(grad_normed * unit, axis=0))


def dot(left, right, dims=(((1,), (0,)), ((), ()))):
    return lax.dot_general(left, right, dims, preferred_element_type=F32)


def high_low(values):
    high = values.astype(BF16)
    return high, (values - high.astype(F32)).astype(BF16)


def expert_places(routes, experts):
    tokens = routes.shape[1]
    ids = jnp.arange(experts, dtype=jnp.int32)
    named = jnp.any(routes[:, None, :, :] == ids[None, :, None, None], axis=3)
    before = (jnp.arange(tokens)[:, None] < jnp.arange(tokens)[None, :]).astype(BF16)
    place = lax.dot_general(
        named.astype(BF16), before, (((2,), (0,)), ((), ())), preferred_element_type=F32
    )
    return named, place.astype(jnp.int32)


def one_hot(named, place, capacity):
    rows = jnp.arange(capacity, dtype=jnp.int32)[:, None]
    return named[..., None, :] & (place[..., None, :] == rows)


def attend_forward_kernel(sources, query_ref, key_ref, value_ref, bounds_ref, out_ref, logsum_ref):
    head = pl.program_id(0)
    capacity = query_ref.shape[0] // sources
    tokens = key_ref.shape[0] // sources
    scaling = HEAD_DIM ** (-0.5) * LOG2_E

    @pl.when(head == 0)
    def _():
        logsum_ref[...] = jnp.zeros_like(logsum_ref)

    for source in range(sources):
        rows = slice(source * capacity, (source + 1) * capacity)
        span = (source + 1) * tokens
        first = bounds_ref[rows, 0:1]
        last = bounds_ref[rows, 1:2]
        scores = dot(query_ref[rows, :], key_ref[:span, :], CONTRACT_COLUMNS) * scaling
        places = lax.broadcasted_iota(jnp.int32, scores.shape, 1)
        scores = jnp.where((places >= first) & (places <= last), scores, NEGATIVE)
        peak = jnp.max(scores, axis=1, keepdims=True)
        exponent = jnp.exp2(scores - peak)
        total = jnp.sum(exponent, axis=1, keepdims=True)
        mixed = dot(exponent.astype(BF16), value_ref[:span, :])
        out_ref[rows, :] = (mixed * (1.0 / total)).astype(BF16)
        lanes = lax.broadcasted_iota(jnp.int32, (capacity, 128), 1)
        logsum_ref[rows, :] = jnp.where(lanes == head, peak + jnp.log2(total), logsum_ref[rows, :])


def attend_forward(queries, keys_values, bounds, sources):
    rows, features = queries.shape
    seq = keys_values.shape[0]
    return pl.pallas_call(
        functools.partial(attend_forward_kernel, sources),
        grid=(HEADS,),
        in_specs=[
            pl.BlockSpec((rows, HEAD_DIM), lambda h: (0, h)),
            pl.BlockSpec((seq, HEAD_DIM), lambda h: (0, 2 * h)),
            pl.BlockSpec((seq, HEAD_DIM), lambda h: (0, 2 * h + 1)),
            pl.BlockSpec((rows, 2), lambda h: (0, 0)),
        ],
        out_specs=[
            pl.BlockSpec((rows, HEAD_DIM), lambda h: (0, h)),
            pl.BlockSpec((rows, 128), lambda h: (0, 0)),
        ],
        out_shape=[
            jax.ShapeDtypeStruct((rows, features), BF16),
            jax.ShapeDtypeStruct((rows, 128), F32),
        ],
        compiler_params=pltpu.CompilerParams(vmem_limit_bytes=VMEM_BYTES),
        cost_estimate=NO_COST,
        name="attend_forward",
    )(queries, keys_values, keys_values, bounds)


def attend_backward_kernel(
    sources,
    query_ref,
    key_ref,
    value_ref,
    grad_ref,
    bounds_ref,
    logsum_ref,
    values_ref,
    grad_query_ref,
    grad_both_ref,
    back_ref,
    key_total,
    value_total,
    local,
    sent,
    got,
):
    head = pl.program_id(0)
    me = lax.axis_index("grp")
    place = lax.axis_index("ep")
    others = [lax.rem(place + shift, sources) for shift in range(1, sources)]
    columns = pl.ds(0, back_ref.shape[2])
    copies = [
        pltpu.make_async_remote_copy(
            src_ref=values_ref.at[other, :, columns],
            dst_ref=back_ref.at[place],
            send_sem=sent.at[index],
            recv_sem=got.at[index],
            device_id=(me, other),
            device_id_type=MESH,
        )
        for index, other in enumerate(others)
    ]
    copies.append(
        pltpu.make_async_copy(values_ref.at[place, :, columns], back_ref.at[place], local)
    )

    @pl.when(head == 0)
    def _():
        pl.semaphore_wait(greet([(me, other) for other in others]), len(others))
        for copy in copies:
            copy.start()

    capacity = query_ref.shape[0] // sources
    tokens = key_ref.shape[0] // sources
    scaling = HEAD_DIM ** (-0.5)
    for source in reversed(range(sources)):
        rows = slice(source * capacity, (source + 1) * capacity)
        span = (source + 1) * tokens
        first = bounds_ref[rows, 0:1]
        last = bounds_ref[rows, 1:2]
        query = query_ref[rows, :]
        grad = grad_ref[rows, :]
        lanes = lax.broadcasted_iota(jnp.int32, (capacity, 128), 1)
        logsum = jnp.sum(
            jnp.where(lanes == head, logsum_ref[rows, :], 0.0), axis=1, keepdims=True
        )
        scores = dot(query, key_ref[:span, :], CONTRACT_COLUMNS) * (scaling * LOG2_E)
        places = lax.broadcasted_iota(jnp.int32, scores.shape, 1)
        scores = jnp.where((places >= first) & (places <= last), scores, NEGATIVE)
        probs = jnp.exp2(scores - logsum)
        grad_probs = dot(grad, value_ref[:span, :], CONTRACT_COLUMNS)
        weighted = probs * grad_probs
        correction = jnp.sum(weighted, axis=1, keepdims=True)
        grad_scores = (weighted - probs * correction).astype(BF16)
        grad_query_ref[rows, :] = (dot(grad_scores, key_ref[:span, :]) * scaling).astype(BF16)
        key_part = dot(grad_scores, query, CONTRACT_ROWS)
        value_part = dot(probs.astype(BF16), grad, CONTRACT_ROWS)
        if source == sources - 1:
            key_total[...] = key_part
            value_total[...] = value_part
        else:
            key_total[:span, :] += key_part
            value_total[:span, :] += value_part
    grad_both_ref[:, :HEAD_DIM] = (key_total[...] * scaling).astype(BF16)
    grad_both_ref[:, HEAD_DIM:] = value_total[...].astype(BF16)

    @pl.when(head == HEADS - 1)
    def _():
        for copy in copies:
            copy.wait()


def attend_backward(
    queries, keys_values, grads, bounds, logsums, values, sources, collective_id
):
    rows = queries.shape[0]
    features = HEADS * HEAD_DIM
    seq = keys_values.shape[0]
    shape = (sources, values.shape[0] // sources, values.shape[1])
    grad_queries, grad_both, back = pl.pallas_call(
        functools.partial(attend_backward_kernel, sources),
        grid=(HEADS,),
        in_specs=[
            pl.BlockSpec((rows, HEAD_DIM), lambda h: (0, h)),
            pl.BlockSpec((seq, HEAD_DIM), lambda h: (0, 2 * h)),
            pl.BlockSpec((seq, HEAD_DIM), lambda h: (0, 2 * h + 1)),
            pl.BlockSpec((rows, HEAD_DIM), lambda h: (0, h)),
            pl.BlockSpec((rows, 2), lambda h: (0, 0)),
            pl.BlockSpec((rows, 128), lambda h: (0, 0)),
            pl.BlockSpec(memory_space=pl.ANY),
        ],
        out_specs=[
            pl.BlockSpec((rows, HEAD_DIM), lambda h: (0, h)),
            pl.BlockSpec((seq, 2 * HEAD_DIM), lambda h: (0, h)),
            pl.BlockSpec(memory_space=pl.ANY),
        ],
        out_shape=[
            jax.ShapeDtypeStruct((rows, features), BF16),
            jax.ShapeDtypeStruct((seq, 2 * features), BF16),
            jax.ShapeDtypeStruct((*shape[:2], shape[2] // 2), BF16),
        ],
        scratch_shapes=[
            pltpu.VMEM((seq, HEAD_DIM), F32),
            pltpu.VMEM((seq, HEAD_DIM), F32),
            pltpu.SemaphoreType.DMA,
            *[pltpu.SemaphoreType.DMA((sources - 1,))] * 2,
        ],
        compiler_params=pltpu.CompilerParams(
            collective_id=collective_id, has_side_effects=True, vmem_limit_bytes=VMEM_BYTES
        ),
        cost_estimate=NO_COST,
        name="attend_backward",
    )(queries, keys_values, keys_values, grads, bounds, logsums, values.reshape(shape))
    return grad_queries, grad_both, back.reshape(values.shape[0], -1)


def feed_kernel(in_ref, grad_ref, gate_up_ref, down_ref, *refs):
    act_ref, grad_gate_up_ref = refs[-2:]
    units = down_ref.shape[0]
    step = units // 2
    for start in range(0, units, step):
        here = slice(start, start + step)
        there = slice(units + start, units + start + step)
        gate = dot(in_ref[...], gate_up_ref[:, here])
        up = dot(in_ref[...], gate_up_ref[:, there])
        grad_act = dot(grad_ref[...], down_ref[here, :], CONTRACT_COLUMNS)
        sigmoid = jax.nn.sigmoid(gate)
        silu = gate * sigmoid
        act_ref[:, here] = (silu * up).astype(BF16)
        grad_gate_up_ref[:, here] = (
            grad_act * up * sigmoid * (1.0 + gate * (1.0 - sigmoid))
        ).astype(BF16)
        grad_gate_up_ref[:, there] = (grad_act * silu).astype(BF16)


def feed(inputs, grads, gate_up, down, offset, acts=None):
    rows, width = inputs.shape
    units = gate_up.shape[1] // 2
    tiles = units // TILE
    start = offset // TILE
    before = [] if acts is None else [acts]
    return pl.pallas_call(
        feed_kernel,
        grid=(tiles,),
        in_specs=[
            pl.BlockSpec((rows, width), lambda j: (0, 0)),
            pl.BlockSpec((rows, width), lambda j: (0, 0)),
            pl.BlockSpec((width, 2 * TILE), lambda j: (0, j)),
            pl.BlockSpec((TILE, width), lambda j: (j + start, 0)),
        ]
        + [pl.BlockSpec(memory_space=pl.ANY)] * len(before),
        out_specs=[
            pl.BlockSpec((rows, TILE), lambda j: (0, j + start)),
            pl.BlockSpec((rows, 2 * TILE), lambda j: (0, j)),
        ],
        out_shape=[
            jax.ShapeDtypeStruct((rows, down.shape[0]), BF16),
            jax.ShapeDtypeStruct((rows, 2 * units), BF16),
        ],
        input_output_aliases={4: 0} if before else {},
        compiler_params=pltpu.CompilerParams(vmem_limit_bytes=VMEM_BYTES),
        cost_estimate=NO_COST,
        name="feed",
    )(inputs, grads, gate_up, down, *before)


def back_kernel(grad_ref, weight_ref, *refs):
    *before, out_ref = refs
    value = dot(grad_ref[...], weight_ref[...], CONTRACT_COLUMNS)
    for ref in before:
        value = value + ref[...]
    out_ref[...] = value.astype(out_ref.dtype)


def back(grads, weights, total, dtype):
    (rows, depth), columns = grads.shape, weights.shape[0]
    before = [] if total is None else [total]
    return pl.pallas_call(
        back_kernel,
        grid=(columns // TILE,),
        in_specs=[
            pl.BlockSpec((rows, depth), lambda j: (0, 0)),
            pl.BlockSpec((TILE, depth), lambda j: (j, 0)),
        ]
        + [pl.BlockSpec((rows, TILE), lambda j: (0, j))] * len(before),
        out_specs=pl.BlockSpec((rows, TILE), lambda j: (0, j)),
        out_shape=jax.ShapeDtypeStruct((rows, columns), dtype),
        compiler_params=pltpu.CompilerParams(vmem_limit_bytes=VMEM_BYTES),
        cost_estimate=NO_COST,
        name="back",
    )(grads, weights, *before)


def weight_kernel(left_ref, right_ref, out_ref):
    out_ref[...] = dot(left_ref[...], right_ref[...], CONTRACT_ROWS).astype(BF16)


def weight_product(left, right):
    (rows, columns), width = left.shape, right.shape[1]
    tile = TILE // 2
    return pl.pallas_call(
        weight_kernel,
        grid=(columns // tile,),
        in_specs=[
            pl.BlockSpec((rows, tile), lambda j: (0, j)),
            pl.BlockSpec((rows, width), lambda j: (0, 0)),
        ],
        out_specs=pl.BlockSpec((tile, width), lambda j: (j, 0)),
        out_shape=jax.ShapeDtypeStruct((columns, width), BF16),
        compiler_params=pltpu.CompilerParams(vmem_limit_bytes=VMEM_BYTES),
        cost_estimate=NO_COST,
        name="weight_product",
    )(left, right)


def assemble_kernel(counts, *refs):
    *refs, out_ref = refs
    hidden = out_ref.shape[1] // 2
    start = 0
    for count in counts:
        terms, refs = refs[:count], refs[count:]
        for tile in range(terms[0].shape[1] // (2 * TILE)):
            for half in range(2):
                there = half * hidden + start
                here = (2 * tile + half) * TILE
                out_ref[:, there : there + TILE] = sum(
                    term[:, here : here + TILE].astype(F32) for term in terms
                )
            start += TILE


def assemble(chunks):
    arrays = [term for terms in chunks for term in terms]
    rows = arrays[0].shape[0]
    step = 32
    columns = sum(terms[0].shape[1] for terms in chunks)
    return pl.pallas_call(
        functools.partial(assemble_kernel, [len(terms) for terms in chunks]),
        grid=(rows // step,),
        in_specs=[pl.BlockSpec((step, term.shape[1]), lambda i: (i, 0)) for term in arrays],
        out_specs=pl.BlockSpec((step, columns), lambda i: (i, 0)),
        out_shape=jax.ShapeDtypeStruct((rows, columns), F32),
        compiler_params=pltpu.CompilerParams(vmem_limit_bytes=VMEM_BYTES),
        cost_estimate=NO_COST,
        name="assemble",
    )(*arrays)


def transpose_kernel(steps, in_ref, out_ref):
    for value in range(2):

        @pl.when(pl.program_id(0) // steps == value)
        def _():
            for head in range(TILE // HEAD_DIM):
                columns = slice((2 * head + value) * HEAD_DIM, (2 * head + value + 1) * HEAD_DIM)
                rows = slice(head * HEAD_DIM, (head + 1) * HEAD_DIM)
                out_ref[rows, :] = in_ref[:, columns].astype(F32).T


def transpose(values):
    rows, columns = values.shape
    steps = columns // (2 * TILE)
    return pl.pallas_call(
        functools.partial(transpose_kernel, steps),
        grid=(2 * steps,),
        in_specs=[pl.BlockSpec((rows, 2 * TILE), lambda j: (0, j % steps))],
        out_specs=pl.BlockSpec((TILE, rows), lambda j: (j, 0)),
        out_shape=jax.ShapeDtypeStruct((columns, rows), F32),
        cost_estimate=NO_COST,
        name="transpose",
    )(values)


MESH = pl.DeviceIdType.MESH


def greet(devices, extra=0):
    barrier = pltpu.get_barrier_semaphore()
    for device in devices:
        pl.semaphore_signal(barrier, inc=1, device_id=device, device_id_type=MESH)
    return barrier


class WeightGather:
    def __init__(self, bits, shard_ref, full_ref, sent, got):
        self.me, self.place = lax.axis_index("grp"), lax.axis_index("ep")
        self.bits, self.rows = bits, shard_ref.shape[0] // 2
        self.shard_ref, self.full_ref, self.sent, self.got = shard_ref, full_ref, sent, got
        self.orders = list(range(1, bits)) + [0], list(range(1, bits))[::-1] + [0]
        self.moves = []
        for index in range(1, 1 << (bits - 1)):
            for part in range(2):
                order = self.orders[part]
                far = sum(1 << bit for at, bit in enumerate(order[:-1]) if index >> at & 1)
                self.moves.append((part, far, order[index.bit_length() :]))

    def neighbours(self):
        return [(self.me ^ (1 << bit), self.place) for bit in range(self.bits)]

    def piece(self, part, far, bit):
        here = pl.ds(part * self.rows, self.rows)
        block = self.full_ref.at[self.me ^ far, here]
        return pltpu.make_async_remote_copy(
            src_ref=self.shard_ref.at[here] if far == 0 else block,
            dst_ref=block,
            send_sem=self.sent.at[part, far, bit],
            recv_sem=self.got.at[part, far ^ (1 << bit)],
            device_id=(self.me ^ (1 << bit), self.place),
            device_id_type=MESH,
        )

    def wait_piece(self, part, far):
        block = self.full_ref.at[self.me ^ far, pl.ds(part * self.rows, self.rows)]
        pltpu.make_async_remote_copy(
            src_ref=block,
            dst_ref=block,
            send_sem=self.sent.at[part, far, 0],
            recv_sem=self.got.at[part, far],
            device_id=(self.me ^ 1, self.place),
            device_id_type=MESH,
        ).wait_recv()

    def first(self):
        for part in range(2):
            for bit in self.orders[part]:
                self.piece(part, 0, bit).start()

    def forward(self, part, far, later):
        self.wait_piece(part, far)
        for bit in later:
            self.piece(part, far, bit).start()

    def finish(self):
        for part in range(2):
            for far in range(1 << (self.bits - 1)):
                self.wait_piece(part, 2 * far + 1)
        for part in range(2):
            for bit in self.orders[part]:
                self.piece(part, 0, bit).wait_send()
        for part, far, later in self.moves:
            for bit in later:
                self.piece(part, far, bit).wait_send()


def weight_gather_semaphores(groups):
    bits = groups.bit_length() - 1
    return [pltpu.SemaphoreType.DMA((2, groups, bits)), pltpu.SemaphoreType.DMA((2, groups))]


def opening_kernel(bits, count, chunks, *refs):
    (tokens_ref, shard_ref, gate_up_ref, down_ref, all_ref, full_ref), refs = refs[:6], refs[6:]
    low_refs, refs = refs[:chunks], refs[chunks:]
    down_low_ref, local, up_send, up_got, down_send, down_got, sent, got = refs
    me = lax.axis_index("grp")
    place = lax.axis_index("ep")
    weights = WeightGather(bits, shard_ref, full_ref, sent, got)

    barrier = greet(weights.neighbours())

    @pl.when(place > 0)
    def _():
        pl.semaphore_signal(barrier, inc=1, device_id=(me, place - 1), device_id_type=MESH)

    @pl.when(place < count - 1)
    def _():
        pl.semaphore_signal(barrier, inc=1, device_id=(me, place + 1), device_id_type=MESH)

    ends = jnp.where(place > 0, 1, 0) + jnp.where(place < count - 1, 1, 0)
    pl.semaphore_wait(barrier, bits + ends)

    def upward(hop):
        block = all_ref.at[jnp.maximum(place - hop, 0)]
        return pltpu.make_async_remote_copy(
            src_ref=tokens_ref if hop == 0 else block,
            dst_ref=block,
            send_sem=up_send.at[hop],
            recv_sem=up_got.at[hop],
            device_id=(me, jnp.minimum(place + 1, count - 1)),
            device_id_type=MESH,
        )

    def downward(hop):
        block = all_ref.at[jnp.minimum(place + hop, count - 1)]
        return pltpu.make_async_remote_copy(
            src_ref=tokens_ref if hop == 0 else block,
            dst_ref=block,
            send_sem=down_send.at[hop],
            recv_sem=down_got.at[hop],
            device_id=(me, jnp.maximum(place - 1, 0)),
            device_id_type=MESH,
        )

    def lines(hop, act):
        @pl.when((place + 1 < count) & (place - hop >= 0))
        def _():
            act(upward(hop))

        @pl.when((place - 1 >= 0) & (place + hop < count))
        def _():
            act(downward(hop))

    def line_got(hop):
        @pl.when(place - hop - 1 >= 0)
        def _():
            upward(hop).wait_recv()

        @pl.when(place + hop + 1 < count)
        def _():
            downward(hop).wait_recv()

    lines(0, lambda copy: copy.start())
    weights.first()
    own = [
        pltpu.make_async_copy(tokens_ref, all_ref.at[place], local.at[0]),
        pltpu.make_async_copy(shard_ref, full_ref.at[me], local.at[1]),
    ]
    for copy in own:
        copy.start()

    def round_block(in_ref, out_ref):
        out_ref[...] = in_ref[...].astype(BF16)

    shard_rows, columns = gate_up_ref.shape
    tiles = columns // (2 * TILE)
    start = 0
    for low_ref in low_refs:
        blocks = low_ref.shape[1] // TILE
        pltpu.emit_pipeline(
            round_block,
            grid=(blocks,),
            in_specs=[
                pl.BlockSpec(
                    (shard_rows, TILE), lambda j, start=start: (0, start + j // 2 + j % 2 * tiles)
                )
            ],
            out_specs=[pl.BlockSpec((shard_rows, TILE), lambda j: (0, j))],
        )(gate_up_ref, low_ref)
        start += blocks // 2
    down_rows, width = down_ref.shape
    step = 176
    pltpu.emit_pipeline(
        round_block,
        grid=(down_rows // step,),
        in_specs=[pl.BlockSpec((step, width), lambda j: (j, 0))],
        out_specs=[pl.BlockSpec((step, width), lambda j: (j, 0))],
    )(down_ref, down_low_ref)

    coming = list(weights.moves)
    hops = list(range(count - 1))
    while hops or coming:
        if hops:
            hop = hops.pop(0)
            line_got(hop)
            if hop + 1 < count - 1:
                lines(hop + 1, lambda copy: copy.start())
        for move in coming[:4]:
            weights.forward(*move)
        coming = coming[4:]
    weights.finish()
    for hop in range(count - 1):
        lines(hop, lambda copy: copy.wait_send())
    for copy in own:
        copy.wait()


def opening(tokens, shard, gate_up, down, cuts):
    groups, count = lax.axis_size("grp"), lax.axis_size("ep")
    bits = groups.bit_length() - 1
    whole, full, *lows = pl.pallas_call(
        functools.partial(opening_kernel, bits, count, len(cuts)),
        in_specs=[pl.BlockSpec(memory_space=pl.ANY)] * 4,
        out_specs=[pl.BlockSpec(memory_space=pl.ANY)] * (3 + len(cuts)),
        out_shape=[
            jax.ShapeDtypeStruct((count, *tokens.shape), BF16),
            jax.ShapeDtypeStruct((groups, *shard.shape), BF16),
            *[jax.ShapeDtypeStruct((gate_up.shape[0], 2 * size), BF16) for _, size in cuts],
            jax.ShapeDtypeStruct(down.shape, BF16),
        ],
        scratch_shapes=[
            pltpu.SemaphoreType.DMA((2,)),
            *[pltpu.SemaphoreType.DMA((count - 1,))] * 4,
            *weight_gather_semaphores(groups),
        ],
        compiler_params=pltpu.CompilerParams(
            collective_id=0, has_side_effects=True, vmem_limit_bytes=VMEM_BYTES
        ),
        cost_estimate=NO_COST,
        name="opening",
    )(tokens, shard, gate_up, down)
    return whole, full.reshape(-1, full.shape[2]), lows[:-1], lows[-1]


def exchange_kernel(
    bits, count, values_ref, shard_ref, back_ref, full_ref, local, out_sent, out_got, sent, got
):
    me = lax.axis_index("grp")
    place = lax.axis_index("ep")
    weights = WeightGather(bits, shard_ref, full_ref, sent, got)
    others = [lax.rem(place + shift, count) for shift in range(1, count)]
    barrier = greet(weights.neighbours() + [(me, other) for other in others])
    pl.semaphore_wait(barrier, bits + count - 1)
    copies = [
        pltpu.make_async_remote_copy(
            src_ref=values_ref.at[other],
            dst_ref=back_ref.at[place],
            send_sem=out_sent.at[index],
            recv_sem=out_got.at[index],
            device_id=(me, other),
            device_id_type=MESH,
        )
        for index, other in enumerate(others)
    ]
    own = [
        pltpu.make_async_copy(values_ref.at[place], back_ref.at[place], local.at[0]),
        pltpu.make_async_copy(shard_ref, full_ref.at[me], local.at[1]),
    ]
    for copy in copies:
        copy.start()
    weights.first()
    for copy in own:
        copy.start()
    for move in weights.moves:
        weights.forward(*move)
    weights.finish()
    for copy in copies:
        copy.wait()
    for copy in own:
        copy.wait()


def exchange_and_gather(values, shard, collective_id):
    groups, count = lax.axis_size("grp"), lax.axis_size("ep")
    bits = groups.bit_length() - 1
    rows, width = values.shape
    shape = (count, rows // count, width)
    back, full = pl.pallas_call(
        functools.partial(exchange_kernel, bits, count),
        in_specs=[pl.BlockSpec(memory_space=pl.ANY)] * 2,
        out_specs=[pl.BlockSpec(memory_space=pl.ANY)] * 2,
        out_shape=[
            jax.ShapeDtypeStruct(shape, BF16),
            jax.ShapeDtypeStruct((groups, *shard.shape), BF16),
        ],
        scratch_shapes=[
            pltpu.SemaphoreType.DMA((2,)),
            *[pltpu.SemaphoreType.DMA((count - 1,))] * 2,
            *weight_gather_semaphores(groups),
        ],
        compiler_params=pltpu.CompilerParams(collective_id=collective_id, has_side_effects=True),
        cost_estimate=NO_COST,
        name="exchange_and_gather",
    )(values.reshape(shape), shard)
    return back.reshape(rows, width), full.reshape(-1, full.shape[2])


def product_block(dims, left_ref, right_ref, out_ref):
    out_ref[...] = dot(left_ref[...], right_ref[...], dims).astype(BF16)


def multiply_rows(left_ref, right_ref, out_ref):
    (rows, depth), columns = left_ref.shape, right_ref.shape[1]
    tile = TILE // 2
    pltpu.emit_pipeline(
        functools.partial(product_block, (((1,), (0,)), ((), ()))),
        grid=(columns // tile,),
        in_specs=[
            pl.BlockSpec((rows, depth), lambda j: (0, 0)),
            pl.BlockSpec((depth, tile), lambda j: (0, j)),
        ],
        out_specs=[pl.BlockSpec((rows, tile), lambda j: (0, j))],
    )(left_ref, right_ref, out_ref)


def multiply_columns(left_ref, right_ref, out_ref):
    (rows, columns), width = left_ref.shape, right_ref.shape[1]
    tile = TILE // 2
    pltpu.emit_pipeline(
        functools.partial(product_block, CONTRACT_ROWS),
        grid=(columns // tile,),
        in_specs=[
            pl.BlockSpec((rows, tile), lambda j: (0, j)),
            pl.BlockSpec((rows, width), lambda j: (0, 0)),
        ],
        out_specs=[pl.BlockSpec((tile, width), lambda j: (j, 0))],
    )(left_ref, right_ref, out_ref)


def exchange_multiply_kernel(count, jobs, bits, *refs):
    values_ref, refs = refs[0], refs[1:]
    given, refs = refs[: 2 * len(jobs)], refs[2 * len(jobs) :]
    passed, refs = refs[: len(bits)], refs[len(bits) :]
    back_ref, refs = refs[0], refs[1:]
    made, refs = refs[: len(jobs)], refs[len(jobs) :]
    taken, refs = refs[: len(bits)], refs[len(bits) :]
    local, sent, got, pass_sent, pass_got = refs
    me = lax.axis_index("grp")
    place = lax.axis_index("ep")
    others = [lax.rem(place + shift, count) for shift in range(1, count)]
    across = [(me ^ (1 << bit), place) for bit in sorted(set(bits))]
    barrier = greet([(me, other) for other in others] + across)
    pl.semaphore_wait(barrier, len(others) + len(across))
    copies = [
        pltpu.make_async_remote_copy(
            src_ref=values_ref.at[other],
            dst_ref=back_ref.at[place],
            send_sem=sent.at[index],
            recv_sem=got.at[index],
            device_id=(me, other),
            device_id_type=MESH,
        )
        for index, other in enumerate(others)
    ]
    copies += [
        pltpu.make_async_remote_copy(
            src_ref=passed[index],
            dst_ref=taken[index],
            send_sem=pass_sent.at[index],
            recv_sem=pass_got.at[index],
            device_id=(me ^ (1 << bit), place),
            device_id_type=MESH,
        )
        for index, bit in enumerate(bits)
    ]
    copies.append(pltpu.make_async_copy(values_ref.at[place], back_ref.at[place], local))
    for copy in copies:
        copy.start()
    for index, job in enumerate(jobs):
        job(given[2 * index], given[2 * index + 1], made[index])
    for copy in copies:
        copy.wait()


def exchange_and_multiply(values, jobs, scatters, collective_id):
    count = lax.axis_size("ep")
    rows, width = values.shape
    shape = (count, rows // count, width)
    outs = []
    for job, left, right in jobs:
        by_rows = job is multiply_rows
        outs.append(
            jax.ShapeDtypeStruct((left.shape[0 if by_rows else 1], right.shape[1]), BF16)
        )
    passed = [scatter.sent for scatter in scatters]
    outs += [jax.ShapeDtypeStruct(array.shape, BF16) for array in passed]
    back, *made = pl.pallas_call(
        functools.partial(
            exchange_multiply_kernel,
            count,
            [job for job, _, _ in jobs],
            [scatter.bit for scatter in scatters],
        ),
        in_specs=[pl.BlockSpec(memory_space=pl.ANY)] * (1 + 2 * len(jobs) + len(passed)),
        out_specs=[pl.BlockSpec(memory_space=pl.ANY)] * (1 + len(outs)),
        out_shape=[jax.ShapeDtypeStruct(shape, BF16), *outs],
        scratch_shapes=[
            pltpu.SemaphoreType.DMA,
            *[pltpu.SemaphoreType.DMA((count - 1,))] * 2,
            *[pltpu.SemaphoreType.DMA((max(len(passed), 1),))] * 2,
        ],
        compiler_params=pltpu.CompilerParams(
            collective_id=collective_id, has_side_effects=True, vmem_limit_bytes=VMEM_BYTES
        ),
        cost_estimate=NO_COST,
        name="exchange_and_multiply",
    )(
        values.reshape(shape),
        *[array for _, left, right in jobs for array in (left, right)],
        *passed,
    )
    for scatter, got in zip(scatters, made[len(jobs) :]):
        scatter.receive(got)
    return back.reshape(rows, width), made[: len(jobs)]


def exchange_scatter_kernel(bits, count, lefts, sources, jobs, exchanged, *refs):
    values_refs, refs = refs[:exchanged], refs[exchanged:]
    splits, refs = refs[: 2 * lefts], refs[2 * lefts :]
    many = 1 + sources[-1][1]
    rights, refs = refs[:many], refs[many:]
    inputs = sum(job.inputs for job in jobs)
    given, refs = refs[:inputs], refs[inputs:]
    back_refs, refs = refs[:exchanged], refs[exchanged:]
    total_ref, *refs = refs
    made, refs = refs[: len(jobs)], refs[len(jobs) :]
    core_send, core_got, kept, *refs = refs
    stages = bits - 1
    sends, refs = refs[:stages], refs[stages:]
    gots, refs = refs[:stages], refs[stages:]
    local, out_sent, out_got, core_sent, core_came, stage_sent, stage_came = refs
    me = lax.axis_index("grp")
    place = lax.axis_index("ep")
    others = [lax.rem(place + shift, count) for shift in range(1, count)] if exchanged else []
    near = [(me ^ (1 << bit), place) for bit in range(bits)]
    barrier = greet(near + [(me, other) for other in others])
    pl.semaphore_wait(barrier, len(near) + len(others))
    copies = []
    for which, (values_ref, back_ref) in enumerate(zip(values_refs, back_refs)):
        width = back_ref.shape[2]
        columns = pl.ds(values_ref.shape[2] - width, width)
        copies += [
            pltpu.make_async_remote_copy(
                src_ref=values_ref.at[other, :, columns],
                dst_ref=back_ref.at[place],
                send_sem=out_sent.at[which, index],
                recv_sem=out_got.at[which, index],
                device_id=(me, other),
                device_id_type=MESH,
            )
            for index, other in enumerate(others)
        ]
        copies.append(
            pltpu.make_async_copy(
                values_ref.at[place, :, columns], back_ref.at[place], local.at[which]
            )
        )
    for copy in copies:
        copy.start()

    chunks, blocks, rows, width = kept.shape
    orders = list(range(1, bits)), list(range(1, bits))[::-1]

    def flip(chunk):
        return pltpu.make_async_remote_copy(
            src_ref=core_send.at[chunk],
            dst_ref=core_got.at[chunk],
            send_sem=core_sent.at[chunk],
            recv_sem=core_came.at[chunk],
            device_id=near[0],
            device_id_type=MESH,
        )

    def products(chunk):
        left, source, at = sources[chunk]
        columns = slice(at * width, (at + 1) * width)

        def fill(left_ref, into):
            @pl.loop(0, blocks)
            def _(block):
                offset = pl.multiple_of(((me ^ (2 * block)) // 2) * rows, rows)
                into[chunk, block] = dot(
                    left_ref[:, pl.ds(offset, rows)], rights[source][:, columns], CONTRACT_ROWS
                ).astype(BF16)

        fill(splits[2 * left + 1], core_send)
        flip(chunk).start()
        fill(splits[2 * left], kept)

    def sent_blocks(chunk, stage):
        order = orders[chunk % 2]
        gone = sum(1 << (bit - 1) for bit in order[:stage])
        return [i for i in range(blocks) if not i & gone and i >> (order[stage] - 1) & 1]

    def total_of(chunk, block, stage):
        value = kept[chunk, block].astype(F32) + core_got[chunk, block].astype(F32)
        for before in range(stage):
            bit = 1 << (orders[chunk % 2][before] - 1)
            at = sent_blocks(chunk, before).index(block ^ bit)
            value = value + gots[before][chunk, at].astype(F32)
        return value

    def transfer(chunk, stage):
        return pltpu.make_async_remote_copy(
            src_ref=sends[stage].at[chunk],
            dst_ref=gots[stage].at[chunk],
            send_sem=stage_sent.at[chunk, stage],
            recv_sem=stage_came.at[chunk, stage],
            device_id=near[orders[chunk % 2][stage]],
            device_id_type=MESH,
        )

    def come(chunk, stage):
        if stage == 0:
            flip(chunk).wait_recv()
        else:
            transfer(chunk, stage - 1).wait_recv()

    def advance(chunk, stage):
        come(chunk, stage)
        for at, block in enumerate(sent_blocks(chunk, stage)):
            sends[stage][chunk, at] = total_of(chunk, block, stage).astype(BF16)
        transfer(chunk, stage).start()

    for chunk in range(chunks):
        products(chunk)
        if chunk:
            advance(chunk - 1, 0)
    advance(chunks - 1, 0)
    for job, out_ref in zip(jobs, made):
        job(*given[: job.inputs], out_ref)
        given = given[job.inputs :]
    for stage in range(1, stages):
        for chunk in range(chunks):
            advance(chunk, stage)
    for chunk in range(chunks):
        come(chunk, stages)
        total_ref[:, chunk * width : (chunk + 1) * width] = total_of(chunk, 0, stages).astype(BF16)
    for chunk in range(chunks):
        flip(chunk).wait_send()
        for stage in range(stages):
            transfer(chunk, stage).wait_send()
    for copy in copies:
        copy.wait()


def exchange_and_scatter(values, products, collective_id, jobs=()):
    groups, count = lax.axis_size("grp"), lax.axis_size("ep")
    bits = groups.bit_length() - 1
    exchanged = len(values)
    columns = 1024
    splits, rights, sources = [], [], []
    for split, right in products:
        if not splits or splits[-1] is not split:
            splits.append(split)
        for at in range(right.shape[1] // columns):
            sources.append((len(splits) - 1, len(rights), at))
        rights.append(right)
    chunks, blocks = len(sources), groups // 2
    own_rows = splits[0][0].shape[1] // blocks
    block = (own_rows, columns)
    buffer = pltpu.VMEM((chunks, blocks, *block), BF16)
    stages = [pltpu.VMEM((chunks, blocks >> (at + 1), *block), BF16) for at in range(bits - 1)]
    vmem = pl.BlockSpec(memory_space=pltpu.VMEM)
    anywhere = pl.BlockSpec(memory_space=pl.ANY)
    arrays = [array for _, inputs, _ in jobs for array in inputs]
    given = [array.reshape(count, -1, array.shape[1]) for array, _ in values]
    back_shape = [
        jax.ShapeDtypeStruct((*array.shape[:2], width), BF16)
        for array, (_, width) in zip(given, values)
    ]
    outs = pl.pallas_call(
        functools.partial(
            exchange_scatter_kernel,
            bits,
            count,
            len(splits),
            sources,
            [job for job, _, _ in jobs],
            exchanged,
        ),
        in_specs=[anywhere] * exchanged
        + [vmem] * (2 * len(splits) + len(rights))
        + [anywhere] * len(arrays),
        out_specs=[anywhere] * exchanged + [vmem] + [anywhere] * len(jobs),
        out_shape=[
            *back_shape,
            jax.ShapeDtypeStruct((own_rows, chunks * columns), BF16),
            *[out for _, _, out in jobs],
        ],
        scratch_shapes=[
            buffer,
            buffer,
            buffer,
            *stages,
            *stages,
            pltpu.SemaphoreType.DMA((max(exchanged, 1),)),
            *[pltpu.SemaphoreType.DMA((max(exchanged, 1), count - 1))] * 2,
            *[pltpu.SemaphoreType.DMA((chunks,))] * 2,
            *[pltpu.SemaphoreType.DMA((chunks, bits - 1))] * 2,
        ],
        compiler_params=pltpu.CompilerParams(
            collective_id=collective_id, has_side_effects=True, vmem_limit_bytes=60 * 2**20
        ),
        cost_estimate=NO_COST,
        name="exchange_and_scatter" if exchanged else "scatter",
    )(
        *given,
        *[half for split in splits for half in split],
        *rights,
        *arrays,
    )
    backs = [out.reshape(-1, out.shape[2]) for out in outs[:exchanged]]
    return backs, outs[exchanged], outs[exchanged + 1 :]


def after(values, *tokens):
    return lax.optimization_barrier((values, *tokens))[0]


def flip(values, bit):
    size = lax.axis_size("grp")
    return lax.ppermute(values, "grp", [(i, i ^ (1 << bit)) for i in range(size)])


def gather_gains(gains):
    size = lax.axis_size("grp")
    me = lax.axis_index("grp")
    for bit in range(size.bit_length() - 1):
        other = flip(gains, bit)
        upper = (me >> bit) & 1
        gains = jnp.where(
            upper == 0,
            jnp.concatenate([gains, other], axis=1),
            jnp.concatenate([other, gains], axis=1),
        )
    return gains


class Scatter:
    def __init__(self, terms, order):
        self.terms = terms
        self.order = list(order)

    def step(self, *tokens):
        if self.order:
            self.prepare(*tokens)
            self.receive(flip(self.sent, self.bit))

    def prepare(self, *tokens):
        self.bit = bit = self.order.pop(0)
        axis = sum(other > bit for other in self.order)
        mine = (lax.axis_index("grp") >> bit) & 1
        terms = self.terms
        if tokens:
            terms = [after(term, *tokens) for term in terms]

        def part(term, which):
            return lax.dynamic_index_in_dim(term, which, axis, keepdims=False)

        self.sent = sum(part(term, 1 - mine).astype(F32) for term in terms).astype(BF16)
        self.kept = sum(part(term, mine).astype(F32) for term in terms).astype(BF16)

    def receive(self, got):
        self.terms = [self.kept, got]

    def finish(self):
        while self.order:
            self.step()
        return sum(term.astype(F32) for term in self.terms)


def core_split(values, groups):
    rows, columns = values.shape
    n = columns // groups
    mine = lax.axis_index("grp") & 1
    even = jnp.concatenate([values[:, i * n : (i + 1) * n] for i in range(0, groups, 2)], axis=1)
    odd = jnp.concatenate([values[:, i * n : (i + 1) * n] for i in range(1, groups, 2)], axis=1)
    return jnp.where(mine == 0, even, odd), jnp.where(mine == 0, odd, even)


def scatter_product(split, rights, groups, first=0):
    bits = groups.bit_length() - 1
    results = []
    for place, right in enumerate(rights):
        order = list(range(1, bits))
        if (place + first) % 2:
            order = order[::-1]
        sent = dot(split[1], right, CONTRACT_ROWS).astype(BF16)
        got = flip(sent, 0)
        kept = dot(split[0], right, CONTRACT_ROWS).astype(BF16)
        shape = (2,) * (bits - 1) + (-1, right.shape[1])
        results.append(Scatter([kept.reshape(shape), got.reshape(shape)], order))
        results[-1].sent = sent
    return results


def steps(scatters, *tokens):
    for scatter in scatters:
        scatter.step(*tokens)


def finish(scatters):
    return jnp.concatenate([scatter.finish() for scatter in scatters], axis=1)


def halves(values):
    middle = values.shape[1] // 2
    return values[:, :middle], values[:, middle:]


def exchange(values, experts):
    rows, width = values.shape
    return lax.all_to_all(
        values.reshape(experts, rows // experts, width),
        "ep",
        split_axis=0,
        concat_axis=0,
        tiled=True,
    ).reshape(rows, width)


def local(
    layer_input,
    kv_weight,
    norm_gains,
    query_maps,
    output_maps,
    gate_up_maps,
    down_maps,
    att_routes,
    att_gates,
    mlp_routes,
    mlp_gates,
    segments,
    cotangent,
):
    experts = lax.axis_size("ep")
    groups = lax.axis_size("grp")
    bits = groups.bit_length() - 1
    me_index = lax.axis_index("ep")
    tok_dev = layer_input.shape[0]
    model_width = layer_input.shape[1]
    capacity = 3 * tok_dev // experts
    rows_total = experts * capacity
    hidden = gate_up_maps.shape[2] // 2

    def gather(shard):
        return lax.all_gather(shard, "grp", axis=0, tiled=True)

    gains_full = gather_gains(norm_gains.astype(BF16))
    gain_one = gains_full[0].astype(F32)
    gain_two = gains_full[1].astype(F32)
    xfloat = layer_input.astype(F32)
    inverse_one, unit_one = normalize(xfloat)
    normed_one = (unit_one * gain_one).astype(BF16)

    kv_heads = kv_weight.reshape(2, HEADS, HEAD_DIM, -1).transpose(1, 0, 2, 3)
    kv_shard = kv_heads.reshape(kv_weight.shape).T.astype(BF16)
    cuts = []
    for count in (4, 2, 2, hidden // TILE - 8):
        cuts.append((sum(size for _, size in cuts), count * TILE))

    def gather(shard):
        return lax.all_gather(shard, "grp", axis=0, tiled=True)

    output_shard = output_maps[0].astype(BF16)
    kv_full = gather(kv_shard)
    output_full = gather(output_shard)
    normed_all, query_full, gate_up_low, down_low = opening(
        after(normed_one, output_shard),
        query_maps[0].astype(BF16),
        gate_up_maps[0],
        down_maps[0],
        cuts,
    )
    down_full = gather(down_low)
    gate_up_full = [gather(gate_up_low[0]), None, None, gather(gate_up_low[3])]

    att_named, att_place = expert_places(att_routes[0].reshape(experts, tok_dev, TOP), experts)
    mlp_named, mlp_place = expert_places(mlp_routes[0].reshape(experts, tok_dev, TOP), experts)

    def mine(values, axis):
        return lax.dynamic_index_in_dim(values, me_index, axis, keepdims=False)

    att_pick = one_hot(mine(att_named, 1), mine(att_place, 1), capacity)
    att_send = one_hot(mine(att_named, 0), mine(att_place, 0), capacity).reshape(
        rows_total, tok_dev
    )
    mlp_send = one_hot(mine(mlp_named, 0), mine(mlp_place, 0), capacity).reshape(
        rows_total, tok_dev
    )

    def gates_at(send, routes, gates):
        ids = jnp.arange(experts, dtype=jnp.int32)
        routes = mine(routes.reshape(experts, tok_dev, TOP), 0)
        per_expert = jnp.sum(jnp.where(routes[None] == ids[:, None, None], gates[None], 0.0), axis=2)
        spread = jnp.where(
            send.reshape(experts, capacity, tok_dev), per_expert[:, None, :], 0.0
        ).reshape(rows_total, tok_dev)
        return high_low(spread)

    att_high, att_low = gates_at(att_send, att_routes, att_gates)
    mlp_high, mlp_low = gates_at(mlp_send, mlp_routes, mlp_gates)
    mlp_send = mlp_send.astype(BF16)
    places = jnp.arange(experts * tok_dev, dtype=jnp.int32).reshape(experts, 1, tok_dev)
    starts = segments[0].reshape(experts, 1, tok_dev)
    bounds = jnp.stack(
        [
            jnp.sum(jnp.where(att_pick, starts, 0), axis=2).reshape(-1),
            jnp.sum(jnp.where(att_pick, places, 0), axis=2).reshape(-1),
        ],
        axis=1,
    )
    att_pick = att_pick.astype(BF16)

    cotangent_send = (dot(mlp_high, cotangent) + dot(mlp_low, cotangent)).astype(BF16)
    cotangent_send = after(cotangent_send, normed_all)
    grad_mlp_rows = exchange(cotangent_send, experts)
    att_in = (
        jnp.einsum(
            "sct,std->scd", att_pick, after(normed_all, cotangent_send), preferred_element_type=F32
        )
        .astype(BF16)
        .reshape(rows_total, model_width)
    )
    normed_all = normed_all.reshape(experts * tok_dev, model_width)
    queries = dot(att_in, query_full).astype(BF16)
    keys_values = dot(after(normed_all, queries), kv_full).astype(BF16)
    att_heads, logsums = attend_forward(queries, keys_values, bounds, experts)
    att_rows = dot(after(att_heads, grad_mlp_rows), output_full).astype(BF16)
    att_back, gate_up_full[1] = exchange_and_gather(att_rows, gate_up_low[1], 1)
    residual_one = (
        xfloat + dot(att_high, att_back, CONTRACT_ROWS) + dot(att_low, att_back, CONTRACT_ROWS)
    )

    inverse_two, unit_two = normalize(residual_one)
    normed_two = (unit_two * gain_two).astype(BF16)
    mlp_given = dot(mlp_send, normed_two).astype(BF16)
    mlp_in, gate_up_full[2] = exchange_and_gather(mlp_given, gate_up_low[2], 2)
    mlp_split = core_split(mlp_in, groups)
    acts = [None]
    grads = [None] * len(cuts)

    def feed_chunk(index, feed_in, total):
        gate_up = gate_up_full[index]
        acts[0], grads[index] = feed(
            feed_in, grad_mlp_rows, gate_up, down_full, cuts[index][0], acts[0]
        )
        if index == 0:
            steps(middle_scatter, grads[0])
            ready = [array for scatter in middle_scatter for array in (scatter.sent, scatter.kept)]
            grads[0] = after(grads[0], *ready)
        return back(grads[index], gate_up, total, BF16 if index == 3 else F32)

    normed_split = core_split(normed_all, groups)
    att_split = core_split(att_in, groups)
    heads_split = core_split(att_heads, groups)
    grad_mlp_in = feed_chunk(
        1, after(mlp_in, *mlp_split, *normed_split, *att_split, *heads_split), None
    )
    grad_mlp_in = feed_chunk(2, after(mlp_in, grad_mlp_in), grad_mlp_in)
    middle_scatter = scatter_product(mlp_split, [after(grads[1], grad_mlp_in), grads[2]], groups)
    ready = [array for scatter in middle_scatter for array in (scatter.terms[0], scatter.sent)]
    grad_mlp_in = feed_chunk(0, after(mlp_in, *ready), grad_mlp_in)
    first_grad = weight_product(mlp_in, after(grads[0], grad_mlp_in))
    first_grad_sum = lax.psum_scatter(first_grad, "grp", scatter_dimension=0, tiled=True)
    grad_mlp_in = feed_chunk(3, after(mlp_in, first_grad), grad_mlp_in)
    activated = acts[0]
    for scatter in middle_scatter:
        scatter.prepare(grad_mlp_in)
    mlp_returned, (down_grad, last_grad) = exchange_and_multiply(
        grad_mlp_in,
        [(multiply_columns, activated, grad_mlp_rows), (multiply_columns, mlp_in, grads[3])],
        middle_scatter,
        3,
    )
    down_grad_sum = lax.psum_scatter(down_grad, "grp", scatter_dimension=0, tiled=True)
    last_grad_sum = lax.psum_scatter(
        after(last_grad, down_grad), "grp", scatter_dimension=0, tiled=True
    )

    grad_final = cotangent.astype(F32)
    grad_normed_two = dot(mlp_send, mlp_returned, CONTRACT_ROWS)
    grad_inner_two, grad_gain_two = norm_backward(grad_normed_two, unit_two, inverse_two, gain_two)
    grad_residual = grad_final + grad_inner_two

    res_high, res_low = high_low(grad_residual)
    sent_four = (
        dot(att_high, res_high) + dot(att_low, res_high) + dot(att_high, res_low)
    ).astype(BF16)
    grad_att_rows, (mlp_rows,) = exchange_and_multiply(
        sent_four, [(multiply_rows, activated, down_full)], [], 4
    )
    grad_heads = dot(grad_att_rows, output_full, CONTRACT_COLUMNS).astype(BF16)
    grad_queries, grad_kv, mlp_first = attend_backward(
        queries, keys_values, grad_heads, bounds, logsums, mlp_rows, experts, 7
    )
    grad_att_in = dot(grad_queries, query_full, CONTRACT_COLUMNS).astype(BF16)
    grad_all = (
        jnp.einsum(
            "sct,scd->std",
            att_pick,
            grad_att_in.reshape(experts, capacity, model_width),
            preferred_element_type=F32,
        ).reshape(experts * tok_dev, model_width)
        + dot(grad_kv, kv_full, CONTRACT_COLUMNS)
    ).astype(BF16)
    grad_all = after(grad_all, first_grad_sum, down_grad_sum)
    (grad_back, mlp_second), kv_part, _ = exchange_and_scatter(
        [(grad_all, model_width), (mlp_rows, model_width // 2)], [(normed_split, grad_kv)], 5
    )
    kv_grad = lax.psum(kv_part, "ep")
    while middle_scatter[0].order:
        steps(middle_scatter)
    middle_terms = [[after(term, kv_part) for term in scatter.terms] for scatter in middle_scatter]
    _, both_maps, _ = exchange_and_scatter(
        [],
        [
            (att_split, after(grad_queries, kv_part, last_grad_sum)),
            (heads_split, grad_att_rows),
        ],
        6,
    )
    kv_grad = after(kv_grad, both_maps)
    chunks = [[first_grad_sum], *middle_terms, [last_grad_sum]]
    gate_up_grad = assemble([[after(term, kv_grad) for term in terms] for terms in chunks])[None]
    down_grad = after(down_grad_sum, kv_grad).astype(F32)[None]
    query_grad, output_grad = [part.astype(F32)[None] for part in halves(both_maps)]
    mlp_back = jnp.concatenate([after(mlp_first, kv_grad), mlp_second], axis=1)
    output = (
        residual_one + dot(mlp_high, mlp_back, CONTRACT_ROWS) + dot(mlp_low, mlp_back, CONTRACT_ROWS)
    ).astype(BF16)
    grad_normed_one = jnp.sum(
        after(grad_back, kv_grad).reshape(experts, tok_dev, model_width).astype(F32), axis=0
    )
    kv_grad = transpose(kv_grad)
    grad_inner_one, grad_gain_one = norm_backward(grad_normed_one, unit_one, inverse_one, gain_one)
    grad_input = grad_residual + grad_inner_one

    gains_grad = jnp.stack([grad_gain_one, grad_gain_two])
    gains_grad = gains_grad.reshape((2,) + (2,) * bits + (-1,))
    beside = [kv_grad, gate_up_grad, down_grad]
    for bit in reversed(range(bits)):
        mine_bit = (lax.axis_index("grp") >> bit) & 1
        kept = lax.dynamic_index_in_dim(gains_grad, mine_bit, 1, keepdims=False)
        sent = lax.dynamic_index_in_dim(gains_grad, 1 - mine_bit, 1, keepdims=False)
        gains_grad = kept + lax.ppermute(
            sent, "grp", [(i, i ^ (1 << bit)) for i in range(groups)]
        )
        if beside:
            gains_grad = after(gains_grad, beside.pop(0))
    for bit in range(experts.bit_length() - 1):
        gains_grad = gains_grad + lax.ppermute(
            gains_grad, "ep", [(i, i ^ (1 << bit)) for i in range(experts)]
        )
    return (
        output,
        grad_input,
        kv_grad,
        gains_grad,
        query_grad,
        output_grad,
        gate_up_grad,
        down_grad,
    )


def solution(mesh):
    placed = (
        P(("grp", "ep"), None),
        P(None, "grp"),
        P(None, "grp"),
        P("ep", "grp", None),
        P("ep", "grp", None),
        P("ep", "grp", None),
        P("ep", "grp", None),
        P("grp", None, None),
        P(("grp", "ep"), None),
        P("grp", None, None),
        P(("grp", "ep"), None),
        P("grp", None),
        P(("grp", "ep"), None),
    )
    return jax.shard_map(
        local,
        mesh=mesh,
        in_specs=placed,
        out_specs=(
            P(("grp", "ep"), None),
            P(("grp", "ep"), None),
            P(None, "grp"),
            P(None, "grp"),
            P("ep", "grp", None),
            P("ep", "grp", None),
            P("ep", "grp", None),
            P("ep", "grp", None),
        ),
        check_vma=False,
    )
```

```python
import functools

import jax
import jax.numpy as jnp
from jax import lax
from jax.experimental import pallas as pl
from jax.experimental.pallas import tpu as pltpu
from jax.sharding import PartitionSpec as P

HEADS = 16
HEAD_DIM = 128
TOP = 2


EPSILON = 1e-06
NEGATIVE = -1e30
LOG2_E = 1.4426950408889634
CONTRACT_ROWS = (((0,), (0,)), ((), ()))
CONTRACT_COLUMNS = (((1,), (1,)), ((), ()))
BF16 = jnp.bfloat16
F32 = jnp.float32
VMEM_BYTES = 56 * 2**20
TILE = 512
NO_COST = pl.CostEstimate(flops=0, bytes_accessed=0, transcendentals=0)


def normalize(values):
    inverse = lax.rsqrt(jnp.mean(values * values, axis=-1, keepdims=True) + EPSILON)
    return (inverse, values * inverse)


def norm_backward(grad_normed, unit, inverse, gain):
    grad_unit = grad_normed * gain
    inner = jnp.mean(grad_unit * unit, axis=-1, keepdims=True)
    return (inverse * (grad_unit - unit * inner), jnp.sum(grad_normed * unit, axis=0))


def dot(left, right, dims=(((1,), (0,)), ((), ()))):
    return lax.dot_general(left, right, dims, preferred_element_type=F32)


def high_low(values):
    high = values.astype(BF16)
    return high, (values - high.astype(F32)).astype(BF16)


def expert_places(routes, experts):
    tokens = routes.shape[1]
    ids = jnp.arange(experts, dtype=jnp.int32)
    named = jnp.any(routes[:, None, :, :] == ids[None, :, None, None], axis=3)
    before = (jnp.arange(tokens)[:, None] < jnp.arange(tokens)[None, :]).astype(BF16)
    place = lax.dot_general(
        named.astype(BF16), before, (((2,), (0,)), ((), ())), preferred_element_type=F32
    )
    return named, place.astype(jnp.int32)


def one_hot(named, place, capacity):
    rows = jnp.arange(capacity, dtype=jnp.int32)[:, None]
    return named[..., None, :] & (place[..., None, :] == rows)


def attend_forward_kernel(sources, query_ref, key_ref, value_ref, bounds_ref, out_ref, logsum_ref):
    head = pl.program_id(0)
    capacity = query_ref.shape[0] // sources
    tokens = key_ref.shape[0] // sources
    scaling = HEAD_DIM ** (-0.5) * LOG2_E

    @pl.when(head == 0)
    def _():
        logsum_ref[...] = jnp.zeros_like(logsum_ref)

    for source in range(sources):
        rows = slice(source * capacity, (source + 1) * capacity)
        span = (source + 1) * tokens
        first = bounds_ref[rows, 0:1]
        last = bounds_ref[rows, 1:2]
        scores = dot(query_ref[rows, :], key_ref[:span, :], CONTRACT_COLUMNS) * scaling
        places = lax.broadcasted_iota(jnp.int32, scores.shape, 1)
        scores = jnp.where((places >= first) & (places <= last), scores, NEGATIVE)
        peak = jnp.max(scores, axis=1, keepdims=True)
        exponent = jnp.exp2(scores - peak)
        total = jnp.sum(exponent, axis=1, keepdims=True)
        mixed = dot(exponent.astype(BF16), value_ref[:span, :])
        out_ref[rows, :] = (mixed * (1.0 / total)).astype(BF16)
        lanes = lax.broadcasted_iota(jnp.int32, (capacity, 128), 1)
        logsum_ref[rows, :] = jnp.where(lanes == head, peak + jnp.log2(total), logsum_ref[rows, :])


def attend_forward(queries, keys_values, bounds, sources):
    rows, features = queries.shape
    seq = keys_values.shape[0]
    return pl.pallas_call(
        functools.partial(attend_forward_kernel, sources),
        grid=(HEADS,),
        in_specs=[
            pl.BlockSpec((rows, HEAD_DIM), lambda h: (0, h)),
            pl.BlockSpec((seq, HEAD_DIM), lambda h: (0, 2 * h)),
            pl.BlockSpec((seq, HEAD_DIM), lambda h: (0, 2 * h + 1)),
            pl.BlockSpec((rows, 2), lambda h: (0, 0)),
        ],
        out_specs=[
            pl.BlockSpec((rows, HEAD_DIM), lambda h: (0, h)),
            pl.BlockSpec((rows, 128), lambda h: (0, 0)),
        ],
        out_shape=[
            jax.ShapeDtypeStruct((rows, features), BF16),
            jax.ShapeDtypeStruct((rows, 128), F32),
        ],
        compiler_params=pltpu.CompilerParams(vmem_limit_bytes=VMEM_BYTES),
        cost_estimate=NO_COST,
        name="attend_forward",
    )(queries, keys_values, keys_values, bounds)


def attend_backward_kernel(
    sources,
    query_ref,
    key_ref,
    value_ref,
    grad_ref,
    bounds_ref,
    logsum_ref,
    values_ref,
    grad_query_ref,
    grad_both_ref,
    back_ref,
    key_total,
    value_total,
    local,
    sent,
    got,
):
    head = pl.program_id(0)
    me = lax.axis_index("grp")
    place = lax.axis_index("ep")
    others = [lax.rem(place + shift, sources) for shift in range(1, sources)]
    columns = pl.ds(0, back_ref.shape[2])
    copies = [
        pltpu.make_async_remote_copy(
            src_ref=values_ref.at[other, :, columns],
            dst_ref=back_ref.at[place],
            send_sem=sent.at[index],
            recv_sem=got.at[index],
            device_id=(me, other),
            device_id_type=MESH,
        )
        for index, other in enumerate(others)
    ]
    copies.append(
        pltpu.make_async_copy(values_ref.at[place, :, columns], back_ref.at[place], local)
    )

    @pl.when(head == 0)
    def _():
        pl.semaphore_wait(greet([(me, other) for other in others]), len(others))
        for copy in copies:
            copy.start()

    capacity = query_ref.shape[0] // sources
    tokens = key_ref.shape[0] // sources
    scaling = HEAD_DIM ** (-0.5)
    for source in reversed(range(sources)):
        rows = slice(source * capacity, (source + 1) * capacity)
        span = (source + 1) * tokens
        first = bounds_ref[rows, 0:1]
        last = bounds_ref[rows, 1:2]
        query = query_ref[rows, :]
        grad = grad_ref[rows, :]
        lanes = lax.broadcasted_iota(jnp.int32, (capacity, 128), 1)
        logsum = jnp.sum(
            jnp.where(lanes == head, logsum_ref[rows, :], 0.0), axis=1, keepdims=True
        )
        scores = dot(query, key_ref[:span, :], CONTRACT_COLUMNS) * (scaling * LOG2_E)
        places = lax.broadcasted_iota(jnp.int32, scores.shape, 1)
        scores = jnp.where((places >= first) & (places <= last), scores, NEGATIVE)
        probs = jnp.exp2(scores - logsum)
        grad_probs = dot(grad, value_ref[:span, :], CONTRACT_COLUMNS)
        weighted = probs * grad_probs
        correction = jnp.sum(weighted, axis=1, keepdims=True)
        grad_scores = (weighted - probs * correction).astype(BF16)
        grad_query_ref[rows, :] = (dot(grad_scores, key_ref[:span, :]) * scaling).astype(BF16)
        key_part = dot(grad_scores, query, CONTRACT_ROWS)
        value_part = dot(probs.astype(BF16), grad, CONTRACT_ROWS)
        if source == sources - 1:
            key_total[...] = key_part
            value_total[...] = value_part
        else:
            key_total[:span, :] += key_part
            value_total[:span, :] += value_part
    grad_both_ref[:, :HEAD_DIM] = (key_total[...] * scaling).astype(BF16)
    grad_both_ref[:, HEAD_DIM:] = value_total[...].astype(BF16)

    @pl.when(head == HEADS - 1)
    def _():
        for copy in copies:
            copy.wait()


def attend_backward(
    queries, keys_values, grads, bounds, logsums, values, sources, collective_id
):
    rows = queries.shape[0]
    features = HEADS * HEAD_DIM
    seq = keys_values.shape[0]
    shape = (sources, values.shape[0] // sources, values.shape[1])
    grad_queries, grad_both, back = pl.pallas_call(
        functools.partial(attend_backward_kernel, sources),
        grid=(HEADS,),
        in_specs=[
            pl.BlockSpec((rows, HEAD_DIM), lambda h: (0, h)),
            pl.BlockSpec((seq, HEAD_DIM), lambda h: (0, 2 * h)),
            pl.BlockSpec((seq, HEAD_DIM), lambda h: (0, 2 * h + 1)),
            pl.BlockSpec((rows, HEAD_DIM), lambda h: (0, h)),
            pl.BlockSpec((rows, 2), lambda h: (0, 0)),
            pl.BlockSpec((rows, 128), lambda h: (0, 0)),
            pl.BlockSpec(memory_space=pl.ANY),
        ],
        out_specs=[
            pl.BlockSpec((rows, HEAD_DIM), lambda h: (0, h)),
            pl.BlockSpec((seq, 2 * HEAD_DIM), lambda h: (0, h)),
            pl.BlockSpec(memory_space=pl.ANY),
        ],
        out_shape=[
            jax.ShapeDtypeStruct((rows, features), BF16),
            jax.ShapeDtypeStruct((seq, 2 * features), BF16),
            jax.ShapeDtypeStruct((*shape[:2], shape[2] // 2), BF16),
        ],
        scratch_shapes=[
            pltpu.VMEM((seq, HEAD_DIM), F32),
            pltpu.VMEM((seq, HEAD_DIM), F32),
            pltpu.SemaphoreType.DMA,
            *[pltpu.SemaphoreType.DMA((sources - 1,))] * 2,
        ],
        compiler_params=pltpu.CompilerParams(
            collective_id=collective_id, has_side_effects=True, vmem_limit_bytes=VMEM_BYTES
        ),
        cost_estimate=NO_COST,
        name="attend_backward",
    )(queries, keys_values, keys_values, grads, bounds, logsums, values.reshape(shape))
    return grad_queries, grad_both, back.reshape(values.shape[0], -1)


def feed_kernel(in_ref, grad_ref, gate_up_ref, down_ref, *refs):
    act_ref, grad_gate_up_ref = refs[-2:]
    units = down_ref.shape[0]
    step = units // 2
    for start in range(0, units, step):
        here = slice(start, start + step)
        there = slice(units + start, units + start + step)
        gate = dot(in_ref[...], gate_up_ref[:, here])
        up = dot(in_ref[...], gate_up_ref[:, there])
        grad_act = dot(grad_ref[...], down_ref[here, :], CONTRACT_COLUMNS)
        sigmoid = jax.nn.sigmoid(gate)
        silu = gate * sigmoid
        act_ref[:, here] = (silu * up).astype(BF16)
        grad_gate_up_ref[:, here] = (
            grad_act * up * sigmoid * (1.0 + gate * (1.0 - sigmoid))
        ).astype(BF16)
        grad_gate_up_ref[:, there] = (grad_act * silu).astype(BF16)


def feed(inputs, grads, gate_up, down, offset, acts=None):
    rows, width = inputs.shape
    units = gate_up.shape[1] // 2
    tiles = units // TILE
    start = offset // TILE
    before = [] if acts is None else [acts]
    return pl.pallas_call(
        feed_kernel,
        grid=(tiles,),
        in_specs=[
            pl.BlockSpec((rows, width), lambda j: (0, 0)),
            pl.BlockSpec((rows, width), lambda j: (0, 0)),
            pl.BlockSpec((width, 2 * TILE), lambda j: (0, j)),
            pl.BlockSpec((TILE, width), lambda j: (j + start, 0)),
        ]
        + [pl.BlockSpec(memory_space=pl.ANY)] * len(before),
        out_specs=[
            pl.BlockSpec((rows, TILE), lambda j: (0, j + start)),
            pl.BlockSpec((rows, 2 * TILE), lambda j: (0, j)),
        ],
        out_shape=[
            jax.ShapeDtypeStruct((rows, down.shape[0]), BF16),
            jax.ShapeDtypeStruct((rows, 2 * units), BF16),
        ],
        input_output_aliases={4: 0} if before else {},
        compiler_params=pltpu.CompilerParams(vmem_limit_bytes=VMEM_BYTES),
        cost_estimate=NO_COST,
        name="feed",
    )(inputs, grads, gate_up, down, *before)


def back_kernel(grad_ref, weight_ref, *refs):
    *before, out_ref = refs
    value = dot(grad_ref[...], weight_ref[...], CONTRACT_COLUMNS)
    for ref in before:
        value = value + ref[...]
    out_ref[...] = value.astype(out_ref.dtype)


def back(grads, weights, total, dtype):
    (rows, depth), columns = grads.shape, weights.shape[0]
    before = [] if total is None else [total]
    return pl.pallas_call(
        back_kernel,
        grid=(columns // TILE,),
        in_specs=[
            pl.BlockSpec((rows, depth), lambda j: (0, 0)),
            pl.BlockSpec((TILE, depth), lambda j: (j, 0)),
        ]
        + [pl.BlockSpec((rows, TILE), lambda j: (0, j))] * len(before),
        out_specs=pl.BlockSpec((rows, TILE), lambda j: (0, j)),
        out_shape=jax.ShapeDtypeStruct((rows, columns), dtype),
        compiler_params=pltpu.CompilerParams(vmem_limit_bytes=VMEM_BYTES),
        cost_estimate=NO_COST,
        name="back",
    )(grads, weights, *before)


def weight_kernel(left_ref, right_ref, out_ref):
    out_ref[...] = dot(left_ref[...], right_ref[...], CONTRACT_ROWS).astype(BF16)


def weight_product(left, right):
    (rows, columns), width = left.shape, right.shape[1]
    tile = TILE // 2
    return pl.pallas_call(
        weight_kernel,
        grid=(columns // tile,),
        in_specs=[
            pl.BlockSpec((rows, tile), lambda j: (0, j)),
            pl.BlockSpec((rows, width), lambda j: (0, 0)),
        ],
        out_specs=pl.BlockSpec((tile, width), lambda j: (j, 0)),
        out_shape=jax.ShapeDtypeStruct((columns, width), BF16),
        compiler_params=pltpu.CompilerParams(vmem_limit_bytes=VMEM_BYTES),
        cost_estimate=NO_COST,
        name="weight_product",
    )(left, right)


def assemble_kernel(counts, *refs):
    *refs, out_ref = refs
    hidden = out_ref.shape[1] // 2
    start = 0
    for count in counts:
        terms, refs = refs[:count], refs[count:]
        for tile in range(terms[0].shape[1] // (2 * TILE)):
            for half in range(2):
                there = half * hidden + start
                here = (2 * tile + half) * TILE
                out_ref[:, there : there + TILE] = sum(
                    term[:, here : here + TILE].astype(F32) for term in terms
                )
            start += TILE


def assemble(chunks):
    arrays = [term for terms in chunks for term in terms]
    rows = arrays[0].shape[0]
    step = 32
    columns = sum(terms[0].shape[1] for terms in chunks)
    return pl.pallas_call(
        functools.partial(assemble_kernel, [len(terms) for terms in chunks]),
        grid=(rows // step,),
        in_specs=[pl.BlockSpec((step, term.shape[1]), lambda i: (i, 0)) for term in arrays],
        out_specs=pl.BlockSpec((step, columns), lambda i: (i, 0)),
        out_shape=jax.ShapeDtypeStruct((rows, columns), F32),
        compiler_params=pltpu.CompilerParams(vmem_limit_bytes=VMEM_BYTES),
        cost_estimate=NO_COST,
        name="assemble",
    )(*arrays)


def transpose_kernel(steps, in_ref, out_ref):
    for value in range(2):

        @pl.when(pl.program_id(0) // steps == value)
        def _():
            for head in range(TILE // HEAD_DIM):
                columns = slice((2 * head + value) * HEAD_DIM, (2 * head + value + 1) * HEAD_DIM)
                rows = slice(head * HEAD_DIM, (head + 1) * HEAD_DIM)
                out_ref[rows, :] = in_ref[:, columns].astype(F32).T


def transpose(values):
    rows, columns = values.shape
    steps = columns // (2 * TILE)
    return pl.pallas_call(
        functools.partial(transpose_kernel, steps),
        grid=(2 * steps,),
        in_specs=[pl.BlockSpec((rows, 2 * TILE), lambda j: (0, j % steps))],
        out_specs=pl.BlockSpec((TILE, rows), lambda j: (j, 0)),
        out_shape=jax.ShapeDtypeStruct((columns, rows), F32),
        cost_estimate=NO_COST,
        name="transpose",
    )(values)


MESH = pl.DeviceIdType.MESH


def greet(devices, extra=0):
    barrier = pltpu.get_barrier_semaphore()
    for device in devices:
        pl.semaphore_signal(barrier, inc=1, device_id=device, device_id_type=MESH)
    return barrier


class WeightGather:
    def __init__(self, bits, shard_ref, full_ref, sent, got):
        self.me, self.place = lax.axis_index("grp"), lax.axis_index("ep")
        self.bits, self.rows = bits, shard_ref.shape[0] // 2
        self.shard_ref, self.full_ref, self.sent, self.got = shard_ref, full_ref, sent, got
        self.orders = list(range(1, bits)) + [0], list(range(1, bits))[::-1] + [0]
        self.moves = []
        for index in range(1, 1 << (bits - 1)):
            for part in range(2):
                order = self.orders[part]
                far = sum(1 << bit for at, bit in enumerate(order[:-1]) if index >> at & 1)
                self.moves.append((part, far, order[index.bit_length() :]))

    def neighbours(self):
        return [(self.me ^ (1 << bit), self.place) for bit in range(self.bits)]

    def piece(self, part, far, bit):
        here = pl.ds(part * self.rows, self.rows)
        block = self.full_ref.at[self.me ^ far, here]
        return pltpu.make_async_remote_copy(
            src_ref=self.shard_ref.at[here] if far == 0 else block,
            dst_ref=block,
            send_sem=self.sent.at[part, far, bit],
            recv_sem=self.got.at[part, far ^ (1 << bit)],
            device_id=(self.me ^ (1 << bit), self.place),
            device_id_type=MESH,
        )

    def wait_piece(self, part, far):
        block = self.full_ref.at[self.me ^ far, pl.ds(part * self.rows, self.rows)]
        pltpu.make_async_remote_copy(
            src_ref=block,
            dst_ref=block,
            send_sem=self.sent.at[part, far, 0],
            recv_sem=self.got.at[part, far],
            device_id=(self.me ^ 1, self.place),
            device_id_type=MESH,
        ).wait_recv()

    def first(self):
        for part in range(2):
            for bit in self.orders[part]:
                self.piece(part, 0, bit).start()

    def forward(self, part, far, later):
        self.wait_piece(part, far)
        for bit in later:
            self.piece(part, far, bit).start()

    def finish(self):
        for part in range(2):
            for far in range(1 << (self.bits - 1)):
                self.wait_piece(part, 2 * far + 1)
        for part in range(2):
            for bit in self.orders[part]:
                self.piece(part, 0, bit).wait_send()
        for part, far, later in self.moves:
            for bit in later:
                self.piece(part, far, bit).wait_send()


def weight_gather_semaphores(groups):
    bits = groups.bit_length() - 1
    return [pltpu.SemaphoreType.DMA((2, groups, bits)), pltpu.SemaphoreType.DMA((2, groups))]


def opening_kernel(bits, count, chunks, *refs):
    (tokens_ref, shard_ref, gate_up_ref, down_ref, all_ref, full_ref), refs = refs[:6], refs[6:]
    low_refs, refs = refs[:chunks], refs[chunks:]
    down_low_ref, local, up_send, up_got, down_send, down_got, sent, got = refs
    me = lax.axis_index("grp")
    place = lax.axis_index("ep")
    weights = WeightGather(bits, shard_ref, full_ref, sent, got)

    barrier = greet(weights.neighbours())

    @pl.when(place > 0)
    def _():
        pl.semaphore_signal(barrier, inc=1, device_id=(me, place - 1), device_id_type=MESH)

    @pl.when(place < count - 1)
    def _():
        pl.semaphore_signal(barrier, inc=1, device_id=(me, place + 1), device_id_type=MESH)

    ends = jnp.where(place > 0, 1, 0) + jnp.where(place < count - 1, 1, 0)
    pl.semaphore_wait(barrier, bits + ends)

    def upward(hop):
        block = all_ref.at[jnp.maximum(place - hop, 0)]
        return pltpu.make_async_remote_copy(
            src_ref=tokens_ref if hop == 0 else block,
            dst_ref=block,
            send_sem=up_send.at[hop],
            recv_sem=up_got.at[hop],
            device_id=(me, jnp.minimum(place + 1, count - 1)),
            device_id_type=MESH,
        )

    def downward(hop):
        block = all_ref.at[jnp.minimum(place + hop, count - 1)]
        return pltpu.make_async_remote_copy(
            src_ref=tokens_ref if hop == 0 else block,
            dst_ref=block,
            send_sem=down_send.at[hop],
            recv_sem=down_got.at[hop],
            device_id=(me, jnp.maximum(place - 1, 0)),
            device_id_type=MESH,
        )

    def lines(hop, act):
        @pl.when((place + 1 < count) & (place - hop >= 0))
        def _():
            act(upward(hop))

        @pl.when((place - 1 >= 0) & (place + hop < count))
        def _():
            act(downward(hop))

    def line_got(hop):
        @pl.when(place - hop - 1 >= 0)
        def _():
            upward(hop).wait_recv()

        @pl.when(place + hop + 1 < count)
        def _():
            downward(hop).wait_recv()

    lines(0, lambda copy: copy.start())
    weights.first()
    own = [
        pltpu.make_async_copy(tokens_ref, all_ref.at[place], local.at[0]),
        pltpu.make_async_copy(shard_ref, full_ref.at[me], local.at[1]),
    ]
    for copy in own:
        copy.start()

    def round_block(in_ref, out_ref):
        out_ref[...] = in_ref[...].astype(BF16)

    shard_rows, columns = gate_up_ref.shape
    tiles = columns // (2 * TILE)
    start = 0
    for low_ref in low_refs:
        blocks = low_ref.shape[1] // TILE
        pltpu.emit_pipeline(
            round_block,
            grid=(blocks,),
            in_specs=[
                pl.BlockSpec(
                    (shard_rows, TILE), lambda j, start=start: (0, start + j // 2 + j % 2 * tiles)
                )
            ],
            out_specs=[pl.BlockSpec((shard_rows, TILE), lambda j: (0, j))],
        )(gate_up_ref, low_ref)
        start += blocks // 2
    down_rows, width = down_ref.shape
    step = 176
    pltpu.emit_pipeline(
        round_block,
        grid=(down_rows // step,),
        in_specs=[pl.BlockSpec((step, width), lambda j: (j, 0))],
        out_specs=[pl.BlockSpec((step, width), lambda j: (j, 0))],
    )(down_ref, down_low_ref)

    coming = list(weights.moves)
    hops = list(range(count - 1))
    while hops or coming:
        if hops:
            hop = hops.pop(0)
            line_got(hop)
            if hop + 1 < count - 1:
                lines(hop + 1, lambda copy: copy.start())
        for move in coming[:4]:
            weights.forward(*move)
        coming = coming[4:]
    weights.finish()
    for hop in range(count - 1):
        lines(hop, lambda copy: copy.wait_send())
    for copy in own:
        copy.wait()


def opening(tokens, shard, gate_up, down, cuts):
    groups, count = lax.axis_size("grp"), lax.axis_size("ep")
    bits = groups.bit_length() - 1
    whole, full, *lows = pl.pallas_call(
        functools.partial(opening_kernel, bits, count, len(cuts)),
        in_specs=[pl.BlockSpec(memory_space=pl.ANY)] * 4,
        out_specs=[pl.BlockSpec(memory_space=pl.ANY)] * (3 + len(cuts)),
        out_shape=[
            jax.ShapeDtypeStruct((count, *tokens.shape), BF16),
            jax.ShapeDtypeStruct((groups, *shard.shape), BF16),
            *[jax.ShapeDtypeStruct((gate_up.shape[0], 2 * size), BF16) for _, size in cuts],
            jax.ShapeDtypeStruct(down.shape, BF16),
        ],
        scratch_shapes=[
            pltpu.SemaphoreType.DMA((2,)),
            *[pltpu.SemaphoreType.DMA((count - 1,))] * 4,
            *weight_gather_semaphores(groups),
        ],
        compiler_params=pltpu.CompilerParams(
            collective_id=0, has_side_effects=True, vmem_limit_bytes=VMEM_BYTES
        ),
        cost_estimate=NO_COST,
        name="opening",
    )(tokens, shard, gate_up, down)
    return whole, full.reshape(-1, full.shape[2]), lows[:-1], lows[-1]


def exchange_kernel(
    bits, count, values_ref, shard_ref, back_ref, full_ref, local, out_sent, out_got, sent, got
):
    me = lax.axis_index("grp")
    place = lax.axis_index("ep")
    weights = WeightGather(bits, shard_ref, full_ref, sent, got)
    others = [lax.rem(place + shift, count) for shift in range(1, count)]
    barrier = greet(weights.neighbours() + [(me, other) for other in others])
    pl.semaphore_wait(barrier, bits + count - 1)
    copies = [
        pltpu.make_async_remote_copy(
            src_ref=values_ref.at[other],
            dst_ref=back_ref.at[place],
            send_sem=out_sent.at[index],
            recv_sem=out_got.at[index],
            device_id=(me, other),
            device_id_type=MESH,
        )
        for index, other in enumerate(others)
    ]
    own = [
        pltpu.make_async_copy(values_ref.at[place], back_ref.at[place], local.at[0]),
        pltpu.make_async_copy(shard_ref, full_ref.at[me], local.at[1]),
    ]
    for copy in copies:
        copy.start()
    weights.first()
    for copy in own:
        copy.start()
    for move in weights.moves:
        weights.forward(*move)
    weights.finish()
    for copy in copies:
        copy.wait()
    for copy in own:
        copy.wait()


def exchange_and_gather(values, shard, collective_id):
    groups, count = lax.axis_size("grp"), lax.axis_size("ep")
    bits = groups.bit_length() - 1
    rows, width = values.shape
    shape = (count, rows // count, width)
    back, full = pl.pallas_call(
        functools.partial(exchange_kernel, bits, count),
        in_specs=[pl.BlockSpec(memory_space=pl.ANY)] * 2,
        out_specs=[pl.BlockSpec(memory_space=pl.ANY)] * 2,
        out_shape=[
            jax.ShapeDtypeStruct(shape, BF16),
            jax.ShapeDtypeStruct((groups, *shard.shape), BF16),
        ],
        scratch_shapes=[
            pltpu.SemaphoreType.DMA((2,)),
            *[pltpu.SemaphoreType.DMA((count - 1,))] * 2,
            *weight_gather_semaphores(groups),
        ],
        compiler_params=pltpu.CompilerParams(collective_id=collective_id, has_side_effects=True),
        cost_estimate=NO_COST,
        name="exchange_and_gather",
    )(values.reshape(shape), shard)
    return back.reshape(rows, width), full.reshape(-1, full.shape[2])


def product_block(dims, left_ref, right_ref, out_ref):
    out_ref[...] = dot(left_ref[...], right_ref[...], dims).astype(BF16)


def multiply_rows(left_ref, right_ref, out_ref):
    (rows, depth), columns = left_ref.shape, right_ref.shape[1]
    tile = TILE // 2
    pltpu.emit_pipeline(
        functools.partial(product_block, (((1,), (0,)), ((), ()))),
        grid=(columns // tile,),
        in_specs=[
            pl.BlockSpec((rows, depth), lambda j: (0, 0)),
            pl.BlockSpec((depth, tile), lambda j: (0, j)),
        ],
        out_specs=[pl.BlockSpec((rows, tile), lambda j: (0, j))],
    )(left_ref, right_ref, out_ref)


def multiply_columns(left_ref, right_ref, out_ref):
    (rows, columns), width = left_ref.shape, right_ref.shape[1]
    tile = TILE // 2
    pltpu.emit_pipeline(
        functools.partial(product_block, CONTRACT_ROWS),
        grid=(columns // tile,),
        in_specs=[
            pl.BlockSpec((rows, tile), lambda j: (0, j)),
            pl.BlockSpec((rows, width), lambda j: (0, 0)),
        ],
        out_specs=[pl.BlockSpec((tile, width), lambda j: (j, 0))],
    )(left_ref, right_ref, out_ref)


def exchange_multiply_kernel(count, jobs, bits, *refs):
    values_ref, refs = refs[0], refs[1:]
    given, refs = refs[: 2 * len(jobs)], refs[2 * len(jobs) :]
    passed, refs = refs[: len(bits)], refs[len(bits) :]
    back_ref, refs = refs[0], refs[1:]
    made, refs = refs[: len(jobs)], refs[len(jobs) :]
    taken, refs = refs[: len(bits)], refs[len(bits) :]
    local, sent, got, pass_sent, pass_got = refs
    me = lax.axis_index("grp")
    place = lax.axis_index("ep")
    others = [lax.rem(place + shift, count) for shift in range(1, count)]
    across = [(me ^ (1 << bit), place) for bit in sorted(set(bits))]
    barrier = greet([(me, other) for other in others] + across)
    pl.semaphore_wait(barrier, len(others) + len(across))
    copies = [
        pltpu.make_async_remote_copy(
            src_ref=values_ref.at[other],
            dst_ref=back_ref.at[place],
            send_sem=sent.at[index],
            recv_sem=got.at[index],
            device_id=(me, other),
            device_id_type=MESH,
        )
        for index, other in enumerate(others)
    ]
    copies += [
        pltpu.make_async_remote_copy(
            src_ref=passed[index],
            dst_ref=taken[index],
            send_sem=pass_sent.at[index],
            recv_sem=pass_got.at[index],
            device_id=(me ^ (1 << bit), place),
            device_id_type=MESH,
        )
        for index, bit in enumerate(bits)
    ]
    copies.append(pltpu.make_async_copy(values_ref.at[place], back_ref.at[place], local))
    for copy in copies:
        copy.start()
    for index, job in enumerate(jobs):
        job(given[2 * index], given[2 * index + 1], made[index])
    for copy in copies:
        copy.wait()


def exchange_and_multiply(values, jobs, scatters, collective_id):
    count = lax.axis_size("ep")
    rows, width = values.shape
    shape = (count, rows // count, width)
    outs = []
    for job, left, right in jobs:
        by_rows = job is multiply_rows
        outs.append(
            jax.ShapeDtypeStruct((left.shape[0 if by_rows else 1], right.shape[1]), BF16)
        )
    passed = [scatter.sent for scatter in scatters]
    outs += [jax.ShapeDtypeStruct(array.shape, BF16) for array in passed]
    back, *made = pl.pallas_call(
        functools.partial(
            exchange_multiply_kernel,
            count,
            [job for job, _, _ in jobs],
            [scatter.bit for scatter in scatters],
        ),
        in_specs=[pl.BlockSpec(memory_space=pl.ANY)] * (1 + 2 * len(jobs) + len(passed)),
        out_specs=[pl.BlockSpec(memory_space=pl.ANY)] * (1 + len(outs)),
        out_shape=[jax.ShapeDtypeStruct(shape, BF16), *outs],
        scratch_shapes=[
            pltpu.SemaphoreType.DMA,
            *[pltpu.SemaphoreType.DMA((count - 1,))] * 2,
            *[pltpu.SemaphoreType.DMA((max(len(passed), 1),))] * 2,
        ],
        compiler_params=pltpu.CompilerParams(
            collective_id=collective_id, has_side_effects=True, vmem_limit_bytes=VMEM_BYTES
        ),
        cost_estimate=NO_COST,
        name="exchange_and_multiply",
    )(
        values.reshape(shape),
        *[array for _, left, right in jobs for array in (left, right)],
        *passed,
    )
    for scatter, got in zip(scatters, made[len(jobs) :]):
        scatter.receive(got)
    return back.reshape(rows, width), made[: len(jobs)]


def exchange_scatter_kernel(bits, count, lefts, sources, jobs, exchanged, *refs):
    values_refs, refs = refs[:exchanged], refs[exchanged:]
    splits, refs = refs[: 2 * lefts], refs[2 * lefts :]
    many = 1 + sources[-1][1]
    rights, refs = refs[:many], refs[many:]
    inputs = sum(job.inputs for job in jobs)
    given, refs = refs[:inputs], refs[inputs:]
    back_refs, refs = refs[:exchanged], refs[exchanged:]
    total_ref, *refs = refs
    made, refs = refs[: len(jobs)], refs[len(jobs) :]
    core_send, core_got, kept, *refs = refs
    stages = bits - 1
    sends, refs = refs[:stages], refs[stages:]
    gots, refs = refs[:stages], refs[stages:]
    local, out_sent, out_got, core_sent, core_came, stage_sent, stage_came = refs
    me = lax.axis_index("grp")
    place = lax.axis_index("ep")
    others = [lax.rem(place + shift, count) for shift in range(1, count)] if exchanged else []
    near = [(me ^ (1 << bit), place) for bit in range(bits)]
    barrier = greet(near + [(me, other) for other in others])
    pl.semaphore_wait(barrier, len(near) + len(others))
    copies = []
    for which, (values_ref, back_ref) in enumerate(zip(values_refs, back_refs)):
        width = back_ref.shape[2]
        columns = pl.ds(values_ref.shape[2] - width, width)
        copies += [
            pltpu.make_async_remote_copy(
                src_ref=values_ref.at[other, :, columns],
                dst_ref=back_ref.at[place],
                send_sem=out_sent.at[which, index],
                recv_sem=out_got.at[which, index],
                device_id=(me, other),
                device_id_type=MESH,
            )
            for index, other in enumerate(others)
        ]
        copies.append(
            pltpu.make_async_copy(
                values_ref.at[place, :, columns], back_ref.at[place], local.at[which]
            )
        )
    for copy in copies:
        copy.start()

    chunks, blocks, rows, width = kept.shape
    orders = list(range(1, bits)), list(range(1, bits))[::-1]

    def flip(chunk):
        return pltpu.make_async_remote_copy(
            src_ref=core_send.at[chunk],
            dst_ref=core_got.at[chunk],
            send_sem=core_sent.at[chunk],
            recv_sem=core_came.at[chunk],
            device_id=near[0],
            device_id_type=MESH,
        )

    def products(chunk):
        left, source, at = sources[chunk]
        columns = slice(at * width, (at + 1) * width)

        def fill(left_ref, into):
            @pl.loop(0, blocks)
            def _(block):
                offset = pl.multiple_of(((me ^ (2 * block)) // 2) * rows, rows)
                into[chunk, block] = dot(
                    left_ref[:, pl.ds(offset, rows)], rights[source][:, columns], CONTRACT_ROWS
                ).astype(BF16)

        fill(splits[2 * left + 1], core_send)
        flip(chunk).start()
        fill(splits[2 * left], kept)

    def sent_blocks(chunk, stage):
        order = orders[chunk % 2]
        gone = sum(1 << (bit - 1) for bit in order[:stage])
        return [i for i in range(blocks) if not i & gone and i >> (order[stage] - 1) & 1]

    def total_of(chunk, block, stage):
        value = kept[chunk, block].astype(F32) + core_got[chunk, block].astype(F32)
        for before in range(stage):
            bit = 1 << (orders[chunk % 2][before] - 1)
            at = sent_blocks(chunk, before).index(block ^ bit)
            value = value + gots[before][chunk, at].astype(F32)
        return value

    def transfer(chunk, stage):
        return pltpu.make_async_remote_copy(
            src_ref=sends[stage].at[chunk],
            dst_ref=gots[stage].at[chunk],
            send_sem=stage_sent.at[chunk, stage],
            recv_sem=stage_came.at[chunk, stage],
            device_id=near[orders[chunk % 2][stage]],
            device_id_type=MESH,
        )

    def come(chunk, stage):
        if stage == 0:
            flip(chunk).wait_recv()
        else:
            transfer(chunk, stage - 1).wait_recv()

    def advance(chunk, stage):
        come(chunk, stage)
        for at, block in enumerate(sent_blocks(chunk, stage)):
            sends[stage][chunk, at] = total_of(chunk, block, stage).astype(BF16)
        transfer(chunk, stage).start()

    for chunk in range(chunks):
        products(chunk)
        if chunk:
            advance(chunk - 1, 0)
    advance(chunks - 1, 0)
    for job, out_ref in zip(jobs, made):
        job(*given[: job.inputs], out_ref)
        given = given[job.inputs :]
    for stage in range(1, stages):
        for chunk in range(chunks):
            advance(chunk, stage)
    for chunk in range(chunks):
        come(chunk, stages)
        total_ref[:, chunk * width : (chunk + 1) * width] = total_of(chunk, 0, stages).astype(BF16)
    for chunk in range(chunks):
        flip(chunk).wait_send()
        for stage in range(stages):
            transfer(chunk, stage).wait_send()
    for copy in copies:
        copy.wait()


def exchange_and_scatter(values, products, collective_id, jobs=()):
    groups, count = lax.axis_size("grp"), lax.axis_size("ep")
    bits = groups.bit_length() - 1
    exchanged = len(values)
    columns = 1024
    splits, rights, sources = [], [], []
    for split, right in products:
        if not splits or splits[-1] is not split:
            splits.append(split)
        for at in range(right.shape[1] // columns):
            sources.append((len(splits) - 1, len(rights), at))
        rights.append(right)
    chunks, blocks = len(sources), groups // 2
    own_rows = splits[0][0].shape[1] // blocks
    block = (own_rows, columns)
    buffer = pltpu.VMEM((chunks, blocks, *block), BF16)
    stages = [pltpu.VMEM((chunks, blocks >> (at + 1), *block), BF16) for at in range(bits - 1)]
    vmem = pl.BlockSpec(memory_space=pltpu.VMEM)
    anywhere = pl.BlockSpec(memory_space=pl.ANY)
    arrays = [array for _, inputs, _ in jobs for array in inputs]
    given = [array.reshape(count, -1, array.shape[1]) for array, _ in values]
    back_shape = [
        jax.ShapeDtypeStruct((*array.shape[:2], width), BF16)
        for array, (_, width) in zip(given, values)
    ]
    outs = pl.pallas_call(
        functools.partial(
            exchange_scatter_kernel,
            bits,
            count,
            len(splits),
            sources,
            [job for job, _, _ in jobs],
            exchanged,
        ),
        in_specs=[anywhere] * exchanged
        + [vmem] * (2 * len(splits) + len(rights))
        + [anywhere] * len(arrays),
        out_specs=[anywhere] * exchanged + [vmem] + [anywhere] * len(jobs),
        out_shape=[
            *back_shape,
            jax.ShapeDtypeStruct((own_rows, chunks * columns), BF16),
            *[out for _, _, out in jobs],
        ],
        scratch_shapes=[
            buffer,
            buffer,
            buffer,
            *stages,
            *stages,
            pltpu.SemaphoreType.DMA((max(exchanged, 1),)),
            *[pltpu.SemaphoreType.DMA((max(exchanged, 1), count - 1))] * 2,
            *[pltpu.SemaphoreType.DMA((chunks,))] * 2,
            *[pltpu.SemaphoreType.DMA((chunks, bits - 1))] * 2,
        ],
        compiler_params=pltpu.CompilerParams(
            collective_id=collective_id, has_side_effects=True, vmem_limit_bytes=60 * 2**20
        ),
        cost_estimate=NO_COST,
        name="exchange_and_scatter" if exchanged else "scatter",
    )(
        *given,
        *[half for split in splits for half in split],
        *rights,
        *arrays,
    )
    backs = [out.reshape(-1, out.shape[2]) for out in outs[:exchanged]]
    return backs, outs[exchanged], outs[exchanged + 1 :]


def after(values, *tokens):
    return lax.optimization_barrier((values, *tokens))[0]


def flip(values, bit):
    size = lax.axis_size("grp")
    return lax.ppermute(values, "grp", [(i, i ^ (1 << bit)) for i in range(size)])


def gather_gains(gains):
    size = lax.axis_size("grp")
    me = lax.axis_index("grp")
    for bit in range(size.bit_length() - 1):
        other = flip(gains, bit)
        upper = (me >> bit) & 1
        gains = jnp.where(
            upper == 0,
            jnp.concatenate([gains, other], axis=1),
            jnp.concatenate([other, gains], axis=1),
        )
    return gains


class Scatter:
    def __init__(self, terms, order):
        self.terms = terms
        self.order = list(order)

    def step(self, *tokens):
        if self.order:
            self.prepare(*tokens)
            self.receive(flip(self.sent, self.bit))

    def prepare(self, *tokens):
        self.bit = bit = self.order.pop(0)
        axis = sum(other > bit for other in self.order)
        mine = (lax.axis_index("grp") >> bit) & 1
        terms = self.terms
        if tokens:
            terms = [after(term, *tokens) for term in terms]

        def part(term, which):
            return lax.dynamic_index_in_dim(term, which, axis, keepdims=False)

        self.sent = sum(part(term, 1 - mine).astype(F32) for term in terms).astype(BF16)
        self.kept = sum(part(term, mine).astype(F32) for term in terms).astype(BF16)

    def receive(self, got):
        self.terms = [self.kept, got]

    def finish(self):
        while self.order:
            self.step()
        return sum(term.astype(F32) for term in self.terms)


def core_split(values, groups):
    rows, columns = values.shape
    n = columns // groups
    mine = lax.axis_index("grp") & 1
    even = jnp.concatenate([values[:, i * n : (i + 1) * n] for i in range(0, groups, 2)], axis=1)
    odd = jnp.concatenate([values[:, i * n : (i + 1) * n] for i in range(1, groups, 2)], axis=1)
    return jnp.where(mine == 0, even, odd), jnp.where(mine == 0, odd, even)


def scatter_product(split, rights, groups, first=0):
    bits = groups.bit_length() - 1
    results = []
    for place, right in enumerate(rights):
        order = list(range(1, bits))
        if (place + first) % 2:
            order = order[::-1]
        sent = dot(split[1], right, CONTRACT_ROWS).astype(BF16)
        got = flip(sent, 0)
        kept = dot(split[0], right, CONTRACT_ROWS).astype(BF16)
        shape = (2,) * (bits - 1) + (-1, right.shape[1])
        results.append(Scatter([kept.reshape(shape), got.reshape(shape)], order))
        results[-1].sent = sent
    return results


def steps(scatters, *tokens):
    for scatter in scatters:
        scatter.step(*tokens)


def finish(scatters):
    return jnp.concatenate([scatter.finish() for scatter in scatters], axis=1)


def halves(values):
    middle = values.shape[1] // 2
    return values[:, :middle], values[:, middle:]


def exchange(values, experts):
    rows, width = values.shape
    return lax.all_to_all(
        values.reshape(experts, rows // experts, width),
        "ep",
        split_axis=0,
        concat_axis=0,
        tiled=True,
    ).reshape(rows, width)


def local(
    layer_input,
    kv_weight,
    norm_gains,
    query_maps,
    output_maps,
    gate_up_maps,
    down_maps,
    att_routes,
    att_gates,
    mlp_routes,
    mlp_gates,
    segments,
    cotangent,
):
    experts = lax.axis_size("ep")
    groups = lax.axis_size("grp")
    bits = groups.bit_length() - 1
    me_index = lax.axis_index("ep")
    tok_dev = layer_input.shape[0]
    model_width = layer_input.shape[1]
    capacity = 3 * tok_dev // experts
    rows_total = experts * capacity
    hidden = gate_up_maps.shape[2] // 2

    def gather(shard):
        return lax.all_gather(shard, "grp", axis=0, tiled=True)

    gains_full = gather_gains(norm_gains.astype(BF16))
    gain_one = gains_full[0].astype(F32)
    gain_two = gains_full[1].astype(F32)
    xfloat = layer_input.astype(F32)
    inverse_one, unit_one = normalize(xfloat)
    normed_one = (unit_one * gain_one).astype(BF16)

    kv_heads = kv_weight.reshape(2, HEADS, HEAD_DIM, -1).transpose(1, 0, 2, 3)
    kv_shard = kv_heads.reshape(kv_weight.shape).T.astype(BF16)
    cuts = []
    for count in (4, 2, 2, hidden // TILE - 8):
        cuts.append((sum(size for _, size in cuts), count * TILE))

    def gather(shard):
        return lax.all_gather(shard, "grp", axis=0, tiled=True)

    output_shard = output_maps[0].astype(BF16)
    kv_full = gather(kv_shard)
    output_full = gather(output_shard)
    normed_all, query_full, gate_up_low, down_low = opening(
        after(normed_one, output_shard),
        query_maps[0].astype(BF16),
        gate_up_maps[0],
        down_maps[0],
        cuts,
    )
    down_full = gather(down_low)
    gate_up_full = [gather(gate_up_low[0]), None, None, gather(gate_up_low[3])]

    att_named, att_place = expert_places(att_routes[0].reshape(experts, tok_dev, TOP), experts)
    mlp_named, mlp_place = expert_places(mlp_routes[0].reshape(experts, tok_dev, TOP), experts)

    def mine(values, axis):
        return lax.dynamic_index_in_dim(values, me_index, axis, keepdims=False)

    att_pick = one_hot(mine(att_named, 1), mine(att_place, 1), capacity)
    att_send = one_hot(mine(att_named, 0), mine(att_place, 0), capacity).reshape(
        rows_total, tok_dev
    )
    mlp_send = one_hot(mine(mlp_named, 0), mine(mlp_place, 0), capacity).reshape(
        rows_total, tok_dev
    )

    def gates_at(send, routes, gates):
        ids = jnp.arange(experts, dtype=jnp.int32)
        routes = mine(routes.reshape(experts, tok_dev, TOP), 0)
        per_expert = jnp.sum(jnp.where(routes[None] == ids[:, None, None], gates[None], 0.0), axis=2)
        spread = jnp.where(
            send.reshape(experts, capacity, tok_dev), per_expert[:, None, :], 0.0
        ).reshape(rows_total, tok_dev)
        return high_low(spread)

    att_high, att_low = gates_at(att_send, att_routes, att_gates)
    mlp_high, mlp_low = gates_at(mlp_send, mlp_routes, mlp_gates)
    mlp_send = mlp_send.astype(BF16)
    places = jnp.arange(experts * tok_dev, dtype=jnp.int32).reshape(experts, 1, tok_dev)
    starts = segments[0].reshape(experts, 1, tok_dev)
    bounds = jnp.stack(
        [
            jnp.sum(jnp.where(att_pick, starts, 0), axis=2).reshape(-1),
            jnp.sum(jnp.where(att_pick, places, 0), axis=2).reshape(-1),
        ],
        axis=1,
    )
    att_pick = att_pick.astype(BF16)

    cotangent_send = (dot(mlp_high, cotangent) + dot(mlp_low, cotangent)).astype(BF16)
    cotangent_send = after(cotangent_send, normed_all)
    grad_mlp_rows = exchange(cotangent_send, experts)
    att_in = (
        jnp.einsum(
            "sct,std->scd", att_pick, after(normed_all, cotangent_send), preferred_element_type=F32
        )
        .astype(BF16)
        .reshape(rows_total, model_width)
    )
    normed_all = normed_all.reshape(experts * tok_dev, model_width)
    queries = dot(att_in, query_full).astype(BF16)
    keys_values = dot(after(normed_all, queries), kv_full).astype(BF16)
    att_heads, logsums = attend_forward(queries, keys_values, bounds, experts)
    att_rows = dot(after(att_heads, grad_mlp_rows), output_full).astype(BF16)
    att_back, gate_up_full[1] = exchange_and_gather(att_rows, gate_up_low[1], 1)
    residual_one = (
        xfloat + dot(att_high, att_back, CONTRACT_ROWS) + dot(att_low, att_back, CONTRACT_ROWS)
    )

    inverse_two, unit_two = normalize(residual_one)
    normed_two = (unit_two * gain_two).astype(BF16)
    mlp_given = dot(mlp_send, normed_two).astype(BF16)
    mlp_in, gate_up_full[2] = exchange_and_gather(mlp_given, gate_up_low[2], 2)
    mlp_split = core_split(mlp_in, groups)
    acts = [None]
    weight_grads = []
    grads = [None] * len(cuts)

    def feed_chunk(index, feed_in, total):
        gate_up = gate_up_full[index]
        acts[0], grads[index] = feed(
            feed_in, grad_mlp_rows, gate_up, down_full, cuts[index][0], acts[0]
        )
        if index == 0:
            weight_grads.append(weight_product(mlp_in, grads[0]))
            steps(middle_scatter, weight_grads[0])
            ready = [array for scatter in middle_scatter for array in (scatter.sent, scatter.kept)]
            grads[0] = after(grads[0], *ready)
        return back(grads[index], gate_up, total, BF16 if index == 3 else F32)

    normed_split = core_split(normed_all, groups)
    att_split = core_split(att_in, groups)
    heads_split = core_split(att_heads, groups)
    grad_mlp_in = feed_chunk(
        1, after(mlp_in, *mlp_split, *normed_split, *att_split, *heads_split), None
    )
    grad_mlp_in = feed_chunk(2, after(mlp_in, grad_mlp_in), grad_mlp_in)
    middle_scatter = scatter_product(mlp_split, [after(grads[1], grad_mlp_in), grads[2]], groups)
    ready = [array for scatter in middle_scatter for array in (scatter.terms[0], scatter.sent)]
    grad_mlp_in = feed_chunk(0, after(mlp_in, *ready), grad_mlp_in)
    first_grad_sum = lax.psum_scatter(weight_grads[0], "grp", scatter_dimension=0, tiled=True)
    grad_mlp_in = feed_chunk(3, after(mlp_in, grad_mlp_in), grad_mlp_in)
    activated = acts[0]
    for scatter in middle_scatter:
        scatter.prepare(grad_mlp_in)
    mlp_returned, (down_grad, last_grad) = exchange_and_multiply(
        grad_mlp_in,
        [(multiply_columns, activated, grad_mlp_rows), (multiply_columns, mlp_in, grads[3])],
        middle_scatter,
        3,
    )
    down_grad_sum = lax.psum_scatter(down_grad, "grp", scatter_dimension=0, tiled=True)
    last_grad_sum = lax.psum_scatter(
        after(last_grad, down_grad), "grp", scatter_dimension=0, tiled=True
    )

    grad_final = cotangent.astype(F32)
    grad_normed_two = dot(mlp_send, mlp_returned, CONTRACT_ROWS)
    grad_inner_two, grad_gain_two = norm_backward(grad_normed_two, unit_two, inverse_two, gain_two)
    grad_residual = grad_final + grad_inner_two

    res_high, res_low = high_low(grad_residual)
    sent_four = (
        dot(att_high, res_high) + dot(att_low, res_high) + dot(att_high, res_low)
    ).astype(BF16)
    grad_att_rows, (mlp_rows,) = exchange_and_multiply(
        sent_four, [(multiply_rows, activated, down_full)], [], 4
    )
    grad_heads = dot(grad_att_rows, output_full, CONTRACT_COLUMNS).astype(BF16)
    grad_queries, grad_kv, mlp_first = attend_backward(
        queries, keys_values, grad_heads, bounds, logsums, mlp_rows, experts, 7
    )
    grad_att_in = dot(grad_queries, query_full, CONTRACT_COLUMNS).astype(BF16)
    grad_all = (
        jnp.einsum(
            "sct,scd->std",
            att_pick,
            grad_att_in.reshape(experts, capacity, model_width),
            preferred_element_type=F32,
        ).reshape(experts * tok_dev, model_width)
        + dot(grad_kv, kv_full, CONTRACT_COLUMNS)
    ).astype(BF16)
    grad_all = after(grad_all, first_grad_sum, down_grad_sum)
    (grad_back, mlp_second), kv_part, _ = exchange_and_scatter(
        [(grad_all, model_width), (mlp_rows, model_width // 2)], [(normed_split, grad_kv)], 5
    )
    kv_grad = lax.psum(kv_part, "ep")
    while middle_scatter[0].order:
        steps(middle_scatter)
    middle_terms = [[after(term, kv_part) for term in scatter.terms] for scatter in middle_scatter]
    _, both_maps, _ = exchange_and_scatter(
        [],
        [
            (att_split, after(grad_queries, kv_part, last_grad_sum)),
            (heads_split, grad_att_rows),
        ],
        6,
    )
    kv_grad = after(kv_grad, both_maps)
    chunks = [[first_grad_sum], *middle_terms, [last_grad_sum]]
    gate_up_grad = assemble([[after(term, kv_grad) for term in terms] for terms in chunks])[None]
    down_grad = after(down_grad_sum, kv_grad).astype(F32)[None]
    query_grad, output_grad = [part.astype(F32)[None] for part in halves(both_maps)]
    mlp_back = jnp.concatenate([after(mlp_first, kv_grad), mlp_second], axis=1)
    output = (
        residual_one + dot(mlp_high, mlp_back, CONTRACT_ROWS) + dot(mlp_low, mlp_back, CONTRACT_ROWS)
    ).astype(BF16)
    grad_normed_one = jnp.sum(
        after(grad_back, kv_grad).reshape(experts, tok_dev, model_width).astype(F32), axis=0
    )
    kv_grad = transpose(kv_grad)
    grad_inner_one, grad_gain_one = norm_backward(grad_normed_one, unit_one, inverse_one, gain_one)
    grad_input = grad_residual + grad_inner_one

    gains_grad = jnp.stack([grad_gain_one, grad_gain_two])
    gains_grad = gains_grad.reshape((2,) + (2,) * bits + (-1,))
    beside = [kv_grad, gate_up_grad, down_grad]
    for bit in reversed(range(bits)):
        mine_bit = (lax.axis_index("grp") >> bit) & 1
        kept = lax.dynamic_index_in_dim(gains_grad, mine_bit, 1, keepdims=False)
        sent = lax.dynamic_index_in_dim(gains_grad, 1 - mine_bit, 1, keepdims=False)
        gains_grad = kept + lax.ppermute(
            sent, "grp", [(i, i ^ (1 << bit)) for i in range(groups)]
        )
        if beside:
            gains_grad = after(gains_grad, beside.pop(0))
    for bit in range(experts.bit_length() - 1):
        gains_grad = gains_grad + lax.ppermute(
            gains_grad, "ep", [(i, i ^ (1 << bit)) for i in range(experts)]
        )
    return (
        output,
        grad_input,
        kv_grad,
        gains_grad,
        query_grad,
        output_grad,
        gate_up_grad,
        down_grad,
    )


def solution(mesh):
    placed = (
        P(("grp", "ep"), None),
        P(None, "grp"),
        P(None, "grp"),
        P("ep", "grp", None),
        P("ep", "grp", None),
        P("ep", "grp", None),
        P("ep", "grp", None),
        P("grp", None, None),
        P(("grp", "ep"), None),
        P("grp", None, None),
        P(("grp", "ep"), None),
        P("grp", None),
        P(("grp", "ep"), None),
    )
    return jax.shard_map(
        local,
        mesh=mesh,
        in_specs=placed,
        out_specs=(
            P(("grp", "ep"), None),
            P(("grp", "ep"), None),
            P(None, "grp"),
            P(None, "grp"),
            P("ep", "grp", None),
            P("ep", "grp", None),
            P("ep", "grp", None),
            P("ep", "grp", None),
        ),
        check_vma=False,
    )
```
